128 devices in a mesh: row: 16 (over y_lo, z, core), col: 8 (over y_hi, x).
Axes of the slice: x: 4, y: 4 (y_hi: 2, y_lo: 2; y = y_hi * 2 + y_lo), z: 4, core: 2. Of those that a mesh axis runs over, the one named last changes fastest.
Arguments:
- features: bfloat16 [65536, 512], P(('row', 'col')), may hold values from -6 to 6
- partition_of: int32 [65536], P(('row', 'col')), may hold values from 0 to 127, as said below
- weight: bfloat16 [512, 512], replicated, may hold values from -0.25 to 0.25
- tile_values: bfloat16 [16, 8, 192, 128, 128], P('row', 'col'), may hold values from -0.109375 to 0.109375
- tile_rows: int32 [16, 8, 192], P('row', 'col'), may hold values from 0 to 31
- tile_cols: int32 [16, 8, 192], P('row', 'col'), may hold values from 0 to 63
- tile_count: int32 [16, 8], P('row', 'col'), may hold values from 48 to 192, as said below
- out_cotangent: bfloat16 [65536, 512], P('row'), may hold values from -6 to 6
Outputs:
- activations: bfloat16 [65536, 512], P(('row', 'col'))
- weight_grad: float32 [512, 512], replicated
The draws below stay inside these ranges and needn't reach their ends.
Inputs may be any that keep to these rules, and one draw needn't show every extreme that they name: `partition_of`: of the 512 regions of each device in detection order, exactly 4 go to each partition. `tile_count`: some grid position has all 192 slots live in every draw.
All inputs are finite; a program needn't handle non-finite values.
Results may differ from the reference program's by a relative error of at most 0.005.
Values may be sent and summed in bfloat16 or wider, within the bound.
No kernel may reach another device: no remote copies, remote signals or barrier semaphores. Data moves between devices by JAX's collectives and lax.ppermute only.
A program may use at most 192 MiB of HBM per device.

```python
import math
import jax
import jax.numpy as jnp
from jax import lax

F = 512
TILE = 128
ROWS_DEV = 512
TILES = 192
NODES = 65536
ROW_TILES = 32
COL_TILES = 64
N_ROW = 16
N_COL = 8


def draw_partition_of(key, part):
    device_total = NODES // ROWS_DEV
    per_peer = ROWS_DEV // device_total
    pattern = jnp.repeat(jnp.arange(device_total, dtype=jnp.int32), per_peer)
    keys = jax.random.split(jax.random.fold_in(key, 7), device_total)

    def shuffle(single_key):
        return jax.random.permutation(single_key, pattern)
    shuffled = jax.vmap(shuffle)(keys)
    return shuffled.reshape(-1).astype(jnp.int32)


def draw_tile_count(key, part):
    first_key, second_key = jax.random.split(jax.random.fold_in(key, 11))
    divisor = jax.random.randint(first_key, (N_ROW * N_COL,), 1, 5)
    counts = TILES // divisor
    chosen = jax.random.randint(second_key, (), 0, N_ROW * N_COL)
    counts = counts.at[chosen].set(TILES)
    return counts.reshape(N_ROW, N_COL).astype(jnp.int32)


def place_ends(result, key, low, largest):
    place = [jax.random.randint(jax.random.fold_in(key, axis), (), 0, length) for axis, length in enumerate(result.shape)]
    longest = result.shape.index(max(result.shape))
    beside = place[:longest] + [(place[longest] + 1) % result.shape[longest]] + place[longest + 1:]
    return result.at[tuple(place)].set(low).at[tuple(beside)].set(largest)


def level_of(stream_key, dims, cuts, smallest, top_value):
    loudness = 1.0
    for position, shards_of in cuts:
        steps = jax.random.uniform(jax.random.fold_in(jax.random.fold_in(stream_key, 6), position), (shards_of,), jnp.float32, smallest / len(cuts), top_value / len(cuts))
        loudness = loudness * jnp.repeat(jnp.exp(steps), dims[position] // shards_of).reshape((-1,) + (1,) * (len(dims) - 1 - position))
    return loudness


def scatter_about(own_key, shape, scale, reach, cuts=(), kind=jnp.bfloat16):
    gain = level_of(own_key, shape, cuts, -0.22, 0.18) if cuts else 1.0
    values = jax.random.normal(own_key, shape, jnp.float32) * scale * gain
    return jnp.minimum(jnp.maximum(values, -reach), reach).astype(kind)


def setup_inputs(seed: int = 0) -> dict:
    splits = jax.random.split(jax.random.key(seed), 9)
    features = scatter_about(splits[0], (NODES, F), 1.0, 6.0, ((0, 128),))
    partition_of = draw_partition_of(jax.random.fold_in(splits[8], 71), 0)
    weight = scatter_about(splits[2], (F, F), F ** -0.5, 0.25)
    tile_values = scatter_about(splits[3], (N_ROW, N_COL, TILES, TILE, TILE), (TILES * TILE * TILE // (2 * ROWS_DEV)) ** -0.5, 0.109375, ((0, 16), (1, 8)))
    tile_rows = place_ends(jax.random.randint(splits[4], (N_ROW, N_COL, TILES), 0, ROW_TILES), jax.random.fold_in(splits[4], 1), 0, ROW_TILES - 1).astype(jnp.int32)
    tile_cols = place_ends(jax.random.randint(splits[5], (N_ROW, N_COL, TILES), 0, COL_TILES), jax.random.fold_in(splits[5], 1), 0, COL_TILES - 1).astype(jnp.int32)
    tile_count = draw_tile_count(jax.random.fold_in(splits[8], 71), 0)
    out_cotangent = scatter_about(splits[7], (NODES, F), 1.0, 6.0, ((0, 16),))
    return dict(features=features, partition_of=partition_of, weight=weight, tile_values=tile_values, tile_rows=tile_rows, tile_cols=tile_cols, tile_count=tile_count, out_cotangent=out_cotangent)


def silu_slope(pre):
    sigmoid = jax.nn.sigmoid(pre)
    return sigmoid * (1.0 + pre * (1.0 - sigmoid))

def accumulate(blocks, live_mask, lookup_ids, place_ids, sources, transposed):
    slot_total = blocks.shape[0]
    group = math.gcd(slot_total, 256)
    groups = slot_total // group
    tile_size = blocks.shape[-1]
    feature_width = sources.shape[-1]
    node_tiles = sources.shape[0]
    items = (blocks.reshape(groups, group, tile_size, tile_size), live_mask.reshape(groups, group), lookup_ids.reshape(groups, group), place_ids.reshape(groups, group))

    def one_group(totals, item):
        tile_block, is_live, lookup_part, place_part = item
        masked = jnp.where(is_live[:, None, None], tile_block.astype(jnp.float32), jnp.zeros((), jnp.float32))
        picked = sources[lookup_part].astype(jnp.float32)
        if transposed:
            products = jnp.einsum('tij,tif->tjf', masked, picked)
        else:
            products = jnp.einsum('tij,tjf->tif', masked, picked)
        return (totals.at[place_part].add(products), None)
    start = jnp.zeros((node_tiles, tile_size, feature_width), jnp.float32)
    totals, unused = lax.scan(one_group, start, items)
    return totals

def reference(features, partition_of, weight, tile_values, tile_rows, tile_cols, tile_count, out_cotangent):
    ordering = jnp.argsort(partition_of, stable=True)
    regrouped = features[ordering]
    hidden = jnp.dot(regrouped, weight, preferred_element_type=jnp.float32).astype(jnp.bfloat16)
    per_slice = ROWS_DEV // TILE
    grid_rows = jnp.arange(N_ROW, dtype=jnp.int32)[:, None, None]
    grid_cols = jnp.arange(N_COL, dtype=jnp.int32)[None, :, None]
    global_rows = (grid_rows * ROW_TILES + tile_rows).reshape(-1).astype(jnp.int32)
    global_cols = ((tile_cols // per_slice * N_COL + grid_cols) * per_slice + tile_cols % per_slice).reshape(-1).astype(jnp.int32)
    live_mask = (jnp.arange(TILES, dtype=jnp.int32)[None, None, :] < tile_count[:, :, None]).reshape(-1)
    blocks = tile_values.reshape(-1, TILE, TILE)
    node_tiles = NODES // TILE
    hidden_tiles = hidden.reshape(node_tiles, TILE, F)
    pre = accumulate(blocks, live_mask, global_cols, global_rows, hidden_tiles, False).reshape(NODES, F)
    activations = jax.nn.silu(pre).astype(jnp.bfloat16)
    slope = (out_cotangent.astype(jnp.float32) * silu_slope(pre)).astype(jnp.bfloat16)
    slope_tiles = slope.reshape(node_tiles, TILE, F)
    hidden_grad = accumulate(blocks, live_mask, global_rows, global_cols, slope_tiles, True).reshape(NODES, F)
    weight_grad = jnp.dot(regrouped.astype(jnp.float32).T, hidden_grad, precision=lax.Precision.HIGHEST, preferred_element_type=jnp.float32) * (1.0 / math.sqrt(NODES))
    return (activations, weight_grad)
```

```python
import jax
import jax.numpy as jnp
from jax import lax
from jax.experimental import pallas as pl
from jax.experimental.pallas import tpu as pltpu
from jax.sharding import PartitionSpec as P

N_ROW = 16
N_COL = 8
TILE = 128
SLOTS = 512
F = 512
PER_PEER = 4
BF16 = jnp.bfloat16
F32 = jnp.float32
VMEM_LIMIT = 56 * 1024 * 1024


def params():
    return pltpu.CompilerParams(vmem_limit_bytes=VMEM_LIMIT)


def selection(position, rows, columns):
    wanted = lax.broadcasted_iota(jnp.int32, (rows, columns), 0)
    return jnp.where(position == wanted, 1.0, 0.0).astype(BF16)


def group_kernel(part_ref, features_ref, out_ref):
    part = part_ref[...]
    devices = N_ROW * N_COL
    member = jnp.where(
        part == lax.broadcasted_iota(jnp.int32, (devices, SLOTS), 0), 1.0, 0.0
    )
    before = jnp.where(
        lax.broadcasted_iota(jnp.int32, (SLOTS, SLOTS), 0)
        < lax.broadcasted_iota(jnp.int32, (SLOTS, SLOTS), 1),
        1.0,
        0.0,
    ).astype(BF16)
    earlier = jnp.dot(member.astype(BF16), before, preferred_element_type=F32)
    rank = jnp.sum(member * earlier, axis=0, keepdims=True).astype(jnp.int32)
    place = ((part & (N_COL - 1)) * N_ROW + (part >> 3)) * PER_PEER + rank
    pick = selection(place, SLOTS, SLOTS)
    out_ref[...] = jnp.dot(pick, features_ref[...], preferred_element_type=F32).astype(BF16)


def interleave_kernel(arrived_ref, out_ref):
    source = lax.broadcasted_iota(jnp.int32, (1, SLOTS), 1)
    giver, inner = source >> 6, source & 63
    place = (inner >> 2) * (N_COL * PER_PEER) + giver * PER_PEER + (inner & 3)
    pick = selection(place, SLOTS, SLOTS)
    out_ref[...] = jnp.dot(pick, arrived_ref[...], preferred_element_type=F32).astype(BF16)


def tiles_kernel(count_ref, rows_ref, cols_ref, tiles_ref, source_ref, out_ref, total):
    total[...] = jnp.zeros_like(total)

    def one_slot(t, carry):
        r = rows_ref[t]
        u = cols_ref[t]
        block = source_ref[pl.ds((u & 3) * 4, 4), u >> 2].reshape(TILE, F)
        total[r] += jnp.dot(tiles_ref[t], block, preferred_element_type=F32)
        return carry

    lax.fori_loop(0, count_ref[0], one_slot, 0)
    out_ref[...] = total[...].astype(BF16)


def layer_kernel(parts_ref, weight_ref, cotangent_ref, act_ref, grad_ref):
    mixed = parts_ref[0].astype(F32)
    for k in range(1, N_COL):
        mixed = mixed + parts_ref[k].astype(F32)
    high = mixed.astype(BF16)
    low = (mixed - high.astype(F32)).astype(BF16)
    weight = weight_ref[...]
    pre = jnp.dot(high, weight, preferred_element_type=F32) + jnp.dot(
        low, weight, preferred_element_type=F32
    )
    sigmoid = jax.nn.sigmoid(pre)
    act_ref[...] = (pre * sigmoid).astype(BF16)
    slope = (
        cotangent_ref[...].astype(F32) * (sigmoid * (1.0 + pre * (1.0 - sigmoid)))
    ).astype(BF16)
    contract = (((0,), (0,)), ((), ()))
    grad = lax.dot_general(high, slope, contract, preferred_element_type=F32)
    grad = grad + lax.dot_general(low, slope, contract, preferred_element_type=F32)
    grad_ref[...] = grad * (1.0 / 256.0)


def row_moves(move):
    pairs = []
    for yl in range(2):
        for z in range(4):
            for c in range(2):
                a, b, d = move(yl, z, c)
                pairs.append(((yl * 4 + z) * 2 + c, (a * 4 + b) * 2 + d))
    return pairs


def all_moves_y(k):
    pairs = []
    for i in range(N_ROW):
        for j in range(N_COL):
            y = (j // 4) * 2 + i // 8
            to = (y + k) % 4
            pairs.append((i * N_COL + j, ((to % 2) * 8 + i % 8) * N_COL + (to // 2) * 4 + j % 4))
    return pairs


def x_moves(k):
    return [(yh * 4 + x, yh * 4 + (x + k) % 4) for yh in range(2) for x in range(4)]


def scatter4(total, me, axis, moves):
    quarter = total.shape[0] // 4
    parts = total.reshape(4, quarter, F)
    out = lax.dynamic_index_in_dim(parts, me, 0, False)
    got = []
    for k in (2, 1, 3):
        send = lax.dynamic_index_in_dim(parts, (me + k) % 4, 0, False)
        got.append(lax.ppermute(send, axis, moves(k)))
    return ((out + got[0]) + got[1]) + got[2]


def gather4(part, me, axis, moves):
    got = [part] + [lax.ppermute(part, axis, moves(k)) for k in (1, 2, 3)]
    stacked = jnp.stack(got)
    order = (me - jnp.arange(4, dtype=jnp.int32)) % 4
    return stacked[order[0]], stacked[order[1]], stacked[order[2]], stacked[order[3]]


def shards(
    features, partition_of, weight, tile_values, tile_rows, tile_cols, tile_count, out_cotangent
):
    row = lax.axis_index("row")
    col = lax.axis_index("col")
    core, z, yl = row % 2, (row // 2) % 4, row // 8
    x, yh = col % 4, col // 4
    y = yh * 2 + yl
    vmem = pl.BlockSpec(memory_space=pltpu.VMEM)
    smem = pl.BlockSpec(memory_space=pltpu.SMEM)

    grouped = pl.pallas_call(
        group_kernel,
        out_shape=jax.ShapeDtypeStruct((SLOTS, F), BF16),
        compiler_params=params(),
    )(partition_of.reshape(1, SLOTS), features)
    arrived = lax.all_to_all(grouped, "col", split_axis=0, concat_axis=0, tiled=True)
    mine = pl.pallas_call(
        interleave_kernel,
        out_shape=jax.ShapeDtypeStruct((SLOTS, F), BF16),
        compiler_params=params(),
    )(arrived)
    sources = lax.all_gather(mine, "row", axis=0, tiled=True)
    sources = sources.reshape(N_ROW, N_ROW, N_COL * PER_PEER, F)

    partial = pl.pallas_call(
        tiles_kernel,
        in_specs=[smem, smem, smem, vmem, vmem],
        out_specs=vmem,
        out_shape=jax.ShapeDtypeStruct((32, TILE, F), BF16),
        scratch_shapes=[pltpu.VMEM((32, TILE, F), F32)],
        compiler_params=params(),
    )(
        tile_count.reshape(1),
        tile_rows.reshape(-1),
        tile_cols.reshape(-1),
        tile_values.reshape(-1, TILE, TILE),
        sources,
    )
    parts = lax.all_to_all(
        partial.reshape(N_COL * SLOTS, F), "col", split_axis=0, concat_axis=0, tiled=True
    ).reshape(N_COL, SLOTS, F)
    cotangent = lax.dynamic_slice_in_dim(out_cotangent, col * SLOTS, SLOTS, 0)
    activations, grad = pl.pallas_call(
        layer_kernel,
        out_shape=(
            jax.ShapeDtypeStruct((SLOTS, F), BF16),
            jax.ShapeDtypeStruct((F, F), F32),
        ),
        compiler_params=params(),
    )(parts, weight, cotangent)

    z_moves = lambda k: row_moves(lambda yl, z, c: (yl, (z + k) % 4, c))
    swap = row_moves(lambda yl, z, c: (yl, z, 1 - c))
    halves = grad.reshape(2, F // 2, F)
    half = lax.dynamic_index_in_dim(halves, core, 0, False) + lax.ppermute(
        lax.dynamic_index_in_dim(halves, 1 - core, 0, False), "row", swap
    )
    eighth = scatter4(half, x, "col", x_moves)
    piece = scatter4(eighth, z, "row", z_moves)
    a, b, c, d = gather4(piece, y, ("row", "col"), all_moves_y)
    piece = (a + b) + (c + d)
    eighth = jnp.concatenate(gather4(piece, z, "row", z_moves))
    half = jnp.concatenate(gather4(eighth, x, "col", x_moves))
    other = lax.ppermute(half, "row", swap)
    first = jnp.where(core == 0, half, other)
    second = jnp.where(core == 0, other, half)
    return activations, jnp.concatenate([first, second])


def solution(mesh):
    placed = (
        P(("row", "col"), None),
        P(("row", "col")),
        P(),
        P("row", "col", None, None, None),
        P("row", "col", None),
        P("row", "col", None),
        P("row", "col"),
        P("row", None),
    )
    return jax.shard_map(
        shards,
        mesh=mesh,
        in_specs=placed,
        out_specs=(P(("row", "col"), None), P()),
        check_vma=False,
    )
```

```python
import jax
import jax.numpy as jnp
from jax import lax
from jax.experimental import pallas as pl
from jax.experimental.pallas import tpu as pltpu
from jax.sharding import PartitionSpec as P

N_ROW = 16
N_COL = 8
TILE = 128
SLOTS = 512
F = 512
PER_PEER = 4
SLOT_CAP = 192
ROW_TILES = 32
GROUP_BITS = 2
GROUP = 1 << GROUP_BITS
PLAN = SLOT_CAP + ROW_TILES * (GROUP - 1)
BF16 = jnp.bfloat16
F32 = jnp.float32
VMEM_LIMIT = 56 * 1024 * 1024


def params():
    return pltpu.CompilerParams(vmem_limit_bytes=VMEM_LIMIT)


def selection(position, rows, columns):
    wanted = lax.broadcasted_iota(jnp.int32, (rows, columns), 0)
    return jnp.where(position == wanted, 1.0, 0.0).astype(BF16)


def group_kernel(part_ref, features_ref, out_ref):
    part = part_ref[...]
    devices = N_ROW * N_COL
    member = jnp.where(
        part == lax.broadcasted_iota(jnp.int32, (devices, SLOTS), 0), 1.0, 0.0
    )
    before = jnp.where(
        lax.broadcasted_iota(jnp.int32, (SLOTS, SLOTS), 0)
        < lax.broadcasted_iota(jnp.int32, (SLOTS, SLOTS), 1),
        1.0,
        0.0,
    ).astype(BF16)
    earlier = jnp.dot(member.astype(BF16), before, preferred_element_type=F32)
    rank = jnp.sum(member * earlier, axis=0, keepdims=True).astype(jnp.int32)
    place = ((part & (N_COL - 1)) * N_ROW + (part >> 3)) * PER_PEER + rank
    pick = selection(place, SLOTS, SLOTS)
    out_ref[...] = jnp.dot(pick, features_ref[...], preferred_element_type=F32).astype(BF16)


def interleave_kernel(arrived_ref, out_ref):
    source = lax.broadcasted_iota(jnp.int32, (1, SLOTS), 1)
    giver, inner = source >> 6, source & 63
    place = (inner >> 2) * (N_COL * PER_PEER) + giver * PER_PEER + (inner & 3)
    pick = selection(place, SLOTS, SLOTS)
    out_ref[...] = jnp.dot(pick, arrived_ref[...], preferred_element_type=F32).astype(BF16)


def plan_kernel(count_ref, rows_ref, cols_ref, plan_ref):
    slot = lax.broadcasted_iota(jnp.int32, (1, SLOT_CAP), 1)
    rows = rows_ref[...]
    live = slot < count_ref[0]
    kinds = lax.broadcasted_iota(jnp.int32, (ROW_TILES, SLOT_CAP), 0)
    member = jnp.where(live & (rows == kinds), 1.0, 0.0)
    before = jnp.where(
        lax.broadcasted_iota(jnp.int32, (SLOT_CAP, SLOT_CAP), 0)
        < lax.broadcasted_iota(jnp.int32, (SLOT_CAP, SLOT_CAP), 1),
        1.0,
        0.0,
    ).astype(BF16)
    earlier = jnp.dot(member.astype(BF16), before, preferred_element_type=F32)
    number = jnp.sum(member, axis=1, keepdims=True).astype(jnp.int32)
    groups = jnp.broadcast_to((number + (GROUP - 1)) >> GROUP_BITS, (ROW_TILES, TILE))
    below = jnp.where(
        lax.broadcasted_iota(jnp.int32, (ROW_TILES, ROW_TILES), 1)
        < lax.broadcasted_iota(jnp.int32, (ROW_TILES, ROW_TILES), 0),
        1.0,
        0.0,
    ).astype(BF16)
    groups = groups.astype(F32)
    start = jnp.dot(below, groups.astype(BF16), preferred_element_type=F32)[:, :1]
    total = jnp.sum(groups, axis=0, keepdims=True)[:, :1]
    place = jnp.sum(member * (GROUP * start + earlier + 1.0), axis=0, keepdims=True) - 1.0
    taken = selection(place.astype(jnp.int32), PLAN, SLOT_CAP)
    line = lax.broadcasted_iota(jnp.int32, (8, SLOT_CAP), 0)
    values = jnp.where(line == 0, slot - SLOT_CAP, jnp.where(line == 1, cols_ref[...], rows))
    found = lax.dot_general(
        values.astype(F32).astype(BF16),
        taken,
        (((1,), (1,)), ((), ())),
        preferred_element_type=F32,
    )
    line = lax.broadcasted_iota(jnp.int32, (8, PLAN), 0)
    found = jnp.where(line == 0, found + SLOT_CAP, jnp.where(line == 3, total, found))
    plan_ref[...] = found.astype(jnp.int32)


def tiles_kernel(plan_ref, tiles_hbm, source_hbm, out_ref, tiles, source, total, sems):
    tiles_copy = pltpu.make_async_copy(tiles_hbm, tiles.at[pl.ds(0, SLOT_CAP)], sems.at[0])
    source_copy = pltpu.make_async_copy(source_hbm, source, sems.at[1])
    tiles_copy.start()
    source_copy.start()
    tiles[SLOT_CAP] = jnp.zeros((TILE, TILE), BF16)
    total[...] = jnp.zeros_like(total)
    tiles_copy.wait()
    source_copy.wait()

    def product(g):
        left, right = [], []
        for e in range(GROUP):
            u = plan_ref[1, g * GROUP + e]
            left.append(tiles[plan_ref[0, g * GROUP + e]])
            right.append(source[pl.ds((u & 3) * 4, 4), u >> 2].reshape(TILE, F))
        return jnp.dot(
            jnp.concatenate(left, axis=1),
            jnp.concatenate(right, axis=0),
            preferred_element_type=F32,
        )

    def two_groups(h, carry):
        g = h * 2
        first, second = product(g), product(g + 1)
        total[plan_ref[2, g * GROUP]] += first
        total[plan_ref[2, g * GROUP + GROUP]] += second
        return carry

    lax.fori_loop(0, (plan_ref[3, 0] + 1) >> 1, two_groups, 0)
    out_ref[...] = total[...].astype(BF16)


def layer_kernel(parts_ref, weight_ref, cotangent_ref, act_ref, grad_ref):
    mixed = parts_ref[0].astype(F32)
    for k in range(1, N_COL):
        mixed = mixed + parts_ref[k].astype(F32)
    high = mixed.astype(BF16)
    low = (mixed - high.astype(F32)).astype(BF16)
    weight = weight_ref[...]
    pre = jnp.dot(high, weight, preferred_element_type=F32) + jnp.dot(
        low, weight, preferred_element_type=F32
    )
    sigmoid = jax.nn.sigmoid(pre)
    act_ref[...] = (pre * sigmoid).astype(BF16)
    slope = (
        cotangent_ref[...].astype(F32) * (sigmoid * (1.0 + pre * (1.0 - sigmoid)))
    ).astype(BF16)
    contract = (((0,), (0,)), ((), ()))
    grad = lax.dot_general(high, slope, contract, preferred_element_type=F32)
    grad = grad + lax.dot_general(low, slope, contract, preferred_element_type=F32)
    grad_ref[...] = grad * (1.0 / 256.0)


def row_moves(move):
    pairs = []
    for yl in range(2):
        for z in range(4):
            for c in range(2):
                a, b, d = move(yl, z, c)
                pairs.append(((yl * 4 + z) * 2 + c, (a * 4 + b) * 2 + d))
    return pairs


def all_moves_y(k):
    pairs = []
    for i in range(N_ROW):
        for j in range(N_COL):
            y = (j // 4) * 2 + i // 8
            to = (y + k) % 4
            pairs.append((i * N_COL + j, ((to % 2) * 8 + i % 8) * N_COL + (to // 2) * 4 + j % 4))
    return pairs


def x_moves(k):
    return [(yh * 4 + x, yh * 4 + (x + k) % 4) for yh in range(2) for x in range(4)]


def scatter4(total, me, axis, moves):
    quarter = total.shape[0] // 4
    parts = total.reshape(4, quarter, F)
    out = lax.dynamic_index_in_dim(parts, me, 0, False)
    for k in (2, 1, 3):
        send = lax.dynamic_index_in_dim(parts, (me + k) % 4, 0, False).astype(BF16)
        out = out + lax.ppermute(send, axis, moves(k)).astype(F32)
    return out


def by_giver(own, me, axis, moves):
    got = jnp.stack([own] + [lax.ppermute(own, axis, moves(k)) for k in (1, 2, 3)])
    return [got[(me - k) % 4] for k in range(4)]


def shards(
    features, partition_of, weight, tile_values, tile_rows, tile_cols, tile_count, out_cotangent
):
    row = lax.axis_index("row")
    col = lax.axis_index("col")
    core, z, yl = row % 2, (row // 2) % 4, row // 8
    x, yh = col % 4, col // 4
    y = yh * 2 + yl
    vmem = pl.BlockSpec(memory_space=pltpu.VMEM)
    smem = pl.BlockSpec(memory_space=pltpu.SMEM)

    hbm = pl.BlockSpec(memory_space=pl.ANY)
    plan = pl.pallas_call(
        plan_kernel,
        in_specs=[smem, vmem, vmem],
        out_specs=vmem,
        out_shape=jax.ShapeDtypeStruct((8, PLAN), jnp.int32),
        compiler_params=params(),
    )(tile_count.reshape(1), tile_rows.reshape(1, -1), tile_cols.reshape(1, -1))
    grouped = pl.pallas_call(
        group_kernel,
        out_shape=jax.ShapeDtypeStruct((SLOTS, F), BF16),
        compiler_params=params(),
    )(partition_of.reshape(1, SLOTS), features)
    arrived = lax.all_to_all(grouped, "col", split_axis=0, concat_axis=0, tiled=True)
    mine = pl.pallas_call(
        interleave_kernel,
        out_shape=jax.ShapeDtypeStruct((SLOTS, F), BF16),
        compiler_params=params(),
    )(arrived)
    sources = lax.all_gather(mine, "row", axis=0, tiled=True)
    sources = sources.reshape(N_ROW, N_ROW, N_COL * PER_PEER, F)

    partial = pl.pallas_call(
        tiles_kernel,
        in_specs=[smem, hbm, hbm],
        out_specs=vmem,
        out_shape=jax.ShapeDtypeStruct((ROW_TILES, TILE, F), BF16),
        scratch_shapes=[
            pltpu.VMEM((SLOT_CAP + 1, TILE, TILE), BF16),
            pltpu.VMEM((N_ROW, N_ROW, N_COL * PER_PEER, F), BF16),
            pltpu.VMEM((ROW_TILES, TILE, F), F32),
            pltpu.SemaphoreType.DMA((2,)),
        ],
        compiler_params=params(),
    )(plan, tile_values.reshape(-1, TILE, TILE), sources)
    parts = lax.all_to_all(
        partial.reshape(N_COL * SLOTS, F), "col", split_axis=0, concat_axis=0, tiled=True
    ).reshape(N_COL, SLOTS, F)
    cotangent = lax.dynamic_slice_in_dim(out_cotangent, col * SLOTS, SLOTS, 0)
    activations, grad = pl.pallas_call(
        layer_kernel,
        out_shape=(
            jax.ShapeDtypeStruct((SLOTS, F), BF16),
            jax.ShapeDtypeStruct((F, F), F32),
        ),
        compiler_params=params(),
    )(parts, weight, cotangent)

    z_moves = lambda k: row_moves(lambda yl, z, c: (yl, (z + k) % 4, c))
    swap = row_moves(lambda yl, z, c: (yl, z, 1 - c))
    halves = grad.reshape(2, F // 2, F)
    half = lax.dynamic_index_in_dim(halves, core, 0, False) + lax.ppermute(
        lax.dynamic_index_in_dim(halves, 1 - core, 0, False), "row", swap
    )
    eighth = scatter4(half, x, "col", x_moves)
    a, b, c, d = by_giver(eighth, z, "row", z_moves)
    eighth = (a + b) + (c + d)
    a, b, c, d = by_giver(eighth, y, ("row", "col"), all_moves_y)
    eighth = (a + b) + (c + d)
    half = jnp.concatenate(by_giver(eighth.astype(BF16), x, "col", x_moves))
    other = lax.ppermute(half, "row", swap)
    first = jnp.where(core == 0, half, other).astype(F32)
    second = jnp.where(core == 0, other, half).astype(F32)
    return activations, jnp.concatenate([first, second])


def solution(mesh):
    placed = (
        P(("row", "col"), None),
        P(("row", "col")),
        P(),
        P("row", "col", None, None, None),
        P("row", "col", None),
        P("row", "col", None),
        P("row", "col"),
        P("row", None),
    )
    return jax.shard_map(
        shards,
        mesh=mesh,
        in_specs=placed,
        out_specs=(P(("row", "col"), None), P()),
        check_vma=False,
    )
```

```python
import jax
import jax.numpy as jnp
from jax import lax
from jax.experimental import pallas as pl
from jax.experimental.pallas import tpu as pltpu
from jax.sharding import PartitionSpec as P

N_ROW = 16
N_COL = 8
TILE = 128
SLOTS = 512
F = 512
PER_PEER = 4
HALF = 256
CHIPS = 8
SLOT_CAP = 192
ROW_TILES = 32
GROUP_BITS = 2
GROUP = 1 << GROUP_BITS
PLAN = SLOT_CAP + ROW_TILES * (GROUP - 1)
BF16 = jnp.bfloat16
F32 = jnp.float32
VMEM_LIMIT = 56 * 1024 * 1024


def params():
    return pltpu.CompilerParams(vmem_limit_bytes=VMEM_LIMIT)


def selection(position, rows, columns):
    wanted = lax.broadcasted_iota(jnp.int32, (rows, columns), 0)
    return jnp.where(position == wanted, 1.0, 0.0).astype(BF16)


def group_kernel(meta_ref, part_ref, features_ref, other_part_ref, other_ref, out_ref):
    core = meta_ref[0]
    devices = N_ROW * N_COL
    before = jnp.where(
        lax.broadcasted_iota(jnp.int32, (SLOTS, SLOTS), 0)
        < lax.broadcasted_iota(jnp.int32, (SLOTS, SLOTS), 1),
        1.0,
        0.0,
    ).astype(BF16)

    def grouped(part, rows):
        member = jnp.where(
            part == lax.broadcasted_iota(jnp.int32, (devices, SLOTS), 0), 1.0, 0.0
        )
        earlier = jnp.dot(member.astype(BF16), before, preferred_element_type=F32)
        rank = jnp.sum(member * earlier, axis=0, keepdims=True).astype(jnp.int32)
        place = ((part & (N_COL - 1)) * N_ROW + (part >> 3)) * PER_PEER + rank
        pick = selection(place, SLOTS, SLOTS)
        wanted = jnp.where(core == 0, rows[:, :HALF], rows[:, HALF:])
        picked = jnp.dot(pick, wanted, preferred_element_type=F32).astype(BF16)
        return picked.reshape(N_COL, 1, SLOTS // N_COL, HALF)

    out_ref[:, pl.ds(core, 1)] = grouped(part_ref[...], features_ref[...])
    out_ref[:, pl.ds(1 - core, 1)] = grouped(other_part_ref[...], other_ref[...])


def interleave_kernel(arrived_ref, out_ref):
    source = lax.broadcasted_iota(jnp.int32, (1, SLOTS), 1)
    giver, inner = source >> 6, source & 63
    place = (inner >> 2) * (N_COL * PER_PEER) + giver * PER_PEER + (inner & 3)
    pick = selection(place, SLOTS, SLOTS)
    for c in range(2):
        rows = arrived_ref[:, c].reshape(SLOTS, HALF)
        out_ref[c] = jnp.dot(pick, rows, preferred_element_type=F32).astype(BF16)


def plan_kernel(count_ref, rows_ref, cols_ref, plan_ref):
    slot = lax.broadcasted_iota(jnp.int32, (1, SLOT_CAP), 1)
    rows = rows_ref[...]
    live = slot < count_ref[0]
    kinds = lax.broadcasted_iota(jnp.int32, (ROW_TILES, SLOT_CAP), 0)
    member = jnp.where(live & (rows == kinds), 1.0, 0.0)
    before = jnp.where(
        lax.broadcasted_iota(jnp.int32, (SLOT_CAP, SLOT_CAP), 0)
        < lax.broadcasted_iota(jnp.int32, (SLOT_CAP, SLOT_CAP), 1),
        1.0,
        0.0,
    ).astype(BF16)
    earlier = jnp.dot(member.astype(BF16), before, preferred_element_type=F32)
    number = jnp.sum(member, axis=1, keepdims=True).astype(jnp.int32)
    groups = jnp.broadcast_to((number + (GROUP - 1)) >> GROUP_BITS, (ROW_TILES, TILE))
    below = jnp.where(
        lax.broadcasted_iota(jnp.int32, (ROW_TILES, ROW_TILES), 1)
        < lax.broadcasted_iota(jnp.int32, (ROW_TILES, ROW_TILES), 0),
        1.0,
        0.0,
    ).astype(BF16)
    groups = groups.astype(F32)
    start = jnp.dot(below, groups.astype(BF16), preferred_element_type=F32)[:, :1]
    total = jnp.sum(groups, axis=0, keepdims=True)[:, :1]
    place = jnp.sum(member * (GROUP * start + earlier + 1.0), axis=0, keepdims=True) - 1.0
    taken = selection(place.astype(jnp.int32), PLAN, SLOT_CAP)
    line = lax.broadcasted_iota(jnp.int32, (8, SLOT_CAP), 0)
    values = jnp.where(line == 0, slot - SLOT_CAP, jnp.where(line == 1, cols_ref[...], rows))
    found = lax.dot_general(
        values.astype(F32).astype(BF16),
        taken,
        (((1,), (1,)), ((), ())),
        preferred_element_type=F32,
    )
    line = lax.broadcasted_iota(jnp.int32, (8, PLAN), 0)
    found = jnp.where(line == 0, found + SLOT_CAP, jnp.where(line == 3, total, found))
    plan_ref[...] = found.astype(jnp.int32)


def tiles_kernel(part, meta_ref, plan_ref, own_hbm, other_hbm, *refs):
    blocks, outs = refs[:CHIPS], refs[CHIPS:-6]
    tiles, source, total, narrow, sems, out_sems = refs[-6:]
    core, x, yh = meta_ref[0], meta_ref[1], meta_ref[2]
    live = tiles.at[pl.ds(0, SLOT_CAP)]
    own_copy = pltpu.make_async_copy(own_hbm, live, sems.at[CHIPS])
    other_copy = pltpu.make_async_copy(other_hbm, live, sems.at[CHIPS])

    @pl.when(core == part)
    def _():
        own_copy.start()

    @pl.when(core != part)
    def _():
        other_copy.start()

    copies = [
        pltpu.make_async_copy(blocks[k], source.at[meta_ref[4 + k]], sems.at[k])
        for k in range(CHIPS)
    ]
    for copy in copies:
        copy.start()
    tiles[SLOT_CAP] = jnp.zeros((TILE, TILE), BF16)
    total[...] = jnp.zeros_like(total)
    own_copy.wait()
    for copy in copies:
        copy.wait()

    def product(g):
        left, right = [], []
        for e in range(GROUP):
            u = plan_ref[1, g * GROUP + e]
            left.append(tiles[plan_ref[0, g * GROUP + e]])
            right.append(source[pl.ds((u & 3) * 2, 2), :, u >> 2].reshape(TILE, HALF))
        return jnp.dot(
            jnp.concatenate(left, axis=1),
            jnp.concatenate(right, axis=0),
            preferred_element_type=F32,
        )

    def two_groups(h, carry):
        g = h * 2
        first, second = product(g), product(g + 1)
        total[plan_ref[2, g * GROUP]] += first
        total[plan_ref[2, g * GROUP + GROUP]] += second
        return carry

    lax.fori_loop(0, (plan_ref[3, 0] + 1) >> 1, two_groups, 0)
    narrow[...] = total[...].astype(BF16).reshape(narrow.shape)
    if part == 0:
        given = [narrow.at[:, (x + k) & 3] for k in range(4)]
    else:
        given = [narrow.at[yh], narrow.at[1 - yh]]
    copies = [
        pltpu.make_async_copy(piece, out, out_sems.at[k])
        for k, (piece, out) in enumerate(zip(given, outs))
    ]
    for copy in copies:
        copy.start()
    for copy in copies:
        copy.wait()


def x_summed_kernel(meta_ref, own_ref, a_ref, b_ref, c_ref, keep_ref, send_ref):
    yh = meta_ref[2]

    def summed(k):
        pair = own_ref[k].astype(F32) + a_ref[k].astype(F32)
        return pair + (b_ref[k].astype(F32) + c_ref[k].astype(F32))

    keep_ref[...] = summed(yh)
    send_ref[...] = summed(1 - yh).astype(BF16)


def y_summed_kernel(meta_ref, own_ref, got_ref, keep_ref, a_ref, b_ref, c_ref):
    x = meta_ref[1]

    def summed(k):
        return own_ref[k].astype(F32) + got_ref[k].astype(F32)

    keep_ref[...] = summed(x)
    for k, out in ((1, a_ref), (2, b_ref), (3, c_ref)):
        out[...] = summed((x + k) & 3).astype(BF16)


def sums_kernel(meta_ref, keep0, got0, keep1, a_ref, b_ref, c_ref, mine_ref, send_ref):
    core = meta_ref[0]
    first = keep0[...] + got0[...].astype(F32)
    second = keep1[...] + a_ref[...].astype(F32)
    second = second + (b_ref[...].astype(F32) + c_ref[...].astype(F32))
    mine_ref[...] = jnp.where(core == 0, first, second)
    send_ref[...] = jnp.where(core == 0, second, first)


def two_parts(value):
    high = value.astype(BF16)
    return high, (value - high.astype(F32)).astype(BF16)


def layer_kernel(meta_ref, mine_ref, got_ref, weight_ref, cotangent_ref, act_ref, slope_ref):
    core = meta_ref[0]
    pre = jnp.zeros((SLOTS, F), F32)
    for half, mixed in ((core, mine_ref[...]), (1 - core, got_ref[...])):
        weight = weight_ref[pl.ds(pl.multiple_of(half * HALF, HALF), HALF), :]
        for piece in two_parts(mixed):
            pre = pre + jnp.dot(piece, weight, preferred_element_type=F32)
    sigmoid = jax.nn.sigmoid(pre)
    act_ref[...] = (pre * sigmoid).astype(BF16)
    slope_ref[...] = (
        cotangent_ref[...].astype(F32) * (sigmoid * (1.0 + pre * (1.0 - sigmoid)))
    ).astype(BF16)


def gradient_kernel(mine_ref, other_ref, slope_ref, other_slope_ref, grad_ref):
    contract = (((0,), (0,)), ((), ()))
    grad = jnp.zeros((HALF, F), F32)
    for mixed, slope in ((mine_ref, slope_ref), (other_ref, other_slope_ref)):
        for piece in two_parts(mixed[...]):
            grad = grad + lax.dot_general(
                piece, slope[...], contract, preferred_element_type=F32
            )
    grad_ref[...] = grad * (1.0 / 256.0)


def row_moves(move):
    pairs = []
    for yl in range(2):
        for z in range(4):
            for c in range(2):
                a, b, d = move(yl, z, c)
                pairs.append(((yl * 4 + z) * 2 + c, (a * 4 + b) * 2 + d))
    return pairs


def all_moves_y(k):
    pairs = []
    for i in range(N_ROW):
        for j in range(N_COL):
            y = (j // 4) * 2 + i // 8
            to = (y + k) % 4
            pairs.append((i * N_COL + j, ((to % 2) * 8 + i % 8) * N_COL + (to // 2) * 4 + j % 4))
    return pairs


def x_moves(k):
    return [(yh * 4 + x, yh * 4 + (x + k) % 4) for yh in range(2) for x in range(4)]


def y_moves():
    return [(yh * 4 + x, (1 - yh) * 4 + x) for yh in range(2) for x in range(4)]


def scatter4(total, me, axis, moves):
    quarter = total.shape[0] // 4
    parts = total.reshape(4, quarter, F)
    out = lax.dynamic_index_in_dim(parts, me, 0, False)
    for k in (2, 1, 3):
        send = lax.dynamic_index_in_dim(parts, (me + k) % 4, 0, False).astype(BF16)
        out = out + lax.ppermute(send, axis, moves(k)).astype(F32)
    return out


def by_giver(own, me, axis, moves):
    got = jnp.stack([own] + [lax.ppermute(own, axis, moves(k)) for k in (1, 2, 3)])
    return [got[(me - k) % 4] for k in range(4)]


def call(kernel, in_specs, outs, scratch=()):
    return pl.pallas_call(
        kernel,
        in_specs=in_specs,
        out_specs=jax.tree.map(lambda _: pl.BlockSpec(memory_space=pltpu.VMEM), outs),
        out_shape=outs,
        scratch_shapes=list(scratch),
        compiler_params=params(),
    )


def array(*shape, dtype=BF16):
    return jax.ShapeDtypeStruct(shape, dtype)


def shards(
    features, partition_of, weight, tile_values, tile_rows, tile_cols, tile_count, out_cotangent
):
    row = lax.axis_index("row")
    col = lax.axis_index("col")
    core, z, yl = row % 2, (row // 2) % 4, row // 8
    x, yh = col % 4, col // 4
    y = yh * 2 + yl
    vmem = pl.BlockSpec(memory_space=pltpu.VMEM)
    smem = pl.BlockSpec(memory_space=pltpu.SMEM)
    hbm = pl.BlockSpec(memory_space=pl.ANY)

    here, there = yl * 4, (1 - yl) * 4
    near = [here + (z - k) % 4 for k in range(4)]
    far = [there + (z - k) % 4 for k in range(4)]
    first = core == 0
    places = [
        near[0],
        jnp.where(first, near[1], far[0]),
        jnp.where(first, near[3], near[1]),
        jnp.where(first, near[2], near[3]),
        jnp.where(first, far[0], near[2]),
        far[1],
        far[3],
        far[2],
    ]
    meta = jnp.stack([core, x, yh, z] + places).astype(jnp.int32)

    swap = row_moves(lambda yl, z, c: (yl, z, 1 - c))
    tiles = tile_values.reshape(-1, TILE, TILE)
    part = partition_of.reshape(1, SLOTS)
    other_part = lax.ppermute(part, "row", swap)
    other_features = lax.ppermute(features, "row", swap)
    other_tiles = lax.ppermute(tiles, "row", swap)
    grouped = call(
        group_kernel,
        [smem, vmem, vmem, vmem, vmem],
        array(N_COL, 2, SLOTS // N_COL, HALF),
    )(meta, part, features, other_part, other_features)
    arrived = lax.all_to_all(grouped, "col", split_axis=0, concat_axis=0, tiled=True)
    plan = call(plan_kernel, [smem, vmem, vmem], array(8, PLAN, dtype=jnp.int32))(
        tile_count.reshape(1), tile_rows.reshape(1, -1), tile_cols.reshape(1, -1)
    )
    other_plan = lax.ppermute(plan, "row", swap)
    own = call(interleave_kernel, [vmem], array(2, SLOTS, HALF))(arrived)

    def hop(block, move0, move1):
        def move(yl, z, c):
            dy, dz = move1 if c else move0
            return (yl + dy) % 2, (z + dz) % 4, c

        return lax.ppermute(block, "row", row_moves(move))

    r1 = hop(own, (0, 1), (1, 0))
    r2 = hop(own, (0, 3), (0, 1))
    r3 = hop(own, (0, 2), (0, 3))
    r4 = hop(own, (1, 0), (0, 2))
    s1 = hop(r1, (1, 0), (0, 1))
    s2 = hop(jnp.where(first, r2, r1), (1, 0), (0, 3))
    s3 = hop(jnp.where(first, r3, r1), (1, 0), (0, 2))
    blocks = [
        b.reshape(2, N_ROW, N_COL * PER_PEER, HALF) for b in (own, r1, r2, r3, r4, s1, s2, s3)
    ]

    def tile_sums(part, outs):
        return pl.pallas_call(
            lambda *refs: tiles_kernel(part, *refs),
            in_specs=[smem, smem] + [hbm] * (2 + CHIPS),
            out_specs=[hbm] * len(outs),
            out_shape=outs,
            scratch_shapes=[
                pltpu.VMEM((SLOT_CAP + 1, TILE, TILE), BF16),
                pltpu.VMEM((CHIPS, 2, N_ROW, N_COL * PER_PEER, HALF), BF16),
                pltpu.VMEM((ROW_TILES, TILE, HALF), F32),
                pltpu.VMEM((2, 4, SLOTS, HALF), BF16),
                pltpu.SemaphoreType.DMA((CHIPS + 1,)),
                pltpu.SemaphoreType.DMA((4,)),
            ],
            compiler_params=params(),
        )(
            meta,
            jnp.where(core == part, plan, other_plan),
            tiles,
            other_tiles,
            *blocks,
        )

    row0 = tile_sums(0, [array(2, SLOTS, HALF)] * 4)
    got0 = [lax.ppermute(row0[k], "col", x_moves(k)) for k in (1, 2, 3)]
    keep1, send1 = tile_sums(1, [array(4, SLOTS, HALF)] * 2)
    got1 = lax.ppermute(send1, "col", y_moves())
    wide, narrow = array(SLOTS, HALF, dtype=F32), array(SLOTS, HALF)
    keep0, send0 = call(x_summed_kernel, [smem] + [vmem] * 4, [wide, narrow])(
        meta, row0[0], *got0
    )
    got0 = lax.ppermute(send0, "col", y_moves())
    keep1, *send1 = call(y_summed_kernel, [smem] + [vmem] * 2, [wide] + [narrow] * 3)(
        meta, keep1, got1
    )
    got1 = [lax.ppermute(send1[k - 1], "col", x_moves(k)) for k in (1, 2, 3)]
    mine, others = call(sums_kernel, [smem] + [vmem] * 6, [wide] * 2)(
        meta, keep0, got0, keep1, *got1
    )
    theirs = lax.ppermute(others, "row", swap)
    cotangent = lax.dynamic_slice_in_dim(out_cotangent, col * SLOTS, SLOTS, 0)
    activations, slope = call(layer_kernel, [smem] + [vmem] * 4, [array(SLOTS, F)] * 2)(
        meta, mine, theirs, weight, cotangent
    )
    other_slope = lax.ppermute(slope, "row", swap)
    half = call(gradient_kernel, [vmem] * 4, array(HALF, F, dtype=F32))(
        mine, others, slope, other_slope
    )

    z_moves = lambda k: row_moves(lambda yl, z, c: (yl, (z + k) % 4, c))
    eighth = scatter4(half, x, "col", x_moves)
    a, b, c, d = by_giver(eighth, z, "row", z_moves)
    eighth = (a + b) + (c + d)
    a, b, c, d = by_giver(eighth, y, ("row", "col"), all_moves_y)
    eighth = (a + b) + (c + d)
    half = jnp.concatenate(by_giver(eighth.astype(BF16), x, "col", x_moves))
    other = lax.ppermute(half, "row", swap)
    first = jnp.where(core == 0, half, other).astype(F32)
    second = jnp.where(core == 0, other, half).astype(F32)
    return activations, jnp.concatenate([first, second])


def solution(mesh):
    placed = (
        P(("row", "col"), None),
        P(("row", "col")),
        P(),
        P("row", "col", None, None, None),
        P("row", "col", None),
        P("row", "col", None),
        P("row", "col"),
        P("row", None),
    )
    return jax.shard_map(
        shards,
        mesh=mesh,
        in_specs=placed,
        out_specs=(P(("row", "col"), None), P()),
        check_vma=False,
    )
```

```python
import jax
import jax.numpy as jnp
from jax import lax
from jax.experimental import pallas as pl
from jax.experimental.pallas import tpu as pltpu
from jax.sharding import PartitionSpec as P

N_ROW = 16
N_COL = 8
TILE = 128
SLOTS = 512
F = 512
PER_PEER = 4
HALF = 256
CHIPS = 8
SLOT_CAP = 192
ROW_TILES = 32
GROUP_BITS = 2
GROUP = 1 << GROUP_BITS
PLAN = SLOT_CAP + ROW_TILES * (GROUP - 1)
UNROLL_BITS = 2
UNROLL = 1 << UNROLL_BITS
BF16 = jnp.bfloat16
F32 = jnp.float32


def params(limit=16):
    return pltpu.CompilerParams(vmem_limit_bytes=limit * 1024 * 1024)


def selection(position, rows, columns):
    wanted = lax.broadcasted_iota(jnp.int32, (rows, columns), 0)
    return jnp.where(position == wanted, 1.0, 0.0).astype(BF16)


def group_kernel(meta_ref, part_ref, features_ref, other_part_ref, other_ref, out_ref):
    core = meta_ref[0]
    devices = N_ROW * N_COL
    before = jnp.where(
        lax.broadcasted_iota(jnp.int32, (SLOTS, SLOTS), 0)
        < lax.broadcasted_iota(jnp.int32, (SLOTS, SLOTS), 1),
        1.0,
        0.0,
    ).astype(BF16)

    def grouped(part, rows):
        member = jnp.where(
            part == lax.broadcasted_iota(jnp.int32, (devices, SLOTS), 0), 1.0, 0.0
        )
        earlier = jnp.dot(member.astype(BF16), before, preferred_element_type=F32)
        rank = jnp.sum(member * earlier, axis=0, keepdims=True).astype(jnp.int32)
        place = ((part & (N_COL - 1)) * N_ROW + (part >> 3)) * PER_PEER + rank
        pick = selection(place, SLOTS, SLOTS)
        wanted = jnp.where(core == 0, rows[:, :HALF], rows[:, HALF:])
        picked = jnp.dot(pick, wanted, preferred_element_type=F32).astype(BF16)
        return picked.reshape(N_COL, 1, SLOTS // N_COL, HALF)

    out_ref[:, pl.ds(core, 1)] = grouped(part_ref[...], features_ref[...])
    out_ref[:, pl.ds(1 - core, 1)] = grouped(other_part_ref[...], other_ref[...])


def interleave_kernel(arrived_ref, out_ref):
    source = lax.broadcasted_iota(jnp.int32, (1, SLOTS), 1)
    giver, inner = source >> 6, source & 63
    place = (inner >> 2) * (N_COL * PER_PEER) + giver * PER_PEER + (inner & 3)
    pick = selection(place, SLOTS, SLOTS)
    for c in range(2):
        rows = arrived_ref[:, c].reshape(SLOTS, HALF)
        out_ref[c] = jnp.dot(pick, rows, preferred_element_type=F32).astype(BF16)


def plan_kernel(count_ref, rows_ref, cols_ref, plan_ref):
    slot = lax.broadcasted_iota(jnp.int32, (1, SLOT_CAP), 1)
    rows = rows_ref[...]
    live = slot < count_ref[0]
    kinds = lax.broadcasted_iota(jnp.int32, (ROW_TILES, SLOT_CAP), 0)
    member = jnp.where(live & (rows == kinds), 1.0, 0.0)
    before = jnp.where(
        lax.broadcasted_iota(jnp.int32, (SLOT_CAP, SLOT_CAP), 0)
        < lax.broadcasted_iota(jnp.int32, (SLOT_CAP, SLOT_CAP), 1),
        1.0,
        0.0,
    ).astype(BF16)
    earlier = jnp.dot(member.astype(BF16), before, preferred_element_type=F32)
    number = jnp.sum(member, axis=1, keepdims=True).astype(jnp.int32)
    groups = jnp.broadcast_to((number + (GROUP - 1)) >> GROUP_BITS, (ROW_TILES, TILE))
    below = jnp.where(
        lax.broadcasted_iota(jnp.int32, (ROW_TILES, ROW_TILES), 1)
        < lax.broadcasted_iota(jnp.int32, (ROW_TILES, ROW_TILES), 0),
        1.0,
        0.0,
    ).astype(BF16)
    groups = groups.astype(F32)
    start = jnp.dot(below, groups.astype(BF16), preferred_element_type=F32)[:, :1]
    total = jnp.sum(groups, axis=0, keepdims=True)[:, :1]
    place = jnp.sum(member * (GROUP * start + earlier + 1.0), axis=0, keepdims=True) - 1.0
    taken = selection(place.astype(jnp.int32), PLAN, SLOT_CAP)
    line = lax.broadcasted_iota(jnp.int32, (8, SLOT_CAP), 0)
    values = jnp.where(line == 0, slot - SLOT_CAP, jnp.where(line == 1, cols_ref[...], rows))
    found = lax.dot_general(
        values.astype(F32).astype(BF16),
        taken,
        (((1,), (1,)), ((), ())),
        preferred_element_type=F32,
    )
    line = lax.broadcasted_iota(jnp.int32, (8, PLAN), 0)
    found = jnp.where(line == 0, found + SLOT_CAP, jnp.where(line == 3, total, found))
    plan_ref[...] = found.astype(jnp.int32)


def stage_kernel(meta_ref, own_hbm, other_hbm, first_ref, second_ref, sems):
    core = meta_ref[0]
    refs = (first_ref, second_ref)
    for out in refs:
        out[SLOT_CAP] = jnp.zeros((TILE, TILE), BF16)
    for c in range(2):

        @pl.when(core == c)
        def _():
            for hbm, out, k in ((own_hbm, refs[c], 0), (other_hbm, refs[1 - c], 1)):
                pltpu.make_async_copy(hbm, out.at[pl.ds(0, SLOT_CAP)], sems.at[k]).start()

    for hbm, k in ((own_hbm, 0), (other_hbm, 1)):
        pltpu.make_async_copy(hbm, refs[k].at[pl.ds(0, SLOT_CAP)], sems.at[k]).wait()


def add_tiles(plan_ref, tiles, source, total):
    total[...] = jnp.zeros_like(total)

    def product(g):
        left, right = [], []
        for e in range(GROUP):
            u = plan_ref[1, g * GROUP + e]
            left.append(tiles[plan_ref[0, g * GROUP + e]])
            right.append(source[pl.ds((u & 3) * 2, 2), :, u >> 2].reshape(TILE, HALF))
        return jnp.dot(
            jnp.concatenate(left, axis=1),
            jnp.concatenate(right, axis=0),
            preferred_element_type=F32,
        )

    def some_groups(h, carry):
        found = [
            (plan_ref[2, (h * UNROLL + k) * GROUP], product(h * UNROLL + k))
            for k in range(UNROLL)
        ]
        for place, value in found:
            total[place] += value
        return carry

    lax.fori_loop(0, (plan_ref[3, 0] + UNROLL - 1) >> UNROLL_BITS, some_groups, 0)


def narrow_block(total, yh, x):
    rows = total[pl.ds((yh * 4 + x) * 4, 4)].astype(BF16)
    return rows.reshape(SLOTS, HALF)


def tiles_y_kernel(meta_ref, plan_ref, tiles, *refs):
    blocks, (keep_ref, send_ref, source) = refs[:CHIPS], refs[CHIPS : CHIPS + 3]
    total, sems = refs[CHIPS + 3 :]
    yh = meta_ref[2]
    copies = [
        pltpu.make_async_copy(blocks[k], source.at[meta_ref[4 + k]], sems.at[k])
        for k in range(CHIPS)
    ]
    for copy in copies:
        copy.start()
    for copy in copies:
        copy.wait()
    add_tiles(plan_ref, tiles, source, total)
    for out, to in ((send_ref, 1 - yh), (keep_ref, yh)):
        for x in range(4):
            out[x] = narrow_block(total, to, x)


def tiles_x_kernel(meta_ref, plan_ref, tiles, source, *refs):
    outs, total = refs[:4], refs[4]
    x = meta_ref[1]
    add_tiles(plan_ref, tiles, source, total)
    for k, out in enumerate(outs):
        for yh in range(2):
            out[yh] = narrow_block(total, yh, (x + k) & 3)


def x_summed_kernel(meta_ref, own_ref, a_ref, b_ref, c_ref, keep_ref, send_ref):
    yh = meta_ref[2]

    def summed(k):
        pair = own_ref[k].astype(F32) + a_ref[k].astype(F32)
        return pair + (b_ref[k].astype(F32) + c_ref[k].astype(F32))

    keep_ref[...] = summed(yh)
    send_ref[...] = summed(1 - yh).astype(BF16)


def y_summed_kernel(meta_ref, own_ref, got_ref, keep_ref, a_ref, b_ref, c_ref):
    x = meta_ref[1]

    def summed(k):
        return own_ref[k].astype(F32) + got_ref[k].astype(F32)

    keep_ref[...] = summed(x)
    for k, out in ((1, a_ref), (2, b_ref), (3, c_ref)):
        out[...] = summed((x + k) & 3).astype(BF16)


def sums_kernel(meta_ref, keep0, got0, keep1, a_ref, b_ref, c_ref, mine_ref, send_ref):
    core = meta_ref[0]
    first = keep0[...] + got0[...].astype(F32)
    second = keep1[...] + a_ref[...].astype(F32)
    second = second + (b_ref[...].astype(F32) + c_ref[...].astype(F32))
    mine_ref[...] = jnp.where(core == 0, first, second)
    send_ref[...] = jnp.where(core == 0, second, first)


def two_parts(value):
    high = value.astype(BF16)
    return high, (value - high.astype(F32)).astype(BF16)


def layer_kernel(meta_ref, mine_ref, got_ref, weight_ref, cotangent_ref, act_ref, slope_ref):
    core = meta_ref[0]
    pre = jnp.zeros((SLOTS, F), F32)
    for half, mixed in ((core, mine_ref[...]), (1 - core, got_ref[...])):
        weight = weight_ref[pl.ds(pl.multiple_of(half * HALF, HALF), HALF), :]
        for piece in two_parts(mixed):
            pre = pre + jnp.dot(piece, weight, preferred_element_type=F32)
    sigmoid = jax.nn.sigmoid(pre)
    act_ref[...] = (pre * sigmoid).astype(BF16)
    slope_ref[...] = (
        cotangent_ref[...].astype(F32) * (sigmoid * (1.0 + pre * (1.0 - sigmoid)))
    ).astype(BF16)


def gradient_kernel(mine_ref, other_ref, slope_ref, other_slope_ref, grad_ref):
    contract = (((0,), (0,)), ((), ()))
    grad = jnp.zeros((HALF, F), F32)
    for mixed, slope in ((mine_ref, slope_ref), (other_ref, other_slope_ref)):
        for piece in two_parts(mixed[...]):
            grad = grad + lax.dot_general(
                piece, slope[...], contract, preferred_element_type=F32
            )
    grad_ref[...] = grad * (1.0 / 256.0)


def row_moves(move):
    pairs = []
    for yl in range(2):
        for z in range(4):
            for c in range(2):
                a, b, d = move(yl, z, c)
                pairs.append(((yl * 4 + z) * 2 + c, (a * 4 + b) * 2 + d))
    return pairs


def all_moves_y(k):
    pairs = []
    for i in range(N_ROW):
        for j in range(N_COL):
            y = (j // 4) * 2 + i // 8
            to = (y + k) % 4
            pairs.append((i * N_COL + j, ((to % 2) * 8 + i % 8) * N_COL + (to // 2) * 4 + j % 4))
    return pairs


def x_moves(k):
    return [(yh * 4 + x, yh * 4 + (x + k) % 4) for yh in range(2) for x in range(4)]


def y_moves():
    return [(yh * 4 + x, (1 - yh) * 4 + x) for yh in range(2) for x in range(4)]


def scatter4(total, me, axis, moves):
    quarter = total.shape[0] // 4
    parts = total.reshape(4, quarter, F)
    out = lax.dynamic_index_in_dim(parts, me, 0, False)
    for k in (2, 1, 3):
        send = lax.dynamic_index_in_dim(parts, (me + k) % 4, 0, False).astype(BF16)
        out = out + lax.ppermute(send, axis, moves(k)).astype(F32)
    return out


def by_giver(own, me, axis, moves):
    got = jnp.stack([own] + [lax.ppermute(own, axis, moves(k)) for k in (1, 2, 3)])
    return [got[(me - k) % 4] for k in range(4)]


def call(kernel, in_specs, outs, scratch=(), limit=16):
    made = pl.pallas_call(
        kernel,
        in_specs=in_specs,
        out_specs=jax.tree.map(lambda _: pl.BlockSpec(memory_space=pltpu.VMEM), outs),
        out_shape=outs,
        scratch_shapes=list(scratch),
        compiler_params=params(limit),
    )

    def run(*operands):
        held = [
            pltpu.with_memory_space_constraint(o, pltpu.VMEM)
            if spec.memory_space == pltpu.VMEM
            else o
            for spec, o in zip(in_specs, operands)
        ]
        return made(*held)

    return run


def array(*shape, dtype=BF16):
    return jax.ShapeDtypeStruct(shape, dtype)


def held(*shape, dtype=BF16):
    return pltpu.VMEM(shape, dtype)


def after(value, *others):
    return lax.optimization_barrier((value, *others))[0]


def shards(
    features, partition_of, weight, tile_values, tile_rows, tile_cols, tile_count, out_cotangent
):
    row = lax.axis_index("row")
    col = lax.axis_index("col")
    core, z, yl = row % 2, (row // 2) % 4, row // 8
    x, yh = col % 4, col // 4
    y = yh * 2 + yl
    vmem = pl.BlockSpec(memory_space=pltpu.VMEM)
    smem = pl.BlockSpec(memory_space=pltpu.SMEM)
    hbm = pl.BlockSpec(memory_space=pl.ANY)

    here, there = yl * 4, (1 - yl) * 4
    near = [here + (z - k) % 4 for k in range(4)]
    far = [there + (z - k) % 4 for k in range(4)]
    first = core == 0
    places = [
        near[0],
        jnp.where(first, near[1], far[0]),
        jnp.where(first, near[3], near[1]),
        jnp.where(first, near[2], near[3]),
        jnp.where(first, far[0], near[2]),
        far[1],
        far[3],
        far[2],
    ]
    meta = jnp.stack([core, x, yh, z] + places).astype(jnp.int32)

    swap = row_moves(lambda yl, z, c: (yl, z, 1 - c))
    tiles = tile_values.reshape(-1, TILE, TILE)
    part = partition_of.reshape(1, SLOTS)
    other_part = lax.ppermute(part, "row", swap)
    other_features = lax.ppermute(features, "row", swap)
    plan = call(plan_kernel, [smem, vmem, vmem], array(8, PLAN, dtype=jnp.int32))(
        tile_count.reshape(1), tile_rows.reshape(1, -1), tile_cols.reshape(1, -1)
    )
    other_plan = lax.ppermute(plan, "row", swap)
    other_features = after(other_features, other_plan)
    plans = [jnp.where(core == c, plan, other_plan) for c in range(2)]
    other_tiles = lax.ppermute(after(tiles, other_features), "row", swap)
    grouped = call(
        group_kernel,
        [smem, vmem, vmem, vmem, vmem],
        held(N_COL, 2, SLOTS // N_COL, HALF),
    )(meta, part, features, other_part, other_features)
    arrived = lax.all_to_all(grouped, "col", split_axis=0, concat_axis=0, tiled=True)
    own = call(interleave_kernel, [vmem], array(2, SLOTS, HALF))(arrived)
    own = after(own, other_tiles)

    tiles0, tiles1 = call(
        stage_kernel,
        [smem, hbm, hbm],
        [held(SLOT_CAP + 1, TILE, TILE)] * 2,
        [pltpu.SemaphoreType.DMA((2,))],
    )(meta, tiles, after(other_tiles, own))

    def hop(block, move0, move1):
        def move(yl, z, c):
            dy, dz = move1 if c else move0
            return (yl + dy) % 2, (z + dz) % 4, c

        return lax.ppermute(block, "row", row_moves(move))

    r1 = hop(own, (0, 1), (1, 0))
    r2 = hop(own, (0, 3), (0, 1))
    r3 = hop(own, (0, 2), (0, 3))
    r4 = hop(own, (1, 0), (0, 2))
    s1 = hop(r1, (1, 0), (0, 1))
    s2 = hop(jnp.where(first, r2, r1), (1, 0), (0, 3))
    s3 = hop(jnp.where(first, r3, r1), (1, 0), (0, 2))
    blocks = [
        b.reshape(2, N_ROW, N_COL * PER_PEER, HALF) for b in (own, r1, r2, r3, r4, s1, s2, s3)
    ]

    total = pltpu.VMEM((ROW_TILES, TILE, HALF), F32)
    source = held(CHIPS, 2, N_ROW, N_COL * PER_PEER, HALF)
    keep1, send1, source = call(
        tiles_y_kernel,
        [smem, smem, vmem] + [hbm] * CHIPS,
        [held(4, SLOTS, HALF), held(4, SLOTS, HALF), source],
        [total, pltpu.SemaphoreType.DMA((CHIPS,))],
    )(meta, plans[1], tiles1, *blocks)
    row0 = call(
        tiles_x_kernel,
        [smem, smem, vmem, vmem],
        [held(2, SLOTS, HALF)] * 4,
        [total],
    )(meta, plans[0], tiles0, source)
    got0 = [lax.ppermute(row0[k], "col", x_moves(k)) for k in (1, 2, 3)]
    got1 = lax.ppermute(send1, "col", y_moves())
    wide, narrow = held(SLOTS, HALF, dtype=F32), held(SLOTS, HALF)
    keep1, *send1 = call(y_summed_kernel, [smem] + [vmem] * 2, [wide] + [narrow] * 3)(
        meta, keep1, got1
    )
    keep0, send0 = call(x_summed_kernel, [smem] + [vmem] * 4, [wide, narrow])(
        meta, after(row0[0], *send1), *got0
    )
    got0 = lax.ppermute(send0, "col", y_moves())
    got1 = [lax.ppermute(send1[k - 1], "col", x_moves(k)) for k in (1, 2, 3)]
    mine, others = call(sums_kernel, [smem] + [vmem] * 6, [wide] * 2)(
        meta, keep0, got0, keep1, *got1
    )
    theirs = lax.ppermute(others, "row", swap)
    cotangent = lax.dynamic_slice_in_dim(out_cotangent, col * SLOTS, SLOTS, 0)
    activations, slope = call(
        layer_kernel, [smem] + [vmem] * 4, [array(SLOTS, F), held(SLOTS, F)]
    )(
        meta, mine, theirs, weight, cotangent
    )
    other_slope = lax.ppermute(slope, "row", swap)
    half = call(gradient_kernel, [vmem] * 4, held(HALF, F, dtype=F32))(
        mine, others, slope, other_slope
    )

    z_moves = lambda k: row_moves(lambda yl, z, c: (yl, (z + k) % 4, c))
    eighth = scatter4(half, x, "col", x_moves)
    a, b, c, d = by_giver(eighth, z, "row", z_moves)
    eighth = (a + b) + (c + d)
    a, b, c, d = by_giver(eighth, y, ("row", "col"), all_moves_y)
    eighth = (a + b) + (c + d)
    half = jnp.concatenate(by_giver(eighth.astype(BF16), x, "col", x_moves))
    other = lax.ppermute(half, "row", swap)
    first = jnp.where(core == 0, half, other).astype(F32)
    second = jnp.where(core == 0, other, half).astype(F32)
    return activations, jnp.concatenate([first, second])


def solution(mesh):
    placed = (
        P(("row", "col"), None),
        P(("row", "col")),
        P(),
        P("row", "col", None, None, None),
        P("row", "col", None),
        P("row", "col", None),
        P("row", "col"),
        P("row", None),
    )
    return jax.shard_map(
        shards,
        mesh=mesh,
        in_specs=placed,
        out_specs=(P(("row", "col"), None), P()),
        check_vma=False,
    )
```

```python
import jax
import jax.numpy as jnp
from jax import lax
from jax.experimental import pallas as pl
from jax.experimental.pallas import tpu as pltpu
from jax.sharding import PartitionSpec as P

N_ROW = 16
N_COL = 8
TILE = 128
SLOTS = 512
F = 512
PER_PEER = 4
HALF = 256
CHIPS = 8
BLOCKS = CHIPS + 2
SLOT_CAP = 192
ROW_TILES = 32
GROUP_BITS = 2
GROUP = 1 << GROUP_BITS
PLAN = SLOT_CAP + ROW_TILES * (GROUP - 1)
UNROLL_BITS = 2
UNROLL = 1 << UNROLL_BITS
BF16 = jnp.bfloat16
F32 = jnp.float32


def params(limit=16):
    return pltpu.CompilerParams(vmem_limit_bytes=limit * 1024 * 1024)


def selection(position, rows, columns):
    wanted = lax.broadcasted_iota(jnp.int32, (rows, columns), 0)
    return jnp.where(position == wanted, 1.0, 0.0).astype(BF16)


def group_kernel(
    meta_ref, part_ref, features_hbm, other_part_ref, other_ref, out_ref, features_ref, sem
):
    copy = pltpu.make_async_copy(features_hbm, features_ref, sem)
    copy.start()
    core = meta_ref[0]
    devices = N_ROW * N_COL
    before = jnp.where(
        lax.broadcasted_iota(jnp.int32, (SLOTS, SLOTS), 0)
        < lax.broadcasted_iota(jnp.int32, (SLOTS, SLOTS), 1),
        1.0,
        0.0,
    ).astype(BF16)

    def grouped(part, rows):
        member = jnp.where(
            part == lax.broadcasted_iota(jnp.int32, (devices, SLOTS), 0), 1.0, 0.0
        )
        earlier = jnp.dot(member.astype(BF16), before, preferred_element_type=F32)
        rank = jnp.sum(member * earlier, axis=0, keepdims=True).astype(jnp.int32)
        place = ((part & (N_COL - 1)) * N_ROW + (part >> 3)) * PER_PEER + rank
        pick = selection(place, SLOTS, SLOTS)
        wanted = jnp.where(core == 0, rows[:, :HALF], rows[:, HALF:])
        picked = jnp.dot(pick, wanted, preferred_element_type=F32).astype(BF16)
        return picked.reshape(N_COL, 1, SLOTS // N_COL, HALF)

    out_ref[:, pl.ds(1 - core, 1)] = grouped(other_part_ref[...], other_ref[...])
    copy.wait()
    out_ref[:, pl.ds(core, 1)] = grouped(part_ref[...], features_ref[...])


def interleave_kernel(arrived_ref, out_ref):
    source = lax.broadcasted_iota(jnp.int32, (1, SLOTS), 1)
    giver, inner = source >> 6, source & 63
    place = (inner >> 2) * (N_COL * PER_PEER) + giver * PER_PEER + (inner & 3)
    pick = selection(place, SLOTS, SLOTS)
    for c in range(2):
        rows = arrived_ref[:, c].reshape(SLOTS, HALF)
        out_ref[c] = jnp.dot(pick, rows, preferred_element_type=F32).astype(BF16)


def plan_kernel(count_ref, rows_ref, cols_ref, plan_ref):
    slot = lax.broadcasted_iota(jnp.int32, (1, SLOT_CAP), 1)
    rows = rows_ref[...]
    live = slot < count_ref[0]
    kinds = lax.broadcasted_iota(jnp.int32, (ROW_TILES, SLOT_CAP), 0)
    member = jnp.where(live & (rows == kinds), 1.0, 0.0)
    before = jnp.where(
        lax.broadcasted_iota(jnp.int32, (SLOT_CAP, SLOT_CAP), 0)
        < lax.broadcasted_iota(jnp.int32, (SLOT_CAP, SLOT_CAP), 1),
        1.0,
        0.0,
    ).astype(BF16)
    earlier = jnp.dot(member.astype(BF16), before, preferred_element_type=F32)
    number = jnp.sum(member, axis=1, keepdims=True).astype(jnp.int32)
    groups = jnp.broadcast_to((number + (GROUP - 1)) >> GROUP_BITS, (ROW_TILES, TILE))
    below = jnp.where(
        lax.broadcasted_iota(jnp.int32, (ROW_TILES, ROW_TILES), 1)
        < lax.broadcasted_iota(jnp.int32, (ROW_TILES, ROW_TILES), 0),
        1.0,
        0.0,
    ).astype(BF16)
    groups = groups.astype(F32)
    start = jnp.dot(below, groups.astype(BF16), preferred_element_type=F32)[:, :1]
    total = jnp.sum(groups, axis=0, keepdims=True)[:, :1]
    place = jnp.sum(member * (GROUP * start + earlier + 1.0), axis=0, keepdims=True) - 1.0
    taken = selection(place.astype(jnp.int32), PLAN, SLOT_CAP)
    line = lax.broadcasted_iota(jnp.int32, (8, SLOT_CAP), 0)
    values = jnp.where(line == 0, slot - SLOT_CAP, jnp.where(line == 1, cols_ref[...], rows))
    found = lax.dot_general(
        values.astype(F32).astype(BF16),
        taken,
        (((1,), (1,)), ((), ())),
        preferred_element_type=F32,
    )
    line = lax.broadcasted_iota(jnp.int32, (8, PLAN), 0)
    found = jnp.where(line == 0, found + SLOT_CAP, jnp.where(line == 3, total, found))
    plan_ref[...] = found.astype(jnp.int32)


def stage_kernel(meta_ref, own_hbm, other_hbm, first_ref, second_ref, sems):
    core = meta_ref[0]
    refs = (first_ref, second_ref)
    for out in refs:
        out[SLOT_CAP] = jnp.zeros((TILE, TILE), BF16)
    for c in range(2):

        @pl.when(core == c)
        def _():
            for hbm, out, k in ((own_hbm, refs[c], 0), (other_hbm, refs[1 - c], 1)):
                pltpu.make_async_copy(hbm, out.at[pl.ds(0, SLOT_CAP)], sems.at[k]).start()

    for hbm, k in ((own_hbm, 0), (other_hbm, 1)):
        pltpu.make_async_copy(hbm, refs[k].at[pl.ds(0, SLOT_CAP)], sems.at[k]).wait()


def add_tiles(plan_ref, tiles, source, total):
    total[...] = jnp.zeros_like(total)

    def product(g):
        left, right = [], []
        for e in range(GROUP):
            u = plan_ref[1, g * GROUP + e]
            left.append(tiles[plan_ref[0, g * GROUP + e]])
            right.append(source[pl.ds((u & 3) * 2, 2), :, u >> 2].reshape(TILE, HALF))
        return jnp.dot(
            jnp.concatenate(left, axis=1),
            jnp.concatenate(right, axis=0),
            preferred_element_type=F32,
        )

    def some_groups(h, carry):
        found = [
            (plan_ref[2, (h * UNROLL + k) * GROUP], product(h * UNROLL + k))
            for k in range(UNROLL)
        ]
        for place, value in found:
            total[place] += value
        return carry

    lax.fori_loop(0, (plan_ref[3, 0] + UNROLL - 1) >> UNROLL_BITS, some_groups, 0)


def narrow_block(total, yh, x):
    rows = total[pl.ds((yh * 4 + x) * 4, 4)].astype(BF16)
    return rows.reshape(SLOTS, HALF)


def tiles_y_kernel(meta_ref, plan_ref, tiles, *refs):
    blocks, (keep_ref, send_ref, source) = refs[:BLOCKS], refs[BLOCKS : BLOCKS + 3]
    total, sems = refs[BLOCKS + 3 :]
    yh = meta_ref[2]
    copies = [
        pltpu.make_async_copy(blocks[k], source.at[meta_ref[4 + k]], sems.at[k])
        for k in range(BLOCKS)
    ]
    for copy in copies:
        copy.start()
    for copy in copies:
        copy.wait()
    add_tiles(plan_ref, tiles, source, total)
    for out, to in ((send_ref, 1 - yh), (keep_ref, yh)):
        for x in range(4):
            out[x] = narrow_block(total, to, x)


def tiles_x_kernel(meta_ref, plan_ref, tiles, source, *refs):
    outs, total = refs[:4], refs[4]
    x = meta_ref[1]
    add_tiles(plan_ref, tiles, source, total)
    for k, out in enumerate(outs):
        for yh in range(2):
            out[yh] = narrow_block(total, yh, (x + k) & 3)


def x_summed_kernel(meta_ref, own_ref, a_ref, b_ref, c_ref, keep_ref, send_ref):
    yh = meta_ref[2]

    def summed(k):
        pair = own_ref[k].astype(F32) + a_ref[k].astype(F32)
        return pair + (b_ref[k].astype(F32) + c_ref[k].astype(F32))

    keep_ref[...] = summed(yh)
    send_ref[...] = summed(1 - yh).astype(BF16)


def y_summed_kernel(meta_ref, own_ref, got_ref, keep_ref, a_ref, b_ref, c_ref):
    x = meta_ref[1]

    def summed(k):
        return own_ref[k].astype(F32) + got_ref[k].astype(F32)

    keep_ref[...] = summed(x)
    for k, out in ((1, a_ref), (2, b_ref), (3, c_ref)):
        out[...] = summed((x + k) & 3).astype(BF16)


def sums_kernel(meta_ref, keep0, got0, keep1, a_ref, b_ref, c_ref, mine_ref, send_ref):
    core = meta_ref[0]
    first = keep0[...] + got0[...].astype(F32)
    second = keep1[...] + a_ref[...].astype(F32)
    second = second + (b_ref[...].astype(F32) + c_ref[...].astype(F32))
    mine_ref[...] = jnp.where(core == 0, first, second)
    send_ref[...] = jnp.where(core == 0, second, first)


def two_parts(value):
    high = value.astype(BF16)
    return high, (value - high.astype(F32)).astype(BF16)


def layer_kernel(meta_ref, mine_ref, got_ref, weight_ref, cotangent_ref, act_ref, slope_ref):
    core = meta_ref[0]
    pre = jnp.zeros((SLOTS, F), F32)
    for half, mixed in ((core, mine_ref[...]), (1 - core, got_ref[...])):
        weight = weight_ref[pl.ds(pl.multiple_of(half * HALF, HALF), HALF), :]
        for piece in two_parts(mixed):
            pre = pre + jnp.dot(piece, weight, preferred_element_type=F32)
    sigmoid = jax.nn.sigmoid(pre)
    act_ref[...] = (pre * sigmoid).astype(BF16)
    slope_ref[...] = (
        cotangent_ref[...].astype(F32) * (sigmoid * (1.0 + pre * (1.0 - sigmoid)))
    ).astype(BF16)


def gradient_kernel(mine_ref, other_ref, slope_ref, other_slope_ref, grad_ref):
    contract = (((0,), (0,)), ((), ()))
    grad = jnp.zeros((HALF, F), F32)
    for mixed, slope in ((mine_ref, slope_ref), (other_ref, other_slope_ref)):
        for piece in two_parts(mixed[...]):
            grad = grad + lax.dot_general(
                piece, slope[...], contract, preferred_element_type=F32
            )
    grad_ref[...] = (grad * (1.0 / 256.0)).astype(BF16)


def row_moves(move):
    pairs = []
    for yl in range(2):
        for z in range(4):
            for c in range(2):
                to = move(yl, z, c)
                if to is not None:
                    a, b, d = to
                    pairs.append(((yl * 4 + z) * 2 + c, (a * 4 + b) * 2 + d))
    return pairs


def x_moves(k):
    return [(yh * 4 + x, yh * 4 + (x + k) % 4) for yh in range(2) for x in range(4)]


def y_moves():
    return [(yh * 4 + x, (1 - yh) * 4 + x) for yh in range(2) for x in range(4)]


def exchange(parts, axis, groups=None):
    return lax.all_to_all(
        parts, axis, split_axis=0, concat_axis=0, axis_index_groups=groups, tiled=True
    )


def added(parts):
    parts = parts.astype(F32)
    a = (parts[0] + parts[1]) + (parts[2] + parts[3])
    return a + ((parts[4] + parts[5]) + (parts[6] + parts[7]))


def call(kernel, in_specs, outs, scratch=(), limit=16):
    made = pl.pallas_call(
        kernel,
        in_specs=in_specs,
        out_specs=jax.tree.map(lambda _: pl.BlockSpec(memory_space=pltpu.VMEM), outs),
        out_shape=outs,
        scratch_shapes=list(scratch),
        compiler_params=params(limit),
    )

    def run(*operands):
        held = [
            pltpu.with_memory_space_constraint(o, spec.memory_space)
            if spec.memory_space in (pltpu.VMEM, pltpu.MemorySpace.HBM)
            else o
            for spec, o in zip(in_specs, operands)
        ]
        return made(*held)

    return run


def array(*shape, dtype=BF16):
    return jax.ShapeDtypeStruct(shape, dtype)


def held(*shape, dtype=BF16):
    return pltpu.VMEM(shape, dtype)


def after(value, *others):
    return lax.optimization_barrier((value, *others))[0]


def shards(
    features, partition_of, weight, tile_values, tile_rows, tile_cols, tile_count, out_cotangent
):
    row = lax.axis_index("row")
    col = lax.axis_index("col")
    core, z, yl = row % 2, (row // 2) % 4, row // 8
    x, yh = col % 4, col // 4
    vmem = pl.BlockSpec(memory_space=pltpu.VMEM)
    smem = pl.BlockSpec(memory_space=pltpu.SMEM)
    hbm = pl.BlockSpec(memory_space=pl.ANY)
    pinned = pl.BlockSpec(memory_space=pltpu.MemorySpace.HBM)

    here, there = yl * 4, (1 - yl) * 4
    near = [here + (z - k) % 4 for k in range(4)]
    far = [there + (z - k) % 4 for k in range(4)]
    first = core == 0
    places = [
        near[0],
        jnp.where(first, near[1], far[0]),
        jnp.where(first, near[3], CHIPS),
        jnp.where(first, near[2], CHIPS + 1),
        jnp.where(first, far[0], near[1]),
        far[1],
        jnp.where(first, far[3], near[3]),
        jnp.where(first, far[2], near[2]),
        jnp.where(first, CHIPS, far[3]),
        jnp.where(first, CHIPS + 1, far[2]),
    ]
    meta = jnp.stack([core, x, yh, z] + places).astype(jnp.int32)

    swap = row_moves(lambda yl, z, c: (yl, z, 1 - c))
    tiles = tile_values.reshape(-1, TILE, TILE)
    part = partition_of.reshape(1, SLOTS)
    other_part = lax.ppermute(part, "row", swap)
    other_features = lax.ppermute(features, "row", swap)
    plan = call(plan_kernel, [smem, vmem, vmem], array(8, PLAN, dtype=jnp.int32))(
        tile_count.reshape(1), tile_rows.reshape(1, -1), tile_cols.reshape(1, -1)
    )
    other_plan = lax.ppermute(plan, "row", swap)
    plans = [jnp.where(core == c, plan, other_plan) for c in range(2)]
    other_tiles = lax.ppermute(after(tiles, other_features, other_part), "row", swap)
    grouped = call(
        group_kernel,
        [smem, vmem, pinned, vmem, vmem],
        held(N_COL, 2, SLOTS // N_COL, HALF),
        [pltpu.VMEM((SLOTS, F), BF16), pltpu.SemaphoreType.DMA],
    )(meta, part, features, other_part, other_features)
    arrived = lax.all_to_all(grouped, "col", split_axis=0, concat_axis=0, tiled=True)
    own = call(interleave_kernel, [vmem], array(2, SLOTS, HALF))(arrived)
    own = after(own, other_tiles, other_plan)

    tiles0, tiles1 = call(
        stage_kernel,
        [smem, pinned, pinned],
        [held(SLOT_CAP + 1, TILE, TILE)] * 2,
        [pltpu.SemaphoreType.DMA((2,))],
    )(meta, tiles, after(other_tiles, own))

    def hop(block, *moves):
        def move(yl, z, c):
            if moves[c] is None:
                return None
            return (yl + moves[c][0]) % 2, (z + moves[c][1]) % 4, c

        return lax.ppermute(block, "row", row_moves(move))

    r1 = hop(own, (0, 1), (1, 0))
    r2 = hop(own, (0, 3), None)
    r3 = hop(own, (0, 2), None)
    r4 = hop(own, (1, 0), (0, 1))
    s1 = hop(r1, (1, 0), (0, 1))
    second = jnp.where(first, after(r2, r1), own)
    s2 = hop(second, (1, 0), (0, 3))
    s3 = hop(jnp.where(first, after(r3, second), own), (1, 0), (0, 2))
    s4 = hop(r1, None, (0, 3))
    s5 = hop(r1, None, (0, 2))
    blocks = [
        b.reshape(2, N_ROW, N_COL * PER_PEER, HALF)
        for b in (own, r1, r2, r3, r4, s1, s2, s3, s4, s5)
    ]

    total = pltpu.VMEM((ROW_TILES, TILE, HALF), F32)
    source = held(BLOCKS, 2, N_ROW, N_COL * PER_PEER, HALF)
    keep1, send1, source = call(
        tiles_y_kernel,
        [smem, smem, vmem] + [hbm] * BLOCKS,
        [held(4, SLOTS, HALF), held(4, SLOTS, HALF), source],
        [total, pltpu.SemaphoreType.DMA((BLOCKS,))],
    )(meta, plans[1], tiles1, *blocks)
    row0 = call(
        tiles_x_kernel,
        [smem, smem, vmem, vmem],
        [held(2, SLOTS, HALF)] * 4,
        [total],
    )(meta, plans[0], tiles0, source)
    got0 = [lax.ppermute(row0[k], "col", x_moves(k)) for k in (1, 2, 3)]
    got1 = lax.ppermute(send1, "col", y_moves())
    wide, narrow = held(SLOTS, HALF, dtype=F32), held(SLOTS, HALF)
    keep1, *send1 = call(y_summed_kernel, [smem] + [vmem] * 2, [wide] + [narrow] * 3)(
        meta, keep1, got1
    )
    keep0, send0 = call(x_summed_kernel, [smem] + [vmem] * 4, [wide, narrow])(
        meta, after(row0[0], *send1), *got0
    )
    got0 = lax.ppermute(send0, "col", y_moves())
    got1 = [lax.ppermute(send1[k - 1], "col", x_moves(k)) for k in (1, 2, 3)]
    mine, others = call(sums_kernel, [smem] + [vmem] * 6, [wide] * 2)(
        meta, keep0, got0, keep1, *got1
    )
    theirs = lax.ppermute(others, "row", swap)
    cotangent = lax.dynamic_slice_in_dim(out_cotangent, col * SLOTS, SLOTS, 0)
    activations, slope = call(
        layer_kernel, [smem] + [vmem] * 4, [array(SLOTS, F), held(SLOTS, F)]
    )(
        meta, mine, theirs, weight, cotangent
    )
    other_slope = lax.ppermute(slope, "row", swap)
    half = call(gradient_kernel, [vmem] * 4, held(HALF, F))(
        mine, others, slope, other_slope
    )

    same_core = [[chip * 2 + c for chip in range(CHIPS)] for c in range(2)]
    shape = (CHIPS, HALF // CHIPS, F)
    piece = added(exchange(half.reshape(shape), "row", same_core))
    piece = added(exchange(jnp.broadcast_to(piece, shape), "col"))
    half = exchange(jnp.broadcast_to(piece.astype(BF16), shape), "row", same_core)
    half = half.reshape(HALF, F)
    other = lax.ppermute(half, "row", swap)
    first = jnp.where(core == 0, half, other).astype(F32)
    second = jnp.where(core == 0, other, half).astype(F32)
    return activations, jnp.concatenate([first, second])


def solution(mesh):
    placed = (
        P(("row", "col"), None),
        P(("row", "col")),
        P(),
        P("row", "col", None, None, None),
        P("row", "col", None),
        P("row", "col", None),
        P("row", "col"),
        P("row", None),
    )
    return jax.shard_map(
        shards,
        mesh=mesh,
        in_specs=placed,
        out_specs=(P(("row", "col"), None), P()),
        check_vma=False,
    )
```

```python
import jax
import jax.numpy as jnp
from jax import lax
from jax.experimental import pallas as pl
from jax.experimental.pallas import tpu as pltpu
from jax.sharding import PartitionSpec as P

N_ROW = 16
N_COL = 8
TILE = 128
SLOTS = 512
F = 512
PER_PEER = 4
HALF = 256
CHIPS = 8
BLOCKS = CHIPS + 1
SLOT_CAP = 192
ROW_TILES = 32
GROUP_BITS = 2
GROUP = 1 << GROUP_BITS
PLAN = SLOT_CAP + ROW_TILES * (GROUP - 1)
UNROLL_BITS = 3
UNROLL = 1 << UNROLL_BITS
BF16 = jnp.bfloat16
F32 = jnp.float32


def params(limit=16):
    return pltpu.CompilerParams(vmem_limit_bytes=limit * 1024 * 1024)


def selection(position, rows, columns):
    wanted = lax.broadcasted_iota(jnp.int32, (rows, columns), 0)
    return jnp.where(position == wanted, 1.0, 0.0).astype(BF16)


def group_kernel(
    meta_ref, part_ref, features_hbm, other_part_ref, other_ref, out_ref, features_ref, sem
):
    copy = pltpu.make_async_copy(features_hbm, features_ref, sem)
    copy.start()
    core = meta_ref[0]
    devices = N_ROW * N_COL
    before = jnp.where(
        lax.broadcasted_iota(jnp.int32, (SLOTS, SLOTS), 0)
        < lax.broadcasted_iota(jnp.int32, (SLOTS, SLOTS), 1),
        1.0,
        0.0,
    ).astype(BF16)

    def grouped(part, rows):
        member = jnp.where(
            part == lax.broadcasted_iota(jnp.int32, (devices, SLOTS), 0), 1.0, 0.0
        )
        earlier = jnp.dot(member.astype(BF16), before, preferred_element_type=F32)
        rank = jnp.sum(member * earlier, axis=0, keepdims=True).astype(jnp.int32)
        place = ((part & (N_COL - 1)) * N_ROW + (part >> 3)) * PER_PEER + rank
        pick = selection(place, SLOTS, SLOTS)
        wanted = jnp.where(core == 0, rows[:, :HALF], rows[:, HALF:])
        picked = jnp.dot(pick, wanted, preferred_element_type=F32).astype(BF16)
        return picked.reshape(N_COL, 1, SLOTS // N_COL, HALF)

    out_ref[:, pl.ds(1 - core, 1)] = grouped(other_part_ref[...], other_ref[...])
    copy.wait()
    out_ref[:, pl.ds(core, 1)] = grouped(part_ref[...], features_ref[...])


def interleave_kernel(arrived_ref, out_ref):
    source = lax.broadcasted_iota(jnp.int32, (1, SLOTS), 1)
    giver, inner = source >> 6, source & 63
    place = (inner >> 2) * (N_COL * PER_PEER) + giver * PER_PEER + (inner & 3)
    pick = selection(place, SLOTS, SLOTS)
    for c in range(2):
        rows = arrived_ref[:, c].reshape(SLOTS, HALF)
        out_ref[c] = jnp.dot(pick, rows, preferred_element_type=F32).astype(BF16)


def plan_kernel(count_ref, rows_ref, cols_ref, plan_ref):
    slot = lax.broadcasted_iota(jnp.int32, (1, SLOT_CAP), 1)
    rows = rows_ref[...]
    live = slot < count_ref[0]
    kinds = lax.broadcasted_iota(jnp.int32, (ROW_TILES, SLOT_CAP), 0)
    member = jnp.where(live & (rows == kinds), 1.0, 0.0)
    before = jnp.where(
        lax.broadcasted_iota(jnp.int32, (SLOT_CAP, SLOT_CAP), 0)
        < lax.broadcasted_iota(jnp.int32, (SLOT_CAP, SLOT_CAP), 1),
        1.0,
        0.0,
    ).astype(BF16)
    earlier = jnp.dot(member.astype(BF16), before, preferred_element_type=F32)
    number = jnp.sum(member, axis=1, keepdims=True).astype(jnp.int32)
    groups = jnp.broadcast_to((number + (GROUP - 1)) >> GROUP_BITS, (ROW_TILES, TILE))
    below = jnp.where(
        lax.broadcasted_iota(jnp.int32, (ROW_TILES, ROW_TILES), 1)
        < lax.broadcasted_iota(jnp.int32, (ROW_TILES, ROW_TILES), 0),
        1.0,
        0.0,
    ).astype(BF16)
    groups = groups.astype(F32)
    start = jnp.dot(below, groups.astype(BF16), preferred_element_type=F32)[:, :1]
    total = jnp.sum(groups, axis=0, keepdims=True)[:, :1]
    place = jnp.sum(member * (GROUP * start + earlier + 1.0), axis=0, keepdims=True) - 1.0
    taken = selection(place.astype(jnp.int32), PLAN, SLOT_CAP)
    line = lax.broadcasted_iota(jnp.int32, (8, SLOT_CAP), 0)
    values = jnp.where(line == 0, slot - SLOT_CAP, jnp.where(line == 1, cols_ref[...], rows))
    found = lax.dot_general(
        values.astype(F32).astype(BF16),
        taken,
        (((1,), (1,)), ((), ())),
        preferred_element_type=F32,
    )
    line = lax.broadcasted_iota(jnp.int32, (8, PLAN), 0)
    found = jnp.where(line == 0, found + SLOT_CAP, jnp.where(line == 3, total, found))
    plan_ref[...] = found.astype(jnp.int32)


def stage_kernel(meta_ref, own_hbm, other_hbm, first_ref, second_ref, sems):
    core = meta_ref[0]
    refs = (first_ref, second_ref)
    for out in refs:
        out[SLOT_CAP] = jnp.zeros((TILE, TILE), BF16)
    for c in range(2):

        @pl.when(core == c)
        def _():
            for hbm, out, k in ((own_hbm, refs[c], 0), (other_hbm, refs[1 - c], 1)):
                pltpu.make_async_copy(hbm, out.at[pl.ds(0, SLOT_CAP)], sems.at[k]).start()

    for hbm, k in ((own_hbm, 0), (other_hbm, 1)):
        pltpu.make_async_copy(hbm, refs[k].at[pl.ds(0, SLOT_CAP)], sems.at[k]).wait()


def add_tiles(plan_ref, tiles, source, total):
    total[...] = jnp.zeros_like(total)

    def product(g):
        left, right = [], []
        for e in range(GROUP):
            u = plan_ref[1, g * GROUP + e]
            left.append(tiles[plan_ref[0, g * GROUP + e]])
            right.append(source[pl.ds((u & 3) * 2, 2), :, u >> 2].reshape(TILE, HALF))
        return jnp.dot(
            jnp.concatenate(left, axis=1),
            jnp.concatenate(right, axis=0),
            preferred_element_type=F32,
        )

    def some_groups(h, carry):
        found = [
            (plan_ref[2, (h * UNROLL + k) * GROUP], product(h * UNROLL + k))
            for k in range(UNROLL)
        ]
        for place, value in found:
            total[place] += value
        return carry

    lax.fori_loop(0, (plan_ref[3, 0] + UNROLL - 1) >> UNROLL_BITS, some_groups, 0)


def narrow_block(total, yh, x):
    rows = total[pl.ds((yh * 4 + x) * 4, 4)].astype(BF16)
    return rows.reshape(SLOTS, HALF)


def tiles_y_kernel(meta_ref, plan_ref, tiles, *refs):
    blocks, (keep_ref, send_ref, source) = refs[:BLOCKS], refs[BLOCKS : BLOCKS + 3]
    total, sems = refs[BLOCKS + 3 :]
    yh = meta_ref[2]
    copies = [
        pltpu.make_async_copy(blocks[k], source.at[meta_ref[4 + k]], sems.at[k])
        for k in range(BLOCKS)
    ]
    for copy in copies:
        copy.start()
    for copy in copies:
        copy.wait()
    add_tiles(plan_ref, tiles, source, total)
    for out, to in ((send_ref, 1 - yh), (keep_ref, yh)):
        for x in range(4):
            out[x] = narrow_block(total, to, x)


def tiles_x_kernel(meta_ref, plan_ref, tiles, source, *refs):
    outs, total = refs[:4], refs[4]
    x = meta_ref[1]
    add_tiles(plan_ref, tiles, source, total)
    for k, out in enumerate(outs):
        for yh in range(2):
            out[yh] = narrow_block(total, yh, (x + k) & 3)


def x_summed_kernel(meta_ref, own_ref, a_ref, b_ref, c_ref, keep_ref, send_ref):
    yh = meta_ref[2]

    def summed(k):
        pair = own_ref[k].astype(F32) + a_ref[k].astype(F32)
        return pair + (b_ref[k].astype(F32) + c_ref[k].astype(F32))

    keep_ref[...] = summed(yh)
    send_ref[...] = summed(1 - yh).astype(BF16)


def y_summed_kernel(meta_ref, own_ref, got_ref, keep_ref, a_ref, b_ref, c_ref):
    x = meta_ref[1]

    def summed(k):
        return own_ref[k].astype(F32) + got_ref[k].astype(F32)

    keep_ref[...] = summed(x)
    for k, out in ((1, a_ref), (2, b_ref), (3, c_ref)):
        out[...] = summed((x + k) & 3).astype(BF16)


def sums_kernel(meta_ref, keep0, got0, keep1, a_ref, b_ref, c_ref, mine_ref, send_ref):
    core = meta_ref[0]
    first = keep0[...] + got0[...].astype(F32)
    second = keep1[...] + a_ref[...].astype(F32)
    second = second + (b_ref[...].astype(F32) + c_ref[...].astype(F32))
    mine_ref[...] = jnp.where(core == 0, first, second)
    send_ref[...] = jnp.where(core == 0, second, first)


def two_parts(value):
    high = value.astype(BF16)
    return high, (value - high.astype(F32)).astype(BF16)


def layer_kernel(meta_ref, mine_ref, got_ref, weight_ref, cotangent_ref, act_ref, slope_ref):
    core = meta_ref[0]
    pre = jnp.zeros((SLOTS, F), F32)
    for half, mixed in ((core, mine_ref[...]), (1 - core, got_ref[...])):
        weight = weight_ref[pl.ds(pl.multiple_of(half * HALF, HALF), HALF), :]
        for piece in two_parts(mixed):
            pre = pre + jnp.dot(piece, weight, preferred_element_type=F32)
    sigmoid = jax.nn.sigmoid(pre)
    act_ref[...] = (pre * sigmoid).astype(BF16)
    slope_ref[...] = (
        cotangent_ref[...].astype(F32) * (sigmoid * (1.0 + pre * (1.0 - sigmoid)))
    ).astype(BF16)


def gradient_kernel(mine_ref, other_ref, slope_ref, other_slope_ref, grad_ref):
    contract = (((0,), (0,)), ((), ()))
    grad = jnp.zeros((HALF, F), F32)
    for mixed, slope in ((mine_ref, slope_ref), (other_ref, other_slope_ref)):
        for piece in two_parts(mixed[...]):
            grad = grad + lax.dot_general(
                piece, slope[...], contract, preferred_element_type=F32
            )
    grad_ref[...] = (grad * (1.0 / 256.0)).astype(BF16)


def row_moves(move):
    pairs = []
    for yl in range(2):
        for z in range(4):
            for c in range(2):
                to = move(yl, z, c)
                if to is not None:
                    a, b, d = to
                    pairs.append(((yl * 4 + z) * 2 + c, (a * 4 + b) * 2 + d))
    return pairs


def x_moves(k):
    return [(yh * 4 + x, yh * 4 + (x + k) % 4) for yh in range(2) for x in range(4)]


def y_moves():
    return [(yh * 4 + x, (1 - yh) * 4 + x) for yh in range(2) for x in range(4)]


def exchange(parts, axis, groups=None):
    return lax.all_to_all(
        parts, axis, split_axis=0, concat_axis=0, axis_index_groups=groups, tiled=True
    )


def added(parts):
    parts = parts.astype(F32)
    a = (parts[0] + parts[1]) + (parts[2] + parts[3])
    return a + ((parts[4] + parts[5]) + (parts[6] + parts[7]))


def call(kernel, in_specs, outs, scratch=(), limit=16):
    made = pl.pallas_call(
        kernel,
        in_specs=in_specs,
        out_specs=jax.tree.map(lambda _: pl.BlockSpec(memory_space=pltpu.VMEM), outs),
        out_shape=outs,
        scratch_shapes=list(scratch),
        compiler_params=params(limit),
    )

    def run(*operands):
        held = [
            pltpu.with_memory_space_constraint(o, spec.memory_space)
            if spec.memory_space in (pltpu.VMEM, pltpu.MemorySpace.HBM)
            else o
            for spec, o in zip(in_specs, operands)
        ]
        return made(*held)

    return run


def array(*shape, dtype=BF16):
    return jax.ShapeDtypeStruct(shape, dtype)


def held(*shape, dtype=BF16):
    return pltpu.VMEM(shape, dtype)


def after(value, *others):
    return lax.optimization_barrier((value, *others))[0]


def shards(
    features, partition_of, weight, tile_values, tile_rows, tile_cols, tile_count, out_cotangent
):
    row = lax.axis_index("row")
    col = lax.axis_index("col")
    core, z, yl = row % 2, (row // 2) % 4, row // 8
    x, yh = col % 4, col // 4
    vmem = pl.BlockSpec(memory_space=pltpu.VMEM)
    smem = pl.BlockSpec(memory_space=pltpu.SMEM)
    hbm = pl.BlockSpec(memory_space=pl.ANY)
    pinned = pl.BlockSpec(memory_space=pltpu.MemorySpace.HBM)

    here, there = yl * 4, (1 - yl) * 4
    near = [here + (z - k) % 4 for k in range(4)]
    far = [there + (z - k) % 4 for k in range(4)]
    first = core == 0
    places = [
        near[0],
        jnp.where(first, near[1], far[0]),
        near[3],
        near[2],
        jnp.where(first, far[0], near[1]),
        far[1],
        jnp.where(first, far[3], CHIPS),
        far[2],
        jnp.where(first, CHIPS, far[3]),
    ]
    meta = jnp.stack([core, x, yh, z] + places).astype(jnp.int32)

    swap = row_moves(lambda yl, z, c: (yl, z, 1 - c))
    tiles = tile_values.reshape(-1, TILE, TILE)
    part = partition_of.reshape(1, SLOTS)
    other_part = lax.ppermute(part, "row", swap)
    other_features = lax.ppermute(features, "row", swap)
    plan = call(plan_kernel, [smem, vmem, vmem], array(8, PLAN, dtype=jnp.int32))(
        tile_count.reshape(1), tile_rows.reshape(1, -1), tile_cols.reshape(1, -1)
    )
    other_plan = lax.ppermute(plan, "row", swap)
    plans = [jnp.where(core == c, plan, other_plan) for c in range(2)]
    grouped = call(
        group_kernel,
        [smem, vmem, pinned, vmem, vmem],
        held(N_COL, 2, SLOTS // N_COL, HALF),
        [pltpu.VMEM((SLOTS, F), BF16), pltpu.SemaphoreType.DMA],
    )(meta, part, features, other_part, other_features)
    other_tiles = lax.ppermute(after(tiles, grouped), "row", swap)
    arrived = lax.all_to_all(grouped, "col", split_axis=0, concat_axis=0, tiled=True)
    own = call(interleave_kernel, [vmem], array(2, SLOTS, HALF))(arrived)
    own = after(own, other_tiles, other_plan)

    tiles0, tiles1 = call(
        stage_kernel,
        [smem, pinned, pinned],
        [held(SLOT_CAP + 1, TILE, TILE)] * 2,
        [pltpu.SemaphoreType.DMA((2,))],
    )(meta, tiles, after(other_tiles, own))

    def hop(block, *moves):
        def move(yl, z, c):
            if moves[c] is None:
                return None
            return (yl + moves[c][0]) % 2, (z + moves[c][1]) % 4, c

        return lax.ppermute(block, "row", row_moves(move))

    r1 = hop(own, (0, 1), (1, 0))
    r2 = hop(own, (0, 3), (0, 3))
    r3 = hop(own, (0, 2), (0, 2))
    r4 = hop(own, (1, 0), (0, 1))
    s1 = hop(r1, (1, 0), (0, 1))
    s2 = hop(r2, (1, 0), None)
    s3 = hop(r3, (1, 0), (1, 0))
    s4 = hop(r1, None, (0, 3))
    blocks = [
        b.reshape(2, N_ROW, N_COL * PER_PEER, HALF)
        for b in (own, r1, r2, r3, r4, s1, s2, s3, s4)
    ]

    total = pltpu.VMEM((ROW_TILES, TILE, HALF), F32)
    source = held(BLOCKS, 2, N_ROW, N_COL * PER_PEER, HALF)
    keep1, send1, source = call(
        tiles_y_kernel,
        [smem, smem, vmem] + [hbm] * BLOCKS,
        [held(4, SLOTS, HALF), held(4, SLOTS, HALF), source],
        [total, pltpu.SemaphoreType.DMA((BLOCKS,))],
    )(meta, plans[1], tiles1, *blocks)
    row0 = call(
        tiles_x_kernel,
        [smem, smem, vmem, vmem],
        [held(2, SLOTS, HALF)] * 4,
        [total],
    )(meta, plans[0], tiles0, source)
    got0 = [lax.ppermute(row0[k], "col", x_moves(k)) for k in (1, 2, 3)]
    got1 = lax.ppermute(send1, "col", y_moves())
    wide, narrow = held(SLOTS, HALF, dtype=F32), held(SLOTS, HALF)
    keep1, *send1 = call(y_summed_kernel, [smem] + [vmem] * 2, [wide] + [narrow] * 3)(
        meta, keep1, got1
    )
    got1 = [lax.ppermute(send1[k - 1], "col", x_moves(k)) for k in (1, 2, 3)]
    keep0, send0 = call(x_summed_kernel, [smem] + [vmem] * 4, [wide, narrow])(
        meta, after(row0[0], got1[0]), *got0
    )
    got0 = lax.ppermute(send0, "col", y_moves())
    mine, others = call(sums_kernel, [smem] + [vmem] * 6, [wide] * 2)(
        meta, keep0, got0, keep1, *got1
    )
    theirs = lax.ppermute(others, "row", swap)
    cotangent = lax.dynamic_slice_in_dim(out_cotangent, col * SLOTS, SLOTS, 0)
    activations, slope = call(
        layer_kernel, [smem] + [vmem] * 4, [array(SLOTS, F), held(SLOTS, F)]
    )(
        meta, mine, theirs, weight, cotangent
    )
    other_slope = lax.ppermute(slope, "row", swap)
    half = call(gradient_kernel, [vmem] * 4, held(HALF, F))(
        mine, others, slope, other_slope
    )

    same_core = [[chip * 2 + c for chip in range(CHIPS)] for c in range(2)]
    shape = (CHIPS, HALF // CHIPS, F)
    piece = added(exchange(half.reshape(shape), "row", same_core))
    piece = added(exchange(jnp.broadcast_to(piece, shape), "col"))
    half = exchange(jnp.broadcast_to(piece.astype(BF16), shape), "row", same_core)
    half = half.reshape(HALF, F)
    other = lax.ppermute(half, "row", swap)
    first = jnp.where(core == 0, half, other).astype(F32)
    second = jnp.where(core == 0, other, half).astype(F32)
    return activations, jnp.concatenate([first, second])


def solution(mesh):
    placed = (
        P(("row", "col"), None),
        P(("row", "col")),
        P(),
        P("row", "col", None, None, None),
        P("row", "col", None),
        P("row", "col", None),
        P("row", "col"),
        P("row", None),
    )
    return jax.shard_map(
        shards,
        mesh=mesh,
        in_specs=placed,
        out_specs=(P(("row", "col"), None), P()),
        check_vma=False,
    )
```

```python
import jax
import jax.numpy as jnp
from jax import lax
from jax.experimental import pallas as pl
from jax.experimental.pallas import tpu as pltpu
from jax.sharding import PartitionSpec as P

N_ROW = 16
N_COL = 8
TILE = 128
SLOTS = 512
F = 512
PER_PEER = 4
HALF = 256
CHIPS = 8
SHARED = 4
BLOCKS = 2 * CHIPS - SHARED
SLOT_CAP = 192
ROW_TILES = 32
GROUP_BITS = 2
GROUP = 1 << GROUP_BITS
PLAN = SLOT_CAP + ROW_TILES * (GROUP - 1)
UNROLL_BITS = 3
UNROLL = 1 << UNROLL_BITS
BF16 = jnp.bfloat16
F32 = jnp.float32


def params(limit=16):
    return pltpu.CompilerParams(vmem_limit_bytes=limit * 1024 * 1024)


def selection(position, rows, columns):
    wanted = lax.broadcasted_iota(jnp.int32, (rows, columns), 0)
    return jnp.where(position == wanted, 1.0, 0.0).astype(BF16)


def group_kernel(
    meta_ref, part_ref, features_hbm, other_part_ref, other_ref, out_ref, features_ref, sem
):
    copy = pltpu.make_async_copy(features_hbm, features_ref, sem)
    copy.start()
    core = meta_ref[0]
    devices = N_ROW * N_COL
    before = jnp.where(
        lax.broadcasted_iota(jnp.int32, (SLOTS, SLOTS), 0)
        < lax.broadcasted_iota(jnp.int32, (SLOTS, SLOTS), 1),
        1.0,
        0.0,
    ).astype(BF16)

    def grouped(part, rows):
        member = jnp.where(
            part == lax.broadcasted_iota(jnp.int32, (devices, SLOTS), 0), 1.0, 0.0
        )
        earlier = jnp.dot(member.astype(BF16), before, preferred_element_type=F32)
        rank = jnp.sum(member * earlier, axis=0, keepdims=True).astype(jnp.int32)
        place = ((part & (N_COL - 1)) * N_ROW + (part >> 3)) * PER_PEER + rank
        pick = selection(place, SLOTS, SLOTS)
        wanted = jnp.where(core == 0, rows[:, :HALF], rows[:, HALF:])
        picked = jnp.dot(pick, wanted, preferred_element_type=F32).astype(BF16)
        return picked.reshape(N_COL, 1, SLOTS // N_COL, HALF)

    out_ref[:, pl.ds(1 - core, 1)] = grouped(other_part_ref[...], other_ref[...])
    copy.wait()
    out_ref[:, pl.ds(core, 1)] = grouped(part_ref[...], features_ref[...])


def interleave_kernel(arrived_ref, out_ref):
    source = lax.broadcasted_iota(jnp.int32, (1, SLOTS), 1)
    giver, inner = source >> 6, source & 63
    place = (inner >> 2) * (N_COL * PER_PEER) + giver * PER_PEER + (inner & 3)
    pick = selection(place, SLOTS, SLOTS)
    for c in range(2):
        rows = arrived_ref[:, c].reshape(SLOTS, HALF)
        out_ref[c] = jnp.dot(pick, rows, preferred_element_type=F32).astype(BF16)


def plan_kernel(count_ref, rows_ref, cols_ref, plan_ref):
    slot = lax.broadcasted_iota(jnp.int32, (1, SLOT_CAP), 1)
    rows = rows_ref[...]
    live = slot < count_ref[0]
    kinds = lax.broadcasted_iota(jnp.int32, (ROW_TILES, SLOT_CAP), 0)
    member = jnp.where(live & (rows == kinds), 1.0, 0.0)
    before = jnp.where(
        lax.broadcasted_iota(jnp.int32, (SLOT_CAP, SLOT_CAP), 0)
        < lax.broadcasted_iota(jnp.int32, (SLOT_CAP, SLOT_CAP), 1),
        1.0,
        0.0,
    ).astype(BF16)
    earlier = jnp.dot(member.astype(BF16), before, preferred_element_type=F32)
    number = jnp.sum(member, axis=1, keepdims=True).astype(jnp.int32)
    groups = jnp.broadcast_to((number + (GROUP - 1)) >> GROUP_BITS, (ROW_TILES, TILE))
    below = jnp.where(
        lax.broadcasted_iota(jnp.int32, (ROW_TILES, ROW_TILES), 1)
        < lax.broadcasted_iota(jnp.int32, (ROW_TILES, ROW_TILES), 0),
        1.0,
        0.0,
    ).astype(BF16)
    groups = groups.astype(F32)
    start = jnp.dot(below, groups.astype(BF16), preferred_element_type=F32)[:, :1]
    total = jnp.sum(groups, axis=0, keepdims=True)[:, :1]
    place = jnp.sum(member * (GROUP * start + earlier + 1.0), axis=0, keepdims=True) - 1.0
    taken = selection(place.astype(jnp.int32), PLAN, SLOT_CAP)
    line = lax.broadcasted_iota(jnp.int32, (8, SLOT_CAP), 0)
    values = jnp.where(line == 0, slot - SLOT_CAP, jnp.where(line == 1, cols_ref[...], rows))
    found = lax.dot_general(
        values.astype(F32).astype(BF16),
        taken,
        (((1,), (1,)), ((), ())),
        preferred_element_type=F32,
    )
    line = lax.broadcasted_iota(jnp.int32, (8, PLAN), 0)
    found = jnp.where(line == 0, found + SLOT_CAP, jnp.where(line == 3, total, found))
    plan_ref[...] = found.astype(jnp.int32)


def stage_kernel(meta_ref, own_hbm, other_hbm, first_ref, second_ref, sems):
    core = meta_ref[0]
    refs = (first_ref, second_ref)
    for out in refs:
        out[SLOT_CAP] = jnp.zeros((TILE, TILE), BF16)
    for c in range(2):

        @pl.when(core == c)
        def _():
            for hbm, out, k in ((own_hbm, refs[c], 0), (other_hbm, refs[1 - c], 1)):
                pltpu.make_async_copy(hbm, out.at[pl.ds(0, SLOT_CAP)], sems.at[k]).start()

    for hbm, k in ((own_hbm, 0), (other_hbm, 1)):
        pltpu.make_async_copy(hbm, refs[k].at[pl.ds(0, SLOT_CAP)], sems.at[k]).wait()


def add_tiles(plan_ref, tiles, source, total):
    total[...] = jnp.zeros_like(total)

    def product(g):
        left, right = [], []
        for e in range(GROUP):
            u = plan_ref[1, g * GROUP + e]
            left.append(tiles[plan_ref[0, g * GROUP + e]])
            right.append(source[pl.ds((u & 3) * 2, 2), :, u >> 2].reshape(TILE, HALF))
        return jnp.dot(
            jnp.concatenate(left, axis=1),
            jnp.concatenate(right, axis=0),
            preferred_element_type=F32,
        )

    def some_groups(h, carry):
        found = [
            (plan_ref[2, (h * UNROLL + k) * GROUP], product(h * UNROLL + k))
            for k in range(UNROLL)
        ]
        for place, value in found:
            total[place] += value
        return carry

    lax.fori_loop(0, (plan_ref[3, 0] + UNROLL - 1) >> UNROLL_BITS, some_groups, 0)


def narrow_block(total, yh, x):
    rows = total[pl.ds((yh * 4 + x) * 4, 4)].astype(BF16)
    return rows.reshape(SLOTS, HALF)


def tiles_y_kernel(meta_ref, plan_ref, tiles, *refs):
    blocks, (keep_ref, send_ref, source) = refs[:BLOCKS], refs[BLOCKS : BLOCKS + 3]
    total, sems = refs[BLOCKS + 3 :]
    yh = meta_ref[2]
    core = meta_ref[0]

    def fetch(block, k):
        return pltpu.make_async_copy(block, source.at[meta_ref[4 + k]], sems.at[k])

    for k in range(SHARED):
        fetch(blocks[k], k).start()
    for c in range(2):

        @pl.when(core == c)
        def _():
            for k in range(SHARED, CHIPS):
                fetch(blocks[k + c * (CHIPS - SHARED)], k).start()

    for k in range(CHIPS):
        fetch(blocks[k], k).wait()
    add_tiles(plan_ref, tiles, source, total)
    for out, to in ((send_ref, 1 - yh), (keep_ref, yh)):
        for x in range(4):
            out[x] = narrow_block(total, to, x)


def tiles_x_kernel(meta_ref, plan_ref, tiles, source, *refs):
    outs, total = refs[:4], refs[4]
    x = meta_ref[1]
    add_tiles(plan_ref, tiles, source, total)
    for k, out in enumerate(outs):
        for yh in range(2):
            out[yh] = narrow_block(total, yh, (x + k) & 3)


def x_summed_kernel(meta_ref, own_ref, a_ref, b_ref, c_ref, keep_ref, send_ref):
    yh = meta_ref[2]

    def summed(k):
        pair = own_ref[k].astype(F32) + a_ref[k].astype(F32)
        return pair + (b_ref[k].astype(F32) + c_ref[k].astype(F32))

    keep_ref[...] = summed(yh)
    send_ref[...] = summed(1 - yh).astype(BF16)


def y_summed_kernel(meta_ref, own_ref, got_ref, keep_ref, a_ref, b_ref, c_ref):
    x = meta_ref[1]

    def summed(k):
        return own_ref[k].astype(F32) + got_ref[k].astype(F32)

    keep_ref[...] = summed(x)
    for k, out in ((1, a_ref), (2, b_ref), (3, c_ref)):
        out[...] = summed((x + k) & 3).astype(BF16)


def sums_kernel(meta_ref, keep0, got0, keep1, a_ref, b_ref, c_ref, mine_ref, send_ref):
    core = meta_ref[0]
    first = keep0[...] + got0[...].astype(F32)
    second = keep1[...] + a_ref[...].astype(F32)
    second = second + (b_ref[...].astype(F32) + c_ref[...].astype(F32))
    mine_ref[...] = jnp.where(core == 0, first, second)
    send_ref[...] = jnp.where(core == 0, second, first)


def two_parts(value):
    high = value.astype(BF16)
    return high, (value - high.astype(F32)).astype(BF16)


def layer_kernel(meta_ref, mine_ref, got_ref, weight_ref, cotangent_ref, act_ref, slope_ref):
    core = meta_ref[0]
    pre = jnp.zeros((SLOTS, F), F32)
    for half, mixed in ((core, mine_ref[...]), (1 - core, got_ref[...])):
        weight = weight_ref[pl.ds(pl.multiple_of(half * HALF, HALF), HALF), :]
        for piece in two_parts(mixed):
            pre = pre + jnp.dot(piece, weight, preferred_element_type=F32)
    sigmoid = jax.nn.sigmoid(pre)
    act_ref[...] = (pre * sigmoid).astype(BF16)
    slope_ref[...] = (
        cotangent_ref[...].astype(F32) * (sigmoid * (1.0 + pre * (1.0 - sigmoid)))
    ).astype(BF16)


def gradient_kernel(mine_ref, other_ref, slope_ref, other_slope_ref, grad_ref):
    contract = (((0,), (0,)), ((), ()))
    grad = jnp.zeros((HALF, F), F32)
    for mixed, slope in ((mine_ref, slope_ref), (other_ref, other_slope_ref)):
        for piece in two_parts(mixed[...]):
            grad = grad + lax.dot_general(
                piece, slope[...], contract, preferred_element_type=F32
            )
    grad_ref[...] = (grad * (1.0 / 256.0)).astype(BF16)


def row_moves(move):
    pairs = []
    for yl in range(2):
        for z in range(4):
            for c in range(2):
                to = move(yl, z, c)
                if to is not None:
                    a, b, d = to
                    pairs.append(((yl * 4 + z) * 2 + c, (a * 4 + b) * 2 + d))
    return pairs


def x_moves(k):
    return [(yh * 4 + x, yh * 4 + (x + k) % 4) for yh in range(2) for x in range(4)]


def y_moves():
    return [(yh * 4 + x, (1 - yh) * 4 + x) for yh in range(2) for x in range(4)]


def exchange(parts, axis, groups=None):
    return lax.all_to_all(
        parts, axis, split_axis=0, concat_axis=0, axis_index_groups=groups, tiled=True
    )


def added(parts):
    parts = parts.astype(F32)
    a = (parts[0] + parts[1]) + (parts[2] + parts[3])
    return a + ((parts[4] + parts[5]) + (parts[6] + parts[7]))


def call(kernel, in_specs, outs, scratch=(), limit=16):
    made = pl.pallas_call(
        kernel,
        in_specs=in_specs,
        out_specs=jax.tree.map(lambda _: pl.BlockSpec(memory_space=pltpu.VMEM), outs),
        out_shape=outs,
        scratch_shapes=list(scratch),
        compiler_params=params(limit),
    )

    def run(*operands):
        held = [
            pltpu.with_memory_space_constraint(o, spec.memory_space)
            if spec.memory_space in (pltpu.VMEM, pltpu.MemorySpace.HBM)
            else o
            for spec, o in zip(in_specs, operands)
        ]
        return made(*held)

    return run


def array(*shape, dtype=BF16):
    return jax.ShapeDtypeStruct(shape, dtype)


def held(*shape, dtype=BF16):
    return pltpu.VMEM(shape, dtype)


def after(value, *others):
    return lax.optimization_barrier((value, *others))[0]


def shards(
    features, partition_of, weight, tile_values, tile_rows, tile_cols, tile_count, out_cotangent
):
    row = lax.axis_index("row")
    col = lax.axis_index("col")
    core, z, yl = row % 2, (row // 2) % 4, row // 8
    x, yh = col % 4, col // 4
    vmem = pl.BlockSpec(memory_space=pltpu.VMEM)
    smem = pl.BlockSpec(memory_space=pltpu.SMEM)
    hbm = pl.BlockSpec(memory_space=pl.ANY)
    pinned = pl.BlockSpec(memory_space=pltpu.MemorySpace.HBM)

    here, there = yl * 4, (1 - yl) * 4
    near = [here + (z - k) % 4 for k in range(4)]
    far = [there + (z - k) % 4 for k in range(4)]
    first = core == 0
    places = [
        near[0],
        jnp.where(first, near[1], far[0]),
        jnp.where(first, far[0], near[1]),
        far[1],
        jnp.where(first, near[3], far[3]),
        jnp.where(first, near[2], near[3]),
        jnp.where(first, far[3], near[2]),
        far[2],
    ]
    meta = jnp.stack([core, x, yh, z] + places).astype(jnp.int32)

    swap = row_moves(lambda yl, z, c: (yl, z, 1 - c))
    tiles = tile_values.reshape(-1, TILE, TILE)
    part = partition_of.reshape(1, SLOTS)
    other_part = lax.ppermute(part, "row", swap)
    other_features = lax.ppermute(features, "row", swap)
    plan = call(plan_kernel, [smem, vmem, vmem], array(8, PLAN, dtype=jnp.int32))(
        tile_count.reshape(1), tile_rows.reshape(1, -1), tile_cols.reshape(1, -1)
    )
    other_plan = lax.ppermute(plan, "row", swap)
    plans = [jnp.where(core == c, plan, other_plan) for c in range(2)]
    grouped = call(
        group_kernel,
        [smem, vmem, pinned, vmem, vmem],
        held(N_COL, 2, SLOTS // N_COL, HALF),
        [pltpu.VMEM((SLOTS, F), BF16), pltpu.SemaphoreType.DMA],
    )(meta, part, features, other_part, other_features)
    other_tiles = lax.ppermute(after(tiles, grouped), "row", swap)
    arrived = lax.all_to_all(grouped, "col", split_axis=0, concat_axis=0, tiled=True)
    own = call(interleave_kernel, [vmem], array(2, SLOTS, HALF))(arrived)
    own = after(own, other_tiles, other_plan)

    tiles0, tiles1 = call(
        stage_kernel,
        [smem, pinned, pinned],
        [held(SLOT_CAP + 1, TILE, TILE)] * 2,
        [pltpu.SemaphoreType.DMA((2,))],
    )(meta, tiles, after(other_tiles, own))

    def hop(block, *moves):
        def move(yl, z, c):
            if moves[c] is None:
                return None
            return (yl + moves[c][0]) % 2, (z + moves[c][1]) % 4, c

        return lax.ppermute(block, "row", row_moves(move))

    r1 = hop(own, (0, 1), (1, 0))
    r2 = hop(own, (0, 3), None)
    r3 = hop(own, (0, 2), None)
    r4 = hop(own, (1, 0), (0, 1))
    s1 = hop(r1, (1, 0), (0, 1))
    s2 = hop(r2, (1, 0), None)
    s3 = hop(r3, (1, 0), None)
    later = after(own, r1)
    t1 = hop(r1, None, (0, 3))
    t2 = hop(later, None, (0, 3))
    t3 = hop(later, None, (0, 2))
    t4 = hop(r1, None, (0, 2))
    blocks = [
        b.reshape(2, N_ROW, N_COL * PER_PEER, HALF)
        for b in (own, r1, r4, s1, r2, r3, s2, s3, t1, t2, t3, t4)
    ]

    total = pltpu.VMEM((ROW_TILES, TILE, HALF), F32)
    source = held(CHIPS, 2, N_ROW, N_COL * PER_PEER, HALF)
    keep1, send1, source = call(
        tiles_y_kernel,
        [smem, smem, vmem] + [hbm] * BLOCKS,
        [held(4, SLOTS, HALF), held(4, SLOTS, HALF), source],
        [total, pltpu.SemaphoreType.DMA((CHIPS,))],
    )(meta, plans[1], tiles1, *blocks)
    row0 = call(
        tiles_x_kernel,
        [smem, smem, vmem, vmem],
        [held(2, SLOTS, HALF)] * 4,
        [total],
    )(meta, plans[0], tiles0, source)
    got0 = [lax.ppermute(row0[k], "col", x_moves(k)) for k in (1, 3, 2)]
    got1 = lax.ppermute(send1, "col", y_moves())
    wide, narrow = held(SLOTS, HALF, dtype=F32), held(SLOTS, HALF)
    keep1, *send1 = call(y_summed_kernel, [smem] + [vmem] * 2, [wide] + [narrow] * 3)(
        meta, keep1, got1
    )
    got1 = [lax.ppermute(send1[k - 1], "col", x_moves(k)) for k in (1, 3, 2)]
    keep0, send0 = call(x_summed_kernel, [smem] + [vmem] * 4, [wide, narrow])(
        meta, after(row0[0], got1[0]), *got0
    )
    got0 = lax.ppermute(send0, "col", y_moves())
    mine, others = call(sums_kernel, [smem] + [vmem] * 6, [wide] * 2)(
        meta, keep0, got0, keep1, *got1
    )
    theirs = lax.ppermute(others, "row", swap)
    cotangent = lax.dynamic_slice_in_dim(out_cotangent, col * SLOTS, SLOTS, 0)
    activations, slope = call(
        layer_kernel, [smem] + [vmem] * 4, [array(SLOTS, F), held(SLOTS, F)]
    )(
        meta, mine, theirs, weight, cotangent
    )
    other_slope = lax.ppermute(slope, "row", swap)
    half = call(gradient_kernel, [vmem] * 4, held(HALF, F))(
        mine, others, slope, other_slope
    )

    same_core = [[chip * 2 + c for chip in range(CHIPS)] for c in range(2)]
    shape = (CHIPS, HALF // CHIPS, F)
    piece = added(exchange(half.reshape(shape), "row", same_core))
    piece = added(exchange(jnp.broadcast_to(piece, shape), "col"))
    half = exchange(jnp.broadcast_to(piece.astype(BF16), shape), "row", same_core)
    half = half.reshape(HALF, F)
    other = lax.ppermute(half, "row", swap)
    first = jnp.where(core == 0, half, other).astype(F32)
    second = jnp.where(core == 0, other, half).astype(F32)
    return activations, jnp.concatenate([first, second])


def solution(mesh):
    placed = (
        P(("row", "col"), None),
        P(("row", "col")),
        P(),
        P("row", "col", None, None, None),
        P("row", "col", None),
        P("row", "col", None),
        P("row", "col"),
        P("row", None),
    )
    return jax.shard_map(
        shards,
        mesh=mesh,
        in_specs=placed,
        out_specs=(P(("row", "col"), None), P()),
        check_vma=False,
    )
```

```python
import jax
import jax.numpy as jnp
from jax import lax
from jax.experimental import pallas as pl
from jax.experimental.pallas import tpu as pltpu
from jax.sharding import PartitionSpec as P

N_ROW = 16
N_COL = 8
TILE = 128
SLOTS = 512
F = 512
PER_PEER = 4
HALF = 256
CHIPS = 8
SHARED = 4
BLOCKS = 2 * CHIPS - SHARED
SLOT_CAP = 192
ROW_TILES = 32
GROUP_BITS = 2
GROUP = 1 << GROUP_BITS
PLAN = SLOT_CAP + ROW_TILES * (GROUP - 1)
UNROLL_BITS = 3
UNROLL = 1 << UNROLL_BITS
BF16 = jnp.bfloat16
F32 = jnp.float32


def params(limit=16):
    return pltpu.CompilerParams(vmem_limit_bytes=limit * 1024 * 1024)


def selection(position, rows, columns):
    wanted = lax.broadcasted_iota(jnp.int32, (rows, columns), 0)
    return jnp.where(position == wanted, 1.0, 0.0).astype(BF16)


def group_kernel(part_ref, features_hbm, out_ref, features_ref, sem):
    copy = pltpu.make_async_copy(features_hbm, features_ref, sem)
    copy.start()
    part = part_ref[...]
    devices = N_ROW * N_COL
    before = jnp.where(
        lax.broadcasted_iota(jnp.int32, (SLOTS, SLOTS), 0)
        < lax.broadcasted_iota(jnp.int32, (SLOTS, SLOTS), 1),
        1.0,
        0.0,
    ).astype(BF16)
    member = jnp.where(
        part == lax.broadcasted_iota(jnp.int32, (devices, SLOTS), 0), 1.0, 0.0
    )
    earlier = jnp.dot(member.astype(BF16), before, preferred_element_type=F32)
    rank = jnp.sum(member * earlier, axis=0, keepdims=True).astype(jnp.int32)
    place = ((part & (N_COL - 1)) * N_ROW + (part >> 3)) * PER_PEER + rank
    pick = selection(place, SLOTS, SLOTS)
    copy.wait()
    for c in range(2):
        wanted = features_ref[:, c * HALF : (c + 1) * HALF]
        picked = jnp.dot(pick, wanted, preferred_element_type=F32).astype(BF16)
        out_ref[c * N_COL : (c + 1) * N_COL] = picked.reshape(N_COL, SLOTS // N_COL, HALF)


def interleave_kernel(arrived_ref, out_ref):
    source = lax.broadcasted_iota(jnp.int32, (1, SLOTS), 1)
    giver, inner = source >> 6, source & 63
    place = (inner >> 2) * (N_COL * PER_PEER) + giver * PER_PEER + (inner & 3)
    pick = selection(place, SLOTS, SLOTS)
    for c in range(2):
        rows = arrived_ref[c * N_COL : (c + 1) * N_COL].reshape(SLOTS, HALF)
        out_ref[c] = jnp.dot(pick, rows, preferred_element_type=F32).astype(BF16)


def plan_kernel(count_ref, rows_ref, cols_ref, plan_ref):
    slot = lax.broadcasted_iota(jnp.int32, (1, SLOT_CAP), 1)
    rows = rows_ref[...]
    live = slot < count_ref[0]
    kinds = lax.broadcasted_iota(jnp.int32, (ROW_TILES, SLOT_CAP), 0)
    member = jnp.where(live & (rows == kinds), 1.0, 0.0)
    before = jnp.where(
        lax.broadcasted_iota(jnp.int32, (SLOT_CAP, SLOT_CAP), 0)
        < lax.broadcasted_iota(jnp.int32, (SLOT_CAP, SLOT_CAP), 1),
        1.0,
        0.0,
    ).astype(BF16)
    earlier = jnp.dot(member.astype(BF16), before, preferred_element_type=F32)
    number = jnp.sum(member, axis=1, keepdims=True).astype(jnp.int32)
    groups = jnp.broadcast_to((number + (GROUP - 1)) >> GROUP_BITS, (ROW_TILES, TILE))
    below = jnp.where(
        lax.broadcasted_iota(jnp.int32, (ROW_TILES, ROW_TILES), 1)
        < lax.broadcasted_iota(jnp.int32, (ROW_TILES, ROW_TILES), 0),
        1.0,
        0.0,
    ).astype(BF16)
    groups = groups.astype(F32)
    start = jnp.dot(below, groups.astype(BF16), preferred_element_type=F32)[:, :1]
    total = jnp.sum(groups, axis=0, keepdims=True)[:, :1]
    place = jnp.sum(member * (GROUP * start + earlier + 1.0), axis=0, keepdims=True) - 1.0
    taken = selection(place.astype(jnp.int32), PLAN, SLOT_CAP)
    line = lax.broadcasted_iota(jnp.int32, (8, SLOT_CAP), 0)
    values = jnp.where(line == 0, slot - SLOT_CAP, jnp.where(line == 1, cols_ref[...], rows))
    found = lax.dot_general(
        values.astype(F32).astype(BF16),
        taken,
        (((1,), (1,)), ((), ())),
        preferred_element_type=F32,
    )
    line = lax.broadcasted_iota(jnp.int32, (8, PLAN), 0)
    found = jnp.where(line == 0, found + SLOT_CAP, jnp.where(line == 3, total, found))
    plan_ref[...] = found.astype(jnp.int32)


def start_tiles(part, core, own_hbm, other_hbm, out, sem):
    out[SLOT_CAP] = jnp.zeros((TILE, TILE), BF16)
    for mine, hbm in ((True, own_hbm), (False, other_hbm)):

        @pl.when((core == part) == mine)
        def _():
            pltpu.make_async_copy(hbm, out.at[pl.ds(0, SLOT_CAP)], sem).start()

    return pltpu.make_async_copy(own_hbm, out.at[pl.ds(0, SLOT_CAP)], sem)


def stage_kernel(meta_ref, own_hbm, other_hbm, out_ref, sem):
    start_tiles(1, meta_ref[0], own_hbm, other_hbm, out_ref, sem).wait()


def add_tiles(plan_ref, tiles, source, total):
    total[...] = jnp.zeros_like(total)

    def product(g):
        left, right = [], []
        for e in range(GROUP):
            u = plan_ref[1, g * GROUP + e]
            left.append(tiles[plan_ref[0, g * GROUP + e]])
            right.append(source[pl.ds((u & 3) * 2, 2), :, u >> 2].reshape(TILE, HALF))
        return jnp.dot(
            jnp.concatenate(left, axis=1),
            jnp.concatenate(right, axis=0),
            preferred_element_type=F32,
        )

    def some_groups(h, carry):
        found = [
            (plan_ref[2, (h * UNROLL + k) * GROUP], product(h * UNROLL + k))
            for k in range(UNROLL)
        ]
        for place, value in found:
            total[place] += value
        return carry

    lax.fori_loop(0, (plan_ref[3, 0] + UNROLL - 1) >> UNROLL_BITS, some_groups, 0)


def narrow_block(total, yh, x):
    rows = total[pl.ds((yh * 4 + x) * 4, 4)].astype(BF16)
    return rows.reshape(SLOTS, HALF)


def tiles_y_kernel(meta_ref, plan_ref, tiles, own_hbm, other_hbm, *refs):
    blocks, (keep_ref, send_ref, source, next_tiles) = refs[:BLOCKS], refs[BLOCKS:-3]
    total, sems, tiles_sem = refs[-3:]
    core, yh = meta_ref[0], meta_ref[2]

    def fetch(block, k):
        return pltpu.make_async_copy(block, source.at[meta_ref[4 + k]], sems.at[k])

    for k in range(SHARED):
        fetch(blocks[k], k).start()
    for c in range(2):

        @pl.when(core == c)
        def _():
            for k in range(SHARED, CHIPS):
                fetch(blocks[k + c * (CHIPS - SHARED)], k).start()

    for k in range(CHIPS):
        fetch(blocks[k], k).wait()
    coming = start_tiles(0, core, own_hbm, other_hbm, next_tiles, tiles_sem)
    add_tiles(plan_ref, tiles, source, total)
    for out, to in ((send_ref, 1 - yh), (keep_ref, yh)):
        for x in range(4):
            out[x] = narrow_block(total, to, x)
    coming.wait()


def tiles_x_kernel(meta_ref, plan_ref, tiles, source, *refs):
    outs, total = refs[:4], refs[4]
    x = meta_ref[1]
    add_tiles(plan_ref, tiles, source, total)
    for k, out in enumerate(outs):
        for yh in range(2):
            out[yh] = narrow_block(total, yh, (x + k) & 3)


def x_summed_kernel(meta_ref, own_ref, a_ref, b_ref, c_ref, keep_ref, send_ref):
    yh = meta_ref[2]

    def summed(k):
        pair = own_ref[k].astype(F32) + a_ref[k].astype(F32)
        return pair + (b_ref[k].astype(F32) + c_ref[k].astype(F32))

    keep_ref[...] = summed(yh)
    send_ref[...] = summed(1 - yh).astype(BF16)


def y_summed_kernel(meta_ref, own_ref, got_ref, keep_ref, a_ref, b_ref, c_ref):
    x = meta_ref[1]

    def summed(k):
        return own_ref[k].astype(F32) + got_ref[k].astype(F32)

    keep_ref[...] = summed(x)
    for k, out in ((1, a_ref), (2, b_ref), (3, c_ref)):
        out[...] = summed((x + k) & 3).astype(BF16)


def sums_kernel(meta_ref, keep0, got0, keep1, a_ref, b_ref, c_ref, mine_ref, send_ref):
    core = meta_ref[0]
    first = keep0[...] + got0[...].astype(F32)
    second = keep1[...] + a_ref[...].astype(F32)
    second = second + (b_ref[...].astype(F32) + c_ref[...].astype(F32))
    mine_ref[...] = jnp.where(core == 0, first, second)
    send_ref[...] = jnp.where(core == 0, second, first)


def two_parts(value):
    high = value.astype(BF16)
    return high, (value - high.astype(F32)).astype(BF16)


def layer_kernel(meta_ref, mine_ref, got_ref, weight_ref, cotangent_ref, act_ref, slope_ref):
    core = meta_ref[0]
    pre = jnp.zeros((SLOTS, F), F32)
    for half, mixed in ((core, mine_ref[...]), (1 - core, got_ref[...])):
        weight = weight_ref[pl.ds(pl.multiple_of(half * HALF, HALF), HALF), :]
        for piece in two_parts(mixed):
            pre = pre + jnp.dot(piece, weight, preferred_element_type=F32)
    sigmoid = jax.nn.sigmoid(pre)
    act_ref[...] = (pre * sigmoid).astype(BF16)
    slope_ref[...] = (
        cotangent_ref[...].astype(F32) * (sigmoid * (1.0 + pre * (1.0 - sigmoid)))
    ).astype(BF16)


def gradient_kernel(mine_ref, other_ref, slope_ref, other_slope_ref, grad_ref):
    contract = (((0,), (0,)), ((), ()))
    grad = jnp.zeros((HALF, F), F32)
    for mixed, slope in ((mine_ref, slope_ref), (other_ref, other_slope_ref)):
        for piece in two_parts(mixed[...]):
            grad = grad + lax.dot_general(
                piece, slope[...], contract, preferred_element_type=F32
            )
    grad_ref[...] = (grad * (1.0 / 256.0)).astype(BF16)


def row_moves(move):
    pairs = []
    for yl in range(2):
        for z in range(4):
            for c in range(2):
                to = move(yl, z, c)
                if to is not None:
                    a, b, d = to
                    pairs.append(((yl * 4 + z) * 2 + c, (a * 4 + b) * 2 + d))
    return pairs


def x_moves(k):
    return [(yh * 4 + x, yh * 4 + (x + k) % 4) for yh in range(2) for x in range(4)]


def y_moves():
    return [(yh * 4 + x, (1 - yh) * 4 + x) for yh in range(2) for x in range(4)]


def exchange(parts, axis, groups=None):
    return lax.all_to_all(
        parts, axis, split_axis=0, concat_axis=0, axis_index_groups=groups, tiled=True
    )


def added(parts):
    parts = parts.astype(F32)
    a = (parts[0] + parts[1]) + (parts[2] + parts[3])
    return a + ((parts[4] + parts[5]) + (parts[6] + parts[7]))


def call(kernel, in_specs, outs, scratch=(), limit=16):
    made = pl.pallas_call(
        kernel,
        in_specs=in_specs,
        out_specs=jax.tree.map(lambda _: pl.BlockSpec(memory_space=pltpu.VMEM), outs),
        out_shape=outs,
        scratch_shapes=list(scratch),
        compiler_params=params(limit),
    )

    def run(*operands):
        held = [
            pltpu.with_memory_space_constraint(o, spec.memory_space)
            if spec.memory_space in (pltpu.VMEM, pltpu.MemorySpace.HBM)
            else o
            for spec, o in zip(in_specs, operands)
        ]
        return made(*held)

    return run


def array(*shape, dtype=BF16):
    return jax.ShapeDtypeStruct(shape, dtype)


def held(*shape, dtype=BF16):
    return pltpu.VMEM(shape, dtype)


def after(value, *others):
    return lax.optimization_barrier((value, *others))[0]


def shards(
    features, partition_of, weight, tile_values, tile_rows, tile_cols, tile_count, out_cotangent
):
    row = lax.axis_index("row")
    col = lax.axis_index("col")
    core, z, yl = row % 2, (row // 2) % 4, row // 8
    x, yh = col % 4, col // 4
    vmem = pl.BlockSpec(memory_space=pltpu.VMEM)
    smem = pl.BlockSpec(memory_space=pltpu.SMEM)
    hbm = pl.BlockSpec(memory_space=pl.ANY)
    pinned = pl.BlockSpec(memory_space=pltpu.MemorySpace.HBM)

    here, there = yl * 4, (1 - yl) * 4
    near = [here + (z - k) % 4 for k in range(4)]
    far = [there + (z - k) % 4 for k in range(4)]
    first = core == 0
    places = [
        near[0],
        jnp.where(first, near[1], far[0]),
        jnp.where(first, far[0], near[1]),
        far[1],
        jnp.where(first, near[3], far[3]),
        jnp.where(first, near[2], near[3]),
        jnp.where(first, far[3], near[2]),
        far[2],
    ]
    meta = jnp.stack([core, x, yh, z] + places).astype(jnp.int32)

    swap = row_moves(lambda yl, z, c: (yl, z, 1 - c))
    tiles = tile_values.reshape(-1, TILE, TILE)
    part = partition_of.reshape(1, SLOTS)
    plan = call(plan_kernel, [smem, vmem, vmem], array(8, PLAN, dtype=jnp.int32))(
        tile_count.reshape(1), tile_rows.reshape(1, -1), tile_cols.reshape(1, -1)
    )
    other_plan = lax.ppermute(plan, "row", swap)
    plans = [jnp.where(core == c, plan, other_plan) for c in range(2)]
    grouped = call(
        group_kernel,
        [vmem, pinned],
        held(2 * N_COL, SLOTS // N_COL, HALF),
        [pltpu.VMEM((SLOTS, F), BF16), pltpu.SemaphoreType.DMA],
    )(part, features)
    other_tiles = lax.ppermute(after(tiles, grouped), "row", swap)
    near_chips = [[k * 2 * N_COL + m for m in range(2 * N_COL)] for k in range(CHIPS)]
    arrived = exchange(grouped, ("row", "col"), near_chips)
    own = call(interleave_kernel, [vmem], array(2, SLOTS, HALF))(arrived)
    own = after(own, other_tiles, other_plan)

    staged = held(SLOT_CAP + 1, TILE, TILE)
    tiles1 = call(stage_kernel, [smem, pinned, pinned], staged, [pltpu.SemaphoreType.DMA])(
        meta, tiles, after(other_tiles, own)
    )

    def hop(block, *moves):
        def move(yl, z, c):
            if moves[c] is None:
                return None
            return (yl + moves[c][0]) % 2, (z + moves[c][1]) % 4, c

        return lax.ppermute(block, "row", row_moves(move))

    r1 = hop(own, (0, 1), (1, 0))
    r2 = hop(own, (0, 3), None)
    r3 = hop(own, (0, 2), None)
    r4 = hop(own, (1, 0), (0, 1))
    s1 = hop(r1, (1, 0), (0, 1))
    s2 = hop(r2, (1, 0), None)
    s3 = hop(r3, (1, 0), None)
    later = after(own, r1)
    t1 = hop(r1, None, (0, 3))
    t2 = hop(later, None, (0, 3))
    t3 = hop(later, None, (0, 2))
    t4 = hop(r1, None, (0, 2))
    blocks = [
        b.reshape(2, N_ROW, N_COL * PER_PEER, HALF)
        for b in (own, r1, r4, s1, r2, r3, s2, s3, t1, t2, t3, t4)
    ]

    total = pltpu.VMEM((ROW_TILES, TILE, HALF), F32)
    source = held(CHIPS, 2, N_ROW, N_COL * PER_PEER, HALF)
    keep1, send1, source, tiles0 = call(
        tiles_y_kernel,
        [smem, smem, vmem, pinned, pinned] + [hbm] * BLOCKS,
        [held(4, SLOTS, HALF), held(4, SLOTS, HALF), source, staged],
        [total, pltpu.SemaphoreType.DMA((CHIPS,)), pltpu.SemaphoreType.DMA],
    )(meta, plans[1], tiles1, tiles, other_tiles, *blocks)
    row0 = call(
        tiles_x_kernel,
        [smem, smem, vmem, vmem],
        [held(2, SLOTS, HALF)] * 4,
        [total],
    )(meta, plans[0], tiles0, source)
    got0 = [lax.ppermute(row0[k], "col", x_moves(k)) for k in (1, 3, 2)]
    got1 = lax.ppermute(send1, "col", y_moves())
    wide, narrow = held(SLOTS, HALF, dtype=F32), held(SLOTS, HALF)
    keep1, *send1 = call(y_summed_kernel, [smem] + [vmem] * 2, [wide] + [narrow] * 3)(
        meta, keep1, got1
    )
    got1 = [lax.ppermute(send1[k - 1], "col", x_moves(k)) for k in (1, 3, 2)]
    keep0, send0 = call(x_summed_kernel, [smem] + [vmem] * 4, [wide, narrow])(
        meta, after(row0[0], got1[0]), *got0
    )
    got0 = lax.ppermute(send0, "col", y_moves())
    mine, others = call(sums_kernel, [smem] + [vmem] * 6, [wide] * 2)(
        meta, keep0, got0, keep1, *got1
    )
    theirs = lax.ppermute(others, "row", swap)
    cotangent = lax.dynamic_slice_in_dim(out_cotangent, col * SLOTS, SLOTS, 0)
    activations, slope = call(
        layer_kernel, [smem] + [vmem] * 4, [array(SLOTS, F), held(SLOTS, F)]
    )(
        meta, mine, theirs, weight, cotangent
    )
    other_slope = lax.ppermute(slope, "row", swap)
    half = call(gradient_kernel, [vmem] * 4, held(HALF, F))(
        mine, others, slope, other_slope
    )

    same_core = [[chip * 2 + c for chip in range(CHIPS)] for c in range(2)]
    shape = (CHIPS, HALF // CHIPS, F)
    piece = added(exchange(half.reshape(shape), "row", same_core))
    piece = added(exchange(jnp.broadcast_to(piece, shape), "col"))
    half = exchange(jnp.broadcast_to(piece.astype(BF16), shape), "row", same_core)
    half = half.reshape(HALF, F)
    other = lax.ppermute(half, "row", swap)
    first = jnp.where(core == 0, half, other).astype(F32)
    second = jnp.where(core == 0, other, half).astype(F32)
    return activations, jnp.concatenate([first, second])


def solution(mesh):
    placed = (
        P(("row", "col"), None),
        P(("row", "col")),
        P(),
        P("row", "col", None, None, None),
        P("row", "col", None),
        P("row", "col", None),
        P("row", "col"),
        P("row", None),
    )
    return jax.shard_map(
        shards,
        mesh=mesh,
        in_specs=placed,
        out_specs=(P(("row", "col"), None), P()),
        check_vma=False,
    )
```

```python
import jax
import jax.numpy as jnp
from jax import lax
from jax.experimental import pallas as pl
from jax.experimental.pallas import tpu as pltpu
from jax.sharding import PartitionSpec as P

N_ROW = 16
N_COL = 8
TILE = 128
SLOTS = 512
F = 512
PER_PEER = 4
HALF = 256
CHIPS = 8
BLOCKS = 7
SLOT_CAP = 192
ROW_TILES = 32
GROUP_BITS = 2
GROUP = 1 << GROUP_BITS
PLAN = SLOT_CAP + ROW_TILES * (GROUP - 1)
UNROLL_BITS = 3
UNROLL = 1 << UNROLL_BITS
BF16 = jnp.bfloat16
F32 = jnp.float32


def params(limit=16):
    return pltpu.CompilerParams(vmem_limit_bytes=limit * 1024 * 1024)


def selection(position, rows, columns):
    wanted = lax.broadcasted_iota(jnp.int32, (rows, columns), 0)
    return jnp.where(position == wanted, 1.0, 0.0).astype(BF16)


def group_kernel(part_ref, features_hbm, out_ref, features_ref, sem):
    copy = pltpu.make_async_copy(features_hbm, features_ref, sem)
    copy.start()
    part = part_ref[...]
    devices = N_ROW * N_COL
    before = jnp.where(
        lax.broadcasted_iota(jnp.int32, (SLOTS, SLOTS), 0)
        < lax.broadcasted_iota(jnp.int32, (SLOTS, SLOTS), 1),
        1.0,
        0.0,
    ).astype(BF16)
    member = jnp.where(
        part == lax.broadcasted_iota(jnp.int32, (devices, SLOTS), 0), 1.0, 0.0
    )
    earlier = jnp.dot(member.astype(BF16), before, preferred_element_type=F32)
    rank = jnp.sum(member * earlier, axis=0, keepdims=True).astype(jnp.int32)
    place = ((part & (N_COL - 1)) * N_ROW + (part >> 3)) * PER_PEER + rank
    pick = selection(place, SLOTS, SLOTS)
    copy.wait()
    for c in range(2):
        wanted = features_ref[:, c * HALF : (c + 1) * HALF]
        picked = jnp.dot(pick, wanted, preferred_element_type=F32).astype(BF16)
        out_ref[c * N_COL : (c + 1) * N_COL] = picked.reshape(N_COL, SLOTS // N_COL, HALF)


def interleave_kernel(arrived_ref, out_ref):
    source = lax.broadcasted_iota(jnp.int32, (1, SLOTS), 1)
    giver, inner = source >> 6, source & 63
    place = (inner >> 2) * (N_COL * PER_PEER) + giver * PER_PEER + (inner & 3)
    pick = selection(place, SLOTS, SLOTS)
    for c in range(2):
        rows = arrived_ref[c * N_COL : (c + 1) * N_COL].reshape(SLOTS, HALF)
        out_ref[c] = jnp.dot(pick, rows, preferred_element_type=F32).astype(BF16)


def pair_kernel(a_ref, b_ref, out_ref):
    out_ref[0] = a_ref[...]
    out_ref[1] = b_ref[...]


def rest_kernel(meta_ref, pair_ref, a_ref, b_ref, out_ref):
    core = meta_ref[0]

    @pl.when(core == 0)
    def _():
        out_ref[0] = a_ref[...]
        out_ref[1] = b_ref[...]

    @pl.when(core != 0)
    def _():
        out_ref[...] = pair_ref[...]


def plan_kernel(count_ref, rows_ref, cols_ref, plan_ref):
    slot = lax.broadcasted_iota(jnp.int32, (1, SLOT_CAP), 1)
    rows = rows_ref[...]
    live = slot < count_ref[0]
    kinds = lax.broadcasted_iota(jnp.int32, (ROW_TILES, SLOT_CAP), 0)
    member = jnp.where(live & (rows == kinds), 1.0, 0.0)
    before = jnp.where(
        lax.broadcasted_iota(jnp.int32, (SLOT_CAP, SLOT_CAP), 0)
        < lax.broadcasted_iota(jnp.int32, (SLOT_CAP, SLOT_CAP), 1),
        1.0,
        0.0,
    ).astype(BF16)
    earlier = jnp.dot(member.astype(BF16), before, preferred_element_type=F32)
    number = jnp.sum(member, axis=1, keepdims=True).astype(jnp.int32)
    groups = jnp.broadcast_to((number + (GROUP - 1)) >> GROUP_BITS, (ROW_TILES, TILE))
    below = jnp.where(
        lax.broadcasted_iota(jnp.int32, (ROW_TILES, ROW_TILES), 1)
        < lax.broadcasted_iota(jnp.int32, (ROW_TILES, ROW_TILES), 0),
        1.0,
        0.0,
    ).astype(BF16)
    groups = groups.astype(F32)
    start = jnp.dot(below, groups.astype(BF16), preferred_element_type=F32)[:, :1]
    total = jnp.sum(groups, axis=0, keepdims=True)[:, :1]
    place = jnp.sum(member * (GROUP * start + earlier + 1.0), axis=0, keepdims=True) - 1.0
    taken = selection(place.astype(jnp.int32), PLAN, SLOT_CAP)
    line = lax.broadcasted_iota(jnp.int32, (8, SLOT_CAP), 0)
    values = jnp.where(line == 0, slot - SLOT_CAP, jnp.where(line == 1, cols_ref[...], rows))
    found = lax.dot_general(
        values.astype(F32).astype(BF16),
        taken,
        (((1,), (1,)), ((), ())),
        preferred_element_type=F32,
    )
    line = lax.broadcasted_iota(jnp.int32, (8, PLAN), 0)
    found = jnp.where(line == 0, found + SLOT_CAP, jnp.where(line == 3, total, found))
    plan_ref[...] = found.astype(jnp.int32)


def start_tiles(part, core, own_hbm, other_hbm, out, sem):
    out[SLOT_CAP] = jnp.zeros((TILE, TILE), BF16)
    for mine, hbm in ((True, own_hbm), (False, other_hbm)):

        @pl.when((core == part) == mine)
        def _():
            pltpu.make_async_copy(hbm, out.at[pl.ds(0, SLOT_CAP)], sem).start()

    return pltpu.make_async_copy(own_hbm, out.at[pl.ds(0, SLOT_CAP)], sem)


def stage_kernel(meta_ref, own_hbm, other_hbm, out_ref, sem):
    start_tiles(1, meta_ref[0], own_hbm, other_hbm, out_ref, sem).wait()


def add_tiles(plan_ref, tiles, source, total):
    total[...] = jnp.zeros_like(total)

    def product(g):
        left, right = [], []
        for e in range(GROUP):
            u = plan_ref[1, g * GROUP + e]
            left.append(tiles[plan_ref[0, g * GROUP + e]])
            right.append(source[pl.ds((u & 3) * 2, 2), :, u >> 2].reshape(TILE, HALF))
        return jnp.dot(
            jnp.concatenate(left, axis=1),
            jnp.concatenate(right, axis=0),
            preferred_element_type=F32,
        )

    def some_groups(h, carry):
        found = [
            (plan_ref[2, (h * UNROLL + k) * GROUP], product(h * UNROLL + k))
            for k in range(UNROLL)
        ]
        for place, value in found:
            total[place] += value
        return carry

    lax.fori_loop(0, (plan_ref[3, 0] + UNROLL - 1) >> UNROLL_BITS, some_groups, 0)


def narrow_block(total, yh, x):
    rows = total[pl.ds((yh * 4 + x) * 4, 4)].astype(BF16)
    return rows.reshape(SLOTS, HALF)


def tiles_y_kernel(meta_ref, plan_ref, tiles, own_hbm, other_hbm, *refs):
    blocks, (keep_ref, send_ref, source, next_tiles) = refs[:BLOCKS], refs[BLOCKS:-3]
    total, sems, tiles_sem = refs[-3:]
    core, yh = meta_ref[0], meta_ref[2]

    own, r1, r2, r3, s1, s3, s2 = blocks
    shared = [(own, 0), (r1, 0), (s1, 0), (s1, 1), (s3, 0), (s3, 1)]

    def fetch(block, k):
        return pltpu.make_async_copy(
            block[0].at[block[1]], source.at[meta_ref[4 + k]], sems.at[k]
        )

    for k, block in enumerate(shared):
        fetch(block, k).start()
    for c, rest in enumerate((((r2, 0), (r3, 0)), ((s2, 0), (s2, 1)))):

        @pl.when(core == c)
        def _():
            for k, block in enumerate(rest):
                fetch(block, len(shared) + k).start()

    for k in range(CHIPS):
        fetch(shared[0], k).wait()
    coming = start_tiles(0, core, own_hbm, other_hbm, next_tiles, tiles_sem)
    add_tiles(plan_ref, tiles, source, total)
    for out, to in ((send_ref, 1 - yh), (keep_ref, yh)):
        for x in range(4):
            out[x] = narrow_block(total, to, x)
    coming.wait()


def tiles_x_kernel(meta_ref, plan_ref, tiles, source, *refs):
    outs, total = refs[:4], refs[4]
    x = meta_ref[1]
    add_tiles(plan_ref, tiles, source, total)
    for k, out in enumerate(outs):
        for yh in range(2):
            out[yh] = narrow_block(total, yh, (x + k) & 3)


def x_summed_kernel(meta_ref, own_ref, a_ref, b_ref, c_ref, keep_ref, send_ref):
    yh = meta_ref[2]

    def summed(k):
        pair = own_ref[k].astype(F32) + a_ref[k].astype(F32)
        return pair + (b_ref[k].astype(F32) + c_ref[k].astype(F32))

    keep_ref[...] = summed(yh)
    send_ref[...] = summed(1 - yh).astype(BF16)


def y_summed_kernel(meta_ref, own_ref, got_ref, keep_ref, a_ref, b_ref, c_ref):
    x = meta_ref[1]

    def summed(k):
        return own_ref[k].astype(F32) + got_ref[k].astype(F32)

    keep_ref[...] = summed(x)
    for k, out in ((1, a_ref), (2, b_ref), (3, c_ref)):
        out[...] = summed((x + k) & 3).astype(BF16)


def sums_kernel(meta_ref, keep0, got0, keep1, a_ref, b_ref, c_ref, mine_ref, send_ref):
    core = meta_ref[0]
    first = keep0[...] + got0[...].astype(F32)
    second = keep1[...] + a_ref[...].astype(F32)
    second = second + (b_ref[...].astype(F32) + c_ref[...].astype(F32))
    mine_ref[...] = jnp.where(core == 0, first, second)
    send_ref[...] = jnp.where(core == 0, second, first)


def two_parts(value):
    high = value.astype(BF16)
    return high, (value - high.astype(F32)).astype(BF16)


def layer_kernel(meta_ref, mine_ref, got_ref, weight_ref, cotangent_ref, act_ref, slope_ref):
    core = meta_ref[0]
    pre = jnp.zeros((SLOTS, F), F32)
    for half, mixed in ((core, mine_ref[...]), (1 - core, got_ref[...])):
        weight = weight_ref[pl.ds(pl.multiple_of(half * HALF, HALF), HALF), :]
        for piece in two_parts(mixed):
            pre = pre + jnp.dot(piece, weight, preferred_element_type=F32)
    sigmoid = jax.nn.sigmoid(pre)
    act_ref[...] = (pre * sigmoid).astype(BF16)
    slope_ref[...] = (
        cotangent_ref[...].astype(F32) * (sigmoid * (1.0 + pre * (1.0 - sigmoid)))
    ).astype(BF16)


def gradient_kernel(mine_ref, other_ref, slope_ref, other_slope_ref, grad_ref):
    contract = (((0,), (0,)), ((), ()))
    grad = jnp.zeros((HALF, F), F32)
    for mixed, slope in ((mine_ref, slope_ref), (other_ref, other_slope_ref)):
        for piece in two_parts(mixed[...]):
            grad = grad + lax.dot_general(
                piece, slope[...], contract, preferred_element_type=F32
            )
    grad_ref[...] = (grad * (1.0 / 256.0)).astype(BF16)


def row_moves(move):
    pairs = []
    for yl in range(2):
        for z in range(4):
            for c in range(2):
                to = move(yl, z, c)
                if to is not None:
                    a, b, d = to
                    pairs.append(((yl * 4 + z) * 2 + c, (a * 4 + b) * 2 + d))
    return pairs


def x_moves(k):
    return [(yh * 4 + x, yh * 4 + (x + k) % 4) for yh in range(2) for x in range(4)]


def y_moves():
    return [(yh * 4 + x, (1 - yh) * 4 + x) for yh in range(2) for x in range(4)]


def exchange(parts, axis, groups=None):
    return lax.all_to_all(
        parts, axis, split_axis=0, concat_axis=0, axis_index_groups=groups, tiled=True
    )


def added(parts):
    parts = parts.astype(F32)
    a = (parts[0] + parts[1]) + (parts[2] + parts[3])
    return a + ((parts[4] + parts[5]) + (parts[6] + parts[7]))


def call(kernel, in_specs, outs, scratch=(), limit=16):
    made = pl.pallas_call(
        kernel,
        in_specs=in_specs,
        out_specs=jax.tree.map(lambda _: pl.BlockSpec(memory_space=pltpu.VMEM), outs),
        out_shape=outs,
        scratch_shapes=list(scratch),
        compiler_params=params(limit),
    )

    def run(*operands):
        held = [
            pltpu.with_memory_space_constraint(o, spec.memory_space)
            if spec.memory_space in (pltpu.VMEM, pltpu.MemorySpace.HBM)
            else o
            for spec, o in zip(in_specs, operands)
        ]
        return made(*held)

    return run


def array(*shape, dtype=BF16):
    return jax.ShapeDtypeStruct(shape, dtype)


def held(*shape, dtype=BF16):
    return pltpu.VMEM(shape, dtype)


def after(value, *others):
    return lax.optimization_barrier((value, *others))[0]


def shards(
    features, partition_of, weight, tile_values, tile_rows, tile_cols, tile_count, out_cotangent
):
    row = lax.axis_index("row")
    col = lax.axis_index("col")
    core, z, yl = row % 2, (row // 2) % 4, row // 8
    x, yh = col % 4, col // 4
    vmem = pl.BlockSpec(memory_space=pltpu.VMEM)
    smem = pl.BlockSpec(memory_space=pltpu.SMEM)
    hbm = pl.BlockSpec(memory_space=pl.ANY)
    pinned = pl.BlockSpec(memory_space=pltpu.MemorySpace.HBM)

    here, there = yl * 4, (1 - yl) * 4
    near = [here + (z - k) % 4 for k in range(4)]
    far = [there + (z - k) % 4 for k in range(4)]
    first = core == 0
    places = [
        near[0],
        jnp.where(first, near[1], far[0]),
        jnp.where(first, far[0], near[1]),
        far[1],
        jnp.where(first, far[3], near[3]),
        jnp.where(first, far[2], far[3]),
        jnp.where(first, near[3], near[2]),
        jnp.where(first, near[2], far[2]),
    ]
    meta = jnp.stack([core, x, yh, z] + places).astype(jnp.int32)

    swap = row_moves(lambda yl, z, c: (yl, z, 1 - c))
    tiles = tile_values.reshape(-1, TILE, TILE)
    part = partition_of.reshape(1, SLOTS)
    plan = call(plan_kernel, [smem, vmem, vmem], array(8, PLAN, dtype=jnp.int32))(
        tile_count.reshape(1), tile_rows.reshape(1, -1), tile_cols.reshape(1, -1)
    )
    other_plan = lax.ppermute(plan, "row", swap)
    plans = [jnp.where(core == c, plan, other_plan) for c in range(2)]
    grouped = call(
        group_kernel,
        [vmem, pinned],
        held(2 * N_COL, SLOTS // N_COL, HALF),
        [pltpu.VMEM((SLOTS, F), BF16), pltpu.SemaphoreType.DMA],
    )(part, features)
    other_tiles = lax.ppermute(after(tiles, grouped), "row", swap)
    near_chips = [[k * 2 * N_COL + m for m in range(2 * N_COL)] for k in range(CHIPS)]
    arrived = exchange(grouped, ("row", "col"), near_chips)
    own = call(interleave_kernel, [vmem], array(2, SLOTS, HALF))(arrived)
    own = after(own, other_tiles, other_plan)

    staged = held(SLOT_CAP + 1, TILE, TILE)
    tiles1 = call(stage_kernel, [smem, pinned, pinned], staged, [pltpu.SemaphoreType.DMA])(
        meta, tiles, after(other_tiles, own)
    )

    def hop(block, *moves):
        def move(yl, z, c):
            if moves[c] is None:
                return None
            return (yl + moves[c][0]) % 2, (z + moves[c][1]) % 4, c

        return lax.ppermute(block, "row", row_moves(move))

    r1 = hop(own, (0, 1), (1, 0))
    r2 = hop(own, (0, 3), None)
    r3 = hop(own, (0, 2), None)
    both = held(2, 2, SLOTS, HALF)
    pair = call(pair_kernel, [vmem] * 2, both)(own, r1)
    s1 = hop(pair, (1, 0), (0, 1))
    s2 = hop(pair, None, (0, 2))
    rest = call(rest_kernel, [smem] + [vmem] * 3, both)(meta, pair, r2, r3)
    s3 = hop(rest, (1, 0), (0, 3))
    shape = (N_ROW, N_COL * PER_PEER, HALF)
    blocks = [b.reshape(1, 2, *shape) for b in (own, r1, r2, r3)]
    blocks += [b.reshape(2, 2, *shape) for b in (s1, s3, s2)]

    total = pltpu.VMEM((ROW_TILES, TILE, HALF), F32)
    source = held(CHIPS, 2, N_ROW, N_COL * PER_PEER, HALF)
    keep1, send1, source, tiles0 = call(
        tiles_y_kernel,
        [smem, smem, vmem, pinned, pinned] + [hbm] * BLOCKS,
        [held(4, SLOTS, HALF), held(4, SLOTS, HALF), source, staged],
        [total, pltpu.SemaphoreType.DMA((CHIPS,)), pltpu.SemaphoreType.DMA],
    )(meta, plans[1], tiles1, tiles, other_tiles, *blocks)
    row0 = call(
        tiles_x_kernel,
        [smem, smem, vmem, vmem],
        [held(2, SLOTS, HALF)] * 4,
        [total],
    )(meta, plans[0], tiles0, source)
    got0 = [lax.ppermute(row0[k], "col", x_moves(k)) for k in (1, 3, 2)]
    got1 = lax.ppermute(send1, "col", y_moves())
    wide, narrow = held(SLOTS, HALF, dtype=F32), held(SLOTS, HALF)
    keep1, *send1 = call(y_summed_kernel, [smem] + [vmem] * 2, [wide] + [narrow] * 3)(
        meta, keep1, got1
    )
    got1 = [lax.ppermute(send1[k - 1], "col", x_moves(k)) for k in (1, 3, 2)]
    keep0, send0 = call(x_summed_kernel, [smem] + [vmem] * 4, [wide, narrow])(
        meta, after(row0[0], got1[0]), *got0
    )
    got0 = lax.ppermute(send0, "col", y_moves())
    mine, others = call(sums_kernel, [smem] + [vmem] * 6, [wide] * 2)(
        meta, keep0, got0, keep1, *got1
    )
    theirs = lax.ppermute(others, "row", swap)
    cotangent = lax.dynamic_slice_in_dim(out_cotangent, col * SLOTS, SLOTS, 0)
    activations, slope = call(
        layer_kernel, [smem] + [vmem] * 4, [array(SLOTS, F), held(SLOTS, F)]
    )(
        meta, mine, theirs, weight, cotangent
    )
    other_slope = lax.ppermute(slope, "row", swap)
    half = call(gradient_kernel, [vmem] * 4, held(HALF, F))(
        mine, others, slope, other_slope
    )

    same_core = [[chip * 2 + c for chip in range(CHIPS)] for c in range(2)]
    shape = (CHIPS, HALF // CHIPS, F)
    piece = added(exchange(half.reshape(shape), "row", same_core))
    piece = added(exchange(jnp.broadcast_to(piece, shape), "col"))
    half = exchange(jnp.broadcast_to(piece.astype(BF16), shape), "row", same_core)
    half = half.reshape(HALF, F)
    other = lax.ppermute(half, "row", swap)
    first = jnp.where(core == 0, half, other).astype(F32)
    second = jnp.where(core == 0, other, half).astype(F32)
    return activations, jnp.concatenate([first, second])


def solution(mesh):
    placed = (
        P(("row", "col"), None),
        P(("row", "col")),
        P(),
        P("row", "col", None, None, None),
        P("row", "col", None),
        P("row", "col", None),
        P("row", "col"),
        P("row", None),
    )
    return jax.shard_map(
        shards,
        mesh=mesh,
        in_specs=placed,
        out_specs=(P(("row", "col"), None), P()),
        check_vma=False,
    )
```

```python
import jax
import jax.numpy as jnp
from jax import lax
from jax.experimental import pallas as pl
from jax.experimental.pallas import tpu as pltpu
from jax.sharding import PartitionSpec as P

N_ROW = 16
N_COL = 8
TILE = 128
SLOTS = 512
F = 512
PER_PEER = 4
HALF = 256
CHIPS = 8
STEPS = (0, 1, 3, 2)
BLOCKS = 7
SLOT_CAP = 192
ROW_TILES = 32
GROUP_BITS = 2
GROUP = 1 << GROUP_BITS
PLAN = SLOT_CAP + ROW_TILES * (GROUP - 1)
UNROLL_BITS = 3
UNROLL = 1 << UNROLL_BITS
BF16 = jnp.bfloat16
F32 = jnp.float32


def params(limit=16):
    return pltpu.CompilerParams(vmem_limit_bytes=limit * 1024 * 1024)


def selection(position, rows, columns):
    wanted = lax.broadcasted_iota(jnp.int32, (rows, columns), 0)
    return jnp.where(position == wanted, 1.0, 0.0).astype(BF16)


def group_kernel(part_ref, features_hbm, out_ref, features_ref, sem):
    copy = pltpu.make_async_copy(features_hbm, features_ref, sem)
    copy.start()
    part = part_ref[...]
    devices = N_ROW * N_COL
    before = jnp.where(
        lax.broadcasted_iota(jnp.int32, (SLOTS, SLOTS), 0)
        < lax.broadcasted_iota(jnp.int32, (SLOTS, SLOTS), 1),
        1.0,
        0.0,
    ).astype(BF16)
    member = jnp.where(
        part == lax.broadcasted_iota(jnp.int32, (devices, SLOTS), 0), 1.0, 0.0
    )
    earlier = jnp.dot(member.astype(BF16), before, preferred_element_type=F32)
    rank = jnp.sum(member * earlier, axis=0, keepdims=True).astype(jnp.int32)
    place = ((part & (N_COL - 1)) * N_ROW + (part >> 3)) * PER_PEER + rank
    pick = selection(place, SLOTS, SLOTS)
    copy.wait()
    for c in range(2):
        wanted = features_ref[:, c * HALF : (c + 1) * HALF]
        picked = jnp.dot(pick, wanted, preferred_element_type=F32).astype(BF16)
        out_ref[c * N_COL : (c + 1) * N_COL] = picked.reshape(N_COL, SLOTS // N_COL, HALF)


def interleave_kernel(arrived_ref, out_ref):
    source = lax.broadcasted_iota(jnp.int32, (1, SLOTS), 1)
    giver, inner = source >> 6, source & 63
    place = (inner >> 2) * (N_COL * PER_PEER) + giver * PER_PEER + (inner & 3)
    pick = selection(place, SLOTS, SLOTS)
    for c in range(2):
        rows = arrived_ref[c * N_COL : (c + 1) * N_COL].reshape(SLOTS, HALF)
        out_ref[c] = jnp.dot(pick, rows, preferred_element_type=F32).astype(BF16)


def pair_kernel(a_ref, b_ref, out_ref):
    out_ref[0] = a_ref[...]
    out_ref[1] = b_ref[...]


def rest_kernel(meta_ref, pair_ref, a_ref, b_ref, out_ref):
    core = meta_ref[0]

    @pl.when(core == 0)
    def _():
        out_ref[0] = a_ref[...]
        out_ref[1] = b_ref[...]

    @pl.when(core != 0)
    def _():
        out_ref[...] = pair_ref[...]


def plan_kernel(count_ref, rows_ref, cols_ref, plan_ref):
    slot = lax.broadcasted_iota(jnp.int32, (1, SLOT_CAP), 1)
    rows = rows_ref[...]
    live = slot < count_ref[0]
    kinds = lax.broadcasted_iota(jnp.int32, (ROW_TILES, SLOT_CAP), 0)
    member = jnp.where(live & (rows == kinds), 1.0, 0.0)
    before = jnp.where(
        lax.broadcasted_iota(jnp.int32, (SLOT_CAP, SLOT_CAP), 0)
        < lax.broadcasted_iota(jnp.int32, (SLOT_CAP, SLOT_CAP), 1),
        1.0,
        0.0,
    ).astype(BF16)
    earlier = jnp.dot(member.astype(BF16), before, preferred_element_type=F32)
    number = jnp.sum(member, axis=1, keepdims=True).astype(jnp.int32)
    groups = jnp.broadcast_to((number + (GROUP - 1)) >> GROUP_BITS, (ROW_TILES, TILE))
    below = jnp.where(
        lax.broadcasted_iota(jnp.int32, (ROW_TILES, ROW_TILES), 1)
        < lax.broadcasted_iota(jnp.int32, (ROW_TILES, ROW_TILES), 0),
        1.0,
        0.0,
    ).astype(BF16)
    groups = groups.astype(F32)
    start = jnp.dot(below, groups.astype(BF16), preferred_element_type=F32)[:, :1]
    total = jnp.sum(groups, axis=0, keepdims=True)[:, :1]
    place = jnp.sum(member * (GROUP * start + earlier + 1.0), axis=0, keepdims=True) - 1.0
    taken = selection(place.astype(jnp.int32), PLAN, SLOT_CAP)
    line = lax.broadcasted_iota(jnp.int32, (8, SLOT_CAP), 0)
    values = jnp.where(line == 0, slot - SLOT_CAP, jnp.where(line == 1, cols_ref[...], rows))
    found = lax.dot_general(
        values.astype(F32).astype(BF16),
        taken,
        (((1,), (1,)), ((), ())),
        preferred_element_type=F32,
    )
    line = lax.broadcasted_iota(jnp.int32, (8, PLAN), 0)
    found = jnp.where(line == 0, found + SLOT_CAP, jnp.where(line == 3, total, found))
    plan_ref[...] = found.astype(jnp.int32)


def start_tiles(part, core, own_hbm, other_hbm, out, sem):
    out[SLOT_CAP] = jnp.zeros((TILE, TILE), BF16)
    for mine, hbm in ((True, own_hbm), (False, other_hbm)):

        @pl.when((core == part) == mine)
        def _():
            pltpu.make_async_copy(hbm, out.at[pl.ds(0, SLOT_CAP)], sem).start()

    return pltpu.make_async_copy(own_hbm, out.at[pl.ds(0, SLOT_CAP)], sem)


def stage_kernel(meta_ref, own_hbm, other_hbm, out_ref, sem):
    start_tiles(1, meta_ref[0], own_hbm, other_hbm, out_ref, sem).wait()


def add_tiles(plan_ref, tiles, source, total):
    total[...] = jnp.zeros_like(total)

    def product(g):
        left, right = [], []
        for e in range(GROUP):
            u = plan_ref[1, g * GROUP + e]
            left.append(tiles[plan_ref[0, g * GROUP + e]])
            right.append(source[pl.ds((u & 3) * 2, 2), :, u >> 2].reshape(TILE, HALF))
        return jnp.dot(
            jnp.concatenate(left, axis=1),
            jnp.concatenate(right, axis=0),
            preferred_element_type=F32,
        )

    def some_groups(h, carry):
        found = [
            (plan_ref[2, (h * UNROLL + k) * GROUP], product(h * UNROLL + k))
            for k in range(UNROLL)
        ]
        for place, value in found:
            total[place] += value
        return carry

    lax.fori_loop(0, (plan_ref[3, 0] + UNROLL - 1) >> UNROLL_BITS, some_groups, 0)


def narrow_block(total, yh, x):
    rows = total[pl.ds((yh * 4 + x) * 4, 4)].astype(BF16)
    return rows.reshape(SLOTS, HALF)


def tiles_kernel(meta_ref, plan0_ref, plan1_ref, tiles1, own_hbm, other_hbm, *refs):
    blocks, outs = refs[:BLOCKS], refs[BLOCKS : BLOCKS + 4]
    source, tiles0, total, sems, tiles_sem = refs[BLOCKS + 4 :]
    core, x, yh = meta_ref[0], meta_ref[1], meta_ref[2]
    own, r1, r2, r3, s1, s3, s2 = blocks
    shared = [(own, 0), (r1, 0), (s1, 0), (s1, 1), (s3, 0), (s3, 1)]

    def fetch(block, k):
        return pltpu.make_async_copy(
            block[0].at[block[1]], source.at[meta_ref[4 + k]], sems.at[k]
        )

    for k, block in enumerate(shared):
        fetch(block, k).start()
    for c, rest in enumerate((((r2, 0), (r3, 0)), ((s2, 0), (s2, 1)))):

        @pl.when(core == c)
        def _():
            for k, block in enumerate(rest):
                fetch(block, len(shared) + k).start()

    for k in range(CHIPS):
        fetch(shared[0], k).wait()
    coming = start_tiles(0, core, own_hbm, other_hbm, tiles0, tiles_sem)
    for part, plan_ref, tiles in ((1, plan1_ref, tiles1), (0, plan0_ref, tiles0)):
        if part == 0:
            coming.wait()
        add_tiles(plan_ref, tiles, source, total)

        @pl.when(core == 0)
        def _():
            for k, out in enumerate(outs):
                for to in range(2):
                    out[part * 2 + to] = narrow_block(total, to, (x + STEPS[k]) & 3)

        @pl.when(core != 0)
        def _():
            for to in range(4):
                outs[0][part * 4 + to] = narrow_block(total, yh, to)
                outs[1 + part][to] = narrow_block(total, 1 - yh, to)


def first_sums_kernel(meta_ref, kept_ref, a_ref, b_ref, c_ref, keep_ref, *sends):
    core, x, yh = meta_ref[0], meta_ref[1], meta_ref[2]

    @pl.when(core == 0)
    def _():
        for part in range(2):
            for to, out in ((yh, keep_ref), (1 - yh, sends[0])):
                k = part * 2 + to
                pair = kept_ref[k].astype(F32) + a_ref[k].astype(F32)
                pair = pair + (b_ref[k].astype(F32) + c_ref[k].astype(F32))
                out[part] = pair.astype(out.dtype)

    @pl.when(core != 0)
    def _():
        for part, got in enumerate((a_ref, b_ref)):
            for step, out in zip(STEPS, (keep_ref, *sends)):
                k = (x + step) & 3
                pair = kept_ref[part * 4 + k].astype(F32) + got[k].astype(F32)
                out[part] = pair.astype(out.dtype)


def sums_kernel(meta_ref, keep_ref, a_ref, b_ref, c_ref, mine_ref, send_ref):
    core = meta_ref[0]

    @pl.when(core == 0)
    def _():
        for part, out in ((0, mine_ref), (1, send_ref)):
            out[...] = keep_ref[part] + a_ref[part].astype(F32)

    @pl.when(core != 0)
    def _():
        for part, out in ((1, mine_ref), (0, send_ref)):
            pair = keep_ref[part] + a_ref[part].astype(F32)
            out[...] = pair + (b_ref[part].astype(F32) + c_ref[part].astype(F32))


def two_parts(value):
    high = value.astype(BF16)
    return high, (value - high.astype(F32)).astype(BF16)


def layer_kernel(meta_ref, mine_ref, got_ref, weight_ref, cotangent_ref, act_ref, slope_ref):
    core = meta_ref[0]
    pre = jnp.zeros((SLOTS, F), F32)
    for half, mixed in ((core, mine_ref[...]), (1 - core, got_ref[...])):
        weight = weight_ref[pl.ds(pl.multiple_of(half * HALF, HALF), HALF), :]
        for piece in two_parts(mixed):
            pre = pre + jnp.dot(piece, weight, preferred_element_type=F32)
    sigmoid = jax.nn.sigmoid(pre)
    act_ref[...] = (pre * sigmoid).astype(BF16)
    slope_ref[...] = (
        cotangent_ref[...].astype(F32) * (sigmoid * (1.0 + pre * (1.0 - sigmoid)))
    ).astype(BF16)


def gradient_kernel(mine_ref, other_ref, slope_ref, other_slope_ref, grad_ref):
    contract = (((0,), (0,)), ((), ()))
    grad = jnp.zeros((HALF, F), F32)
    for mixed, slope in ((mine_ref, slope_ref), (other_ref, other_slope_ref)):
        for piece in two_parts(mixed[...]):
            grad = grad + lax.dot_general(
                piece, slope[...], contract, preferred_element_type=F32
            )
    grad_ref[...] = (grad * (1.0 / 256.0)).astype(BF16)


def row_moves(move):
    pairs = []
    for yl in range(2):
        for z in range(4):
            for c in range(2):
                to = move(yl, z, c)
                if to is not None:
                    a, b, d = to
                    pairs.append(((yl * 4 + z) * 2 + c, (a * 4 + b) * 2 + d))
    return pairs


def col_moves(move0, move1):
    pairs = []
    for row in range(N_ROW):
        move = (move0, move1)[row % 2]
        if move is not None:
            for col in range(N_COL):
                yh, x = move(col // 4, col % 4)
                pairs.append((row * N_COL + col, row * N_COL + yh * 4 + x))
    return pairs


def exchange(parts, axis, groups=None):
    return lax.all_to_all(
        parts, axis, split_axis=0, concat_axis=0, axis_index_groups=groups, tiled=True
    )


def added(parts):
    parts = parts.astype(F32)
    a = (parts[0] + parts[1]) + (parts[2] + parts[3])
    return a + ((parts[4] + parts[5]) + (parts[6] + parts[7]))


def call(kernel, in_specs, outs, scratch=(), limit=16):
    made = pl.pallas_call(
        kernel,
        in_specs=in_specs,
        out_specs=jax.tree.map(lambda _: pl.BlockSpec(memory_space=pltpu.VMEM), outs),
        out_shape=outs,
        scratch_shapes=list(scratch),
        compiler_params=params(limit),
    )

    def run(*operands):
        held = [
            pltpu.with_memory_space_constraint(o, spec.memory_space)
            if spec.memory_space in (pltpu.VMEM, pltpu.MemorySpace.HBM)
            else o
            for spec, o in zip(in_specs, operands)
        ]
        return made(*held)

    return run


def array(*shape, dtype=BF16):
    return jax.ShapeDtypeStruct(shape, dtype)


def held(*shape, dtype=BF16):
    return pltpu.VMEM(shape, dtype)


def after(value, *others):
    return lax.optimization_barrier((value, *others))[0]


def shards(
    features, partition_of, weight, tile_values, tile_rows, tile_cols, tile_count, out_cotangent
):
    row = lax.axis_index("row")
    col = lax.axis_index("col")
    core, z, yl = row % 2, (row // 2) % 4, row // 8
    x, yh = col % 4, col // 4
    vmem = pl.BlockSpec(memory_space=pltpu.VMEM)
    smem = pl.BlockSpec(memory_space=pltpu.SMEM)
    hbm = pl.BlockSpec(memory_space=pl.ANY)
    pinned = pl.BlockSpec(memory_space=pltpu.MemorySpace.HBM)

    here, there = yl * 4, (1 - yl) * 4
    near = [here + (z - k) % 4 for k in range(4)]
    far = [there + (z - k) % 4 for k in range(4)]
    first = core == 0
    places = [
        near[0],
        jnp.where(first, near[1], far[0]),
        jnp.where(first, far[0], near[1]),
        far[1],
        jnp.where(first, far[3], near[3]),
        jnp.where(first, far[2], far[3]),
        jnp.where(first, near[3], near[2]),
        jnp.where(first, near[2], far[2]),
    ]
    meta = jnp.stack([core, x, yh, z] + places).astype(jnp.int32)

    swap = row_moves(lambda yl, z, c: (yl, z, 1 - c))
    tiles = tile_values.reshape(-1, TILE, TILE)
    part = partition_of.reshape(1, SLOTS)
    plan = call(plan_kernel, [smem, vmem, vmem], array(8, PLAN, dtype=jnp.int32))(
        tile_count.reshape(1), tile_rows.reshape(1, -1), tile_cols.reshape(1, -1)
    )
    other_plan = lax.ppermute(plan, "row", swap)
    plans = [jnp.where(core == c, plan, other_plan) for c in range(2)]
    grouped = call(
        group_kernel,
        [vmem, pinned],
        held(2 * N_COL, SLOTS // N_COL, HALF),
        [pltpu.VMEM((SLOTS, F), BF16), pltpu.SemaphoreType.DMA],
    )(part, features)
    other_tiles = lax.ppermute(after(tiles, grouped), "row", swap)
    near_chips = [[k * 2 * N_COL + m for m in range(2 * N_COL)] for k in range(CHIPS)]
    arrived = exchange(grouped, ("row", "col"), near_chips)
    own = call(interleave_kernel, [vmem], array(2, SLOTS, HALF))(arrived)
    own = after(own, other_tiles, other_plan)

    staged = held(SLOT_CAP + 1, TILE, TILE)
    tiles1 = call(stage_kernel, [smem, pinned, pinned], staged, [pltpu.SemaphoreType.DMA])(
        meta, tiles, after(other_tiles, own)
    )

    def hop(block, *moves):
        def move(yl, z, c):
            if moves[c] is None:
                return None
            return (yl + moves[c][0]) % 2, (z + moves[c][1]) % 4, c

        return lax.ppermute(block, "row", row_moves(move))

    r3 = hop(own, (0, 2), None)
    r1 = hop(own, (0, 1), (1, 0))
    r2 = hop(own, (0, 3), None)
    both = held(2, 2, SLOTS, HALF)
    pair = call(pair_kernel, [vmem] * 2, both)(own, r1)
    s1 = hop(pair, (1, 0), (0, 1))
    s2 = hop(pair, None, (0, 2))
    rest = call(rest_kernel, [smem] + [vmem] * 3, both)(meta, pair, r2, r3)
    s3 = hop(rest, (1, 0), (0, 3))
    shape = (N_ROW, N_COL * PER_PEER, HALF)
    blocks = [b.reshape(1, 2, *shape) for b in (own, r1, r2, r3)]
    blocks += [b.reshape(2, 2, *shape) for b in (s1, s3, s2)]

    four = held(4, SLOTS, HALF)
    kept, *sends = call(
        tiles_kernel,
        [smem, smem, smem, vmem, pinned, pinned] + [hbm] * BLOCKS,
        [held(8, SLOTS, HALF), four, four, four],
        [
            pltpu.VMEM((CHIPS, 2, N_ROW, N_COL * PER_PEER, HALF), BF16),
            pltpu.VMEM((SLOT_CAP + 1, TILE, TILE), BF16),
            pltpu.VMEM((ROW_TILES, TILE, HALF), F32),
            pltpu.SemaphoreType.DMA((CHIPS,)),
            pltpu.SemaphoreType.DMA,
        ],
        limit=24,
    )(meta, *plans, tiles1, tiles, other_tiles, *blocks)

    along_x = [lambda yh, x, k=k: (yh, (x + k) % 4) for k in STEPS]
    along_y = lambda yh, x: (1 - yh, x)
    got = [
        lax.ppermute(block, ("row", "col"), col_moves(*moves))
        for block, moves in zip(
            sends, ((along_x[1], along_y), (along_x[2], along_y), (along_x[3], None))
        )
    ]
    two = held(2, SLOTS, HALF)
    keep, *sends = call(
        first_sums_kernel,
        [smem] + [vmem] * 4,
        [held(2, SLOTS, HALF, dtype=F32), two, two, two],
    )(meta, kept, *got)
    got = [
        lax.ppermute(block, ("row", "col"), col_moves(*moves))
        for block, moves in zip(
            sends, ((along_y, along_x[1]), (None, along_x[2]), (None, along_x[3]))
        )
    ]
    wide = held(SLOTS, HALF, dtype=F32)
    mine, others = call(sums_kernel, [smem] + [vmem] * 4, [wide] * 2)(meta, keep, *got)
    theirs = lax.ppermute(others, "row", swap)
    cotangent = lax.dynamic_slice_in_dim(out_cotangent, col * SLOTS, SLOTS, 0)
    activations, slope = call(
        layer_kernel, [smem] + [vmem] * 4, [array(SLOTS, F), held(SLOTS, F)]
    )(
        meta, mine, theirs, weight, cotangent
    )
    other_slope = lax.ppermute(slope, "row", swap)
    half = call(gradient_kernel, [vmem] * 4, held(HALF, F))(
        mine, others, slope, other_slope
    )

    same_core = [[chip * 2 + c for chip in range(CHIPS)] for c in range(2)]
    shape = (CHIPS, HALF // CHIPS, F)
    piece = added(exchange(half.reshape(shape), "row", same_core))
    piece = added(exchange(jnp.broadcast_to(piece, shape), "col"))
    half = exchange(jnp.broadcast_to(piece.astype(BF16), shape), "row", same_core)
    half = half.reshape(HALF, F)
    other = lax.ppermute(half, "row", swap)
    first = jnp.where(core == 0, half, other).astype(F32)
    second = jnp.where(core == 0, other, half).astype(F32)
    return activations, jnp.concatenate([first, second])


def solution(mesh):
    placed = (
        P(("row", "col"), None),
        P(("row", "col")),
        P(),
        P("row", "col", None, None, None),
        P("row", "col", None),
        P("row", "col", None),
        P("row", "col"),
        P("row", None),
    )
    return jax.shard_map(
        shards,
        mesh=mesh,
        in_specs=placed,
        out_specs=(P(("row", "col"), None), P()),
        check_vma=False,
    )
```

```python
import jax
import jax.numpy as jnp
from jax import lax
from jax.experimental import pallas as pl
from jax.experimental.pallas import tpu as pltpu
from jax.sharding import PartitionSpec as P

N_ROW = 16
N_COL = 8
TILE = 128
SLOTS = 512
F = 512
PER_PEER = 4
HALF = 256
CHIPS = 8
BLOCKS = 7
SLOT_CAP = 192
ROW_TILES = 32
GROUP_BITS = 2
GROUP = 1 << GROUP_BITS
PLAN = SLOT_CAP + ROW_TILES * (GROUP - 1)
UNROLL_BITS = 3
UNROLL = 1 << UNROLL_BITS
BF16 = jnp.bfloat16
F32 = jnp.float32


def params(limit=16):
    return pltpu.CompilerParams(vmem_limit_bytes=limit * 1024 * 1024)


def selection(position, rows, columns):
    wanted = lax.broadcasted_iota(jnp.int32, (rows, columns), 0)
    return jnp.where(position == wanted, 1.0, 0.0).astype(BF16)


def group_kernel(part_ref, features_hbm, out_ref, features_ref, sem):
    copy = pltpu.make_async_copy(features_hbm, features_ref, sem)
    copy.start()
    part = part_ref[...]
    devices = N_ROW * N_COL
    before = jnp.where(
        lax.broadcasted_iota(jnp.int32, (SLOTS, SLOTS), 0)
        < lax.broadcasted_iota(jnp.int32, (SLOTS, SLOTS), 1),
        1.0,
        0.0,
    ).astype(BF16)
    member = jnp.where(
        part == lax.broadcasted_iota(jnp.int32, (devices, SLOTS), 0), 1.0, 0.0
    )
    earlier = jnp.dot(member.astype(BF16), before, preferred_element_type=F32)
    rank = jnp.sum(member * earlier, axis=0, keepdims=True).astype(jnp.int32)
    place = ((part & (N_COL - 1)) * N_ROW + (part >> 3)) * PER_PEER + rank
    pick = selection(place, SLOTS, SLOTS)
    copy.wait()
    for c in range(2):
        wanted = features_ref[:, c * HALF : (c + 1) * HALF]
        picked = jnp.dot(pick, wanted, preferred_element_type=F32).astype(BF16)
        out_ref[c * N_COL : (c + 1) * N_COL] = picked.reshape(N_COL, SLOTS // N_COL, HALF)


def interleave_kernel(arrived_ref, out_ref):
    source = lax.broadcasted_iota(jnp.int32, (1, SLOTS), 1)
    giver, inner = source >> 6, source & 63
    place = (inner >> 2) * (N_COL * PER_PEER) + giver * PER_PEER + (inner & 3)
    pick = selection(place, SLOTS, SLOTS)
    for c in range(2):
        rows = arrived_ref[c * N_COL : (c + 1) * N_COL].reshape(SLOTS, HALF)
        out_ref[c] = jnp.dot(pick, rows, preferred_element_type=F32).astype(BF16)


def pair_kernel(a_ref, b_ref, out_ref):
    out_ref[0] = a_ref[...]
    out_ref[1] = b_ref[...]


def rest_kernel(meta_ref, pair_ref, a_ref, b_ref, out_ref):
    core = meta_ref[0]

    @pl.when(core == 0)
    def _():
        out_ref[0] = a_ref[...]
        out_ref[1] = b_ref[...]

    @pl.when(core != 0)
    def _():
        out_ref[...] = pair_ref[...]


def plan_kernel(count_ref, rows_ref, cols_ref, plan_ref):
    slot = lax.broadcasted_iota(jnp.int32, (1, SLOT_CAP), 1)
    rows = rows_ref[...]
    live = slot < count_ref[0]
    kinds = lax.broadcasted_iota(jnp.int32, (ROW_TILES, SLOT_CAP), 0)
    member = jnp.where(live & (rows == kinds), 1.0, 0.0)
    before = jnp.where(
        lax.broadcasted_iota(jnp.int32, (SLOT_CAP, SLOT_CAP), 0)
        < lax.broadcasted_iota(jnp.int32, (SLOT_CAP, SLOT_CAP), 1),
        1.0,
        0.0,
    ).astype(BF16)
    earlier = jnp.dot(member.astype(BF16), before, preferred_element_type=F32)
    number = jnp.sum(member, axis=1, keepdims=True).astype(jnp.int32)
    groups = jnp.broadcast_to((number + (GROUP - 1)) >> GROUP_BITS, (ROW_TILES, TILE))
    below = jnp.where(
        lax.broadcasted_iota(jnp.int32, (ROW_TILES, ROW_TILES), 1)
        < lax.broadcasted_iota(jnp.int32, (ROW_TILES, ROW_TILES), 0),
        1.0,
        0.0,
    ).astype(BF16)
    groups = groups.astype(F32)
    start = jnp.dot(below, groups.astype(BF16), preferred_element_type=F32)[:, :1]
    total = jnp.sum(groups, axis=0, keepdims=True)[:, :1]
    place = jnp.sum(member * (GROUP * start + earlier + 1.0), axis=0, keepdims=True) - 1.0
    taken = selection(place.astype(jnp.int32), PLAN, SLOT_CAP)
    line = lax.broadcasted_iota(jnp.int32, (8, SLOT_CAP), 0)
    values = jnp.where(line == 0, slot - SLOT_CAP, jnp.where(line == 1, cols_ref[...], rows))
    found = lax.dot_general(
        values.astype(F32).astype(BF16),
        taken,
        (((1,), (1,)), ((), ())),
        preferred_element_type=F32,
    )
    line = lax.broadcasted_iota(jnp.int32, (8, PLAN), 0)
    found = jnp.where(line == 0, found + SLOT_CAP, jnp.where(line == 3, total, found))
    plan_ref[...] = found.astype(jnp.int32)


def start_tiles(part, core, own_hbm, other_hbm, out, sem):
    out[SLOT_CAP] = jnp.zeros((TILE, TILE), BF16)
    for mine, hbm in ((True, own_hbm), (False, other_hbm)):

        @pl.when((core == part) == mine)
        def _():
            pltpu.make_async_copy(hbm, out.at[pl.ds(0, SLOT_CAP)], sem).start()

    return pltpu.make_async_copy(own_hbm, out.at[pl.ds(0, SLOT_CAP)], sem)


def stage_kernel(meta_ref, own_hbm, other_hbm, out_ref, sem):
    start_tiles(1, meta_ref[0], own_hbm, other_hbm, out_ref, sem).wait()


def add_tiles(plan_ref, tiles, source, total):
    total[...] = jnp.zeros_like(total)

    def product(g):
        left, right = [], []
        for e in range(GROUP):
            u = plan_ref[1, g * GROUP + e]
            left.append(tiles[plan_ref[0, g * GROUP + e]])
            right.append(source[pl.ds((u & 3) * 2, 2), :, u >> 2].reshape(TILE, HALF))
        return jnp.dot(
            jnp.concatenate(left, axis=1),
            jnp.concatenate(right, axis=0),
            preferred_element_type=F32,
        )

    def some_groups(h, carry):
        found = [
            (plan_ref[2, (h * UNROLL + k) * GROUP], product(h * UNROLL + k))
            for k in range(UNROLL)
        ]
        for place, value in found:
            total[place] += value
        return carry

    lax.fori_loop(0, (plan_ref[3, 0] + UNROLL - 1) >> UNROLL_BITS, some_groups, 0)


def narrow_block(total, yh, x):
    rows = total[pl.ds((yh * 4 + x) * 4, 4)].astype(BF16)
    return rows.reshape(SLOTS, HALF)


def tiles_y_kernel(meta_ref, plan_ref, tiles, own_hbm, other_hbm, *refs):
    blocks, (keep_ref, send_ref, source, next_tiles) = refs[:BLOCKS], refs[BLOCKS:-3]
    total, sems, tiles_sem = refs[-3:]
    core, yh = meta_ref[0], meta_ref[2]

    own, r1, r2, r3, s1, s3, s2 = blocks
    shared = [(own, 0), (r1, 0), (s1, 0), (s1, 1), (s3, 0), (s3, 1)]

    def fetch(block, k):
        return pltpu.make_async_copy(
            block[0].at[block[1]], source.at[meta_ref[4 + k]], sems.at[k]
        )

    for k, block in enumerate(shared):
        fetch(block, k).start()
    for c, rest in enumerate((((r2, 0), (r3, 0)), ((s2, 0), (s2, 1)))):

        @pl.when(core == c)
        def _():
            for k, block in enumerate(rest):
                fetch(block, len(shared) + k).start()

    for k in range(CHIPS):
        fetch(shared[0], k).wait()
    coming = start_tiles(0, core, own_hbm, other_hbm, next_tiles, tiles_sem)
    add_tiles(plan_ref, tiles, source, total)
    for out, to in ((send_ref, 1 - yh), (keep_ref, yh)):
        for x in range(4):
            out[x] = narrow_block(total, to, x)
    coming.wait()


def tiles_x_kernel(meta_ref, plan_ref, tiles, source, *refs):
    outs, total = refs[:4], refs[4]
    x = meta_ref[1]
    add_tiles(plan_ref, tiles, source, total)
    for k, out in enumerate(outs):
        for yh in range(2):
            out[yh] = narrow_block(total, yh, (x + k) & 3)


def x_summed_kernel(meta_ref, own_ref, a_ref, b_ref, c_ref, keep_ref, send_ref):
    yh = meta_ref[2]

    def summed(k):
        pair = own_ref[k].astype(F32) + a_ref[k].astype(F32)
        return pair + (b_ref[k].astype(F32) + c_ref[k].astype(F32))

    keep_ref[...] = summed(yh)
    send_ref[...] = summed(1 - yh).astype(BF16)


def y_summed_kernel(meta_ref, own_ref, got_ref, keep_ref, a_ref, b_ref, c_ref):
    x = meta_ref[1]

    def summed(k):
        return own_ref[k].astype(F32) + got_ref[k].astype(F32)

    keep_ref[...] = summed(x)
    for k, out in ((1, a_ref), (2, b_ref), (3, c_ref)):
        out[...] = summed((x + k) & 3).astype(BF16)


def sums_kernel(meta_ref, keep0, got0, keep1, a_ref, b_ref, c_ref, mine_ref, send_ref):
    core = meta_ref[0]
    first = keep0[...] + got0[...].astype(F32)
    second = keep1[...] + a_ref[...].astype(F32)
    second = second + (b_ref[...].astype(F32) + c_ref[...].astype(F32))
    mine_ref[...] = jnp.where(core == 0, first, second)
    send_ref[...] = jnp.where(core == 0, second, first)


def two_parts(value):
    high = value.astype(BF16)
    return high, (value - high.astype(F32)).astype(BF16)


def layer_kernel(meta_ref, mine_ref, got_ref, weight_ref, cotangent_ref, act_ref, slope_ref):
    core = meta_ref[0]
    pre = jnp.zeros((SLOTS, F), F32)
    for half, mixed in ((core, mine_ref[...]), (1 - core, got_ref[...])):
        weight = weight_ref[pl.ds(pl.multiple_of(half * HALF, HALF), HALF), :]
        for piece in two_parts(mixed):
            pre = pre + jnp.dot(piece, weight, preferred_element_type=F32)
    sigmoid = jax.nn.sigmoid(pre)
    act_ref[...] = (pre * sigmoid).astype(BF16)
    slope_ref[...] = (
        cotangent_ref[...].astype(F32) * (sigmoid * (1.0 + pre * (1.0 - sigmoid)))
    ).astype(BF16)


def gradient_kernel(mine_ref, other_ref, slope_ref, other_slope_ref, grad_ref):
    contract = (((0,), (0,)), ((), ()))
    grad = jnp.zeros((HALF, F), F32)
    for mixed, slope in ((mine_ref, slope_ref), (other_ref, other_slope_ref)):
        for piece in two_parts(mixed[...]):
            grad = grad + lax.dot_general(
                piece, slope[...], contract, preferred_element_type=F32
            )
    grad_ref[...] = (grad * (1.0 / 256.0)).astype(BF16)


def row_moves(move):
    pairs = []
    for yl in range(2):
        for z in range(4):
            for c in range(2):
                to = move(yl, z, c)
                if to is not None:
                    a, b, d = to
                    pairs.append(((yl * 4 + z) * 2 + c, (a * 4 + b) * 2 + d))
    return pairs


def x_moves(k):
    return [(yh * 4 + x, yh * 4 + (x + k) % 4) for yh in range(2) for x in range(4)]


def y_moves():
    return [(yh * 4 + x, (1 - yh) * 4 + x) for yh in range(2) for x in range(4)]


def exchange(parts, axis, groups=None):
    return lax.all_to_all(
        parts, axis, split_axis=0, concat_axis=0, axis_index_groups=groups, tiled=True
    )


def added(parts):
    parts = parts.astype(F32)
    a = (parts[0] + parts[1]) + (parts[2] + parts[3])
    return a + ((parts[4] + parts[5]) + (parts[6] + parts[7]))


def call(kernel, in_specs, outs, scratch=(), limit=16):
    made = pl.pallas_call(
        kernel,
        in_specs=in_specs,
        out_specs=jax.tree.map(lambda _: pl.BlockSpec(memory_space=pltpu.VMEM), outs),
        out_shape=outs,
        scratch_shapes=list(scratch),
        compiler_params=params(limit),
    )

    def run(*operands):
        held = [
            pltpu.with_memory_space_constraint(o, spec.memory_space)
            if spec.memory_space in (pltpu.VMEM, pltpu.MemorySpace.HBM)
            else o
            for spec, o in zip(in_specs, operands)
        ]
        return made(*held)

    return run


def array(*shape, dtype=BF16):
    return jax.ShapeDtypeStruct(shape, dtype)


def held(*shape, dtype=BF16):
    return pltpu.VMEM(shape, dtype)


def after(value, *others):
    return lax.optimization_barrier((value, *others))[0]


def shards(
    features, partition_of, weight, tile_values, tile_rows, tile_cols, tile_count, out_cotangent
):
    row = lax.axis_index("row")
    col = lax.axis_index("col")
    core, z, yl = row % 2, (row // 2) % 4, row // 8
    x, yh = col % 4, col // 4
    vmem = pl.BlockSpec(memory_space=pltpu.VMEM)
    smem = pl.BlockSpec(memory_space=pltpu.SMEM)
    hbm = pl.BlockSpec(memory_space=pl.ANY)
    pinned = pl.BlockSpec(memory_space=pltpu.MemorySpace.HBM)

    here, there = yl * 4, (1 - yl) * 4
    near = [here + (z - k) % 4 for k in range(4)]
    far = [there + (z - k) % 4 for k in range(4)]
    first = core == 0
    places = [
        near[0],
        jnp.where(first, near[1], far[0]),
        jnp.where(first, far[0], near[1]),
        far[1],
        jnp.where(first, far[3], near[3]),
        jnp.where(first, far[2], far[3]),
        jnp.where(first, near[3], near[2]),
        jnp.where(first, near[2], far[2]),
    ]
    meta = jnp.stack([core, x, yh, z] + places).astype(jnp.int32)

    swap = row_moves(lambda yl, z, c: (yl, z, 1 - c))
    tiles = tile_values.reshape(-1, TILE, TILE)
    part = partition_of.reshape(1, SLOTS)
    plan = call(plan_kernel, [smem, vmem, vmem], array(8, PLAN, dtype=jnp.int32))(
        tile_count.reshape(1), tile_rows.reshape(1, -1), tile_cols.reshape(1, -1)
    )
    other_plan = lax.ppermute(plan, "row", swap)
    plans = [jnp.where(core == c, plan, other_plan) for c in range(2)]
    grouped = call(
        group_kernel,
        [vmem, pinned],
        held(2 * N_COL, SLOTS // N_COL, HALF),
        [pltpu.VMEM((SLOTS, F), BF16), pltpu.SemaphoreType.DMA],
    )(part, features)
    other_tiles = lax.ppermute(after(tiles, grouped), "row", swap)
    near_chips = [[k * 2 * N_COL + m for m in range(2 * N_COL)] for k in range(CHIPS)]
    arrived = exchange(grouped, ("row", "col"), near_chips)
    own = call(interleave_kernel, [vmem], array(2, SLOTS, HALF))(arrived)
    own = after(own, other_tiles, other_plan)

    staged = held(SLOT_CAP + 1, TILE, TILE)
    tiles1 = call(stage_kernel, [smem, pinned, pinned], staged, [pltpu.SemaphoreType.DMA])(
        meta, tiles, after(other_tiles, own)
    )

    def hop(block, *moves):
        def move(yl, z, c):
            if moves[c] is None:
                return None
            return (yl + moves[c][0]) % 2, (z + moves[c][1]) % 4, c

        return lax.ppermute(block, "row", row_moves(move))

    r1 = hop(own, (0, 1), (1, 0))
    r2 = hop(own, (0, 3), None)
    r3 = hop(r2, (0, 3), None)
    both = held(2, 2, SLOTS, HALF)
    pair = call(pair_kernel, [vmem] * 2, both)(own, r1)
    s1 = hop(pair, (1, 0), (0, 1))
    s2 = hop(s1, None, (0, 1))
    rest = call(rest_kernel, [smem] + [vmem] * 3, both)(meta, pair, r2, r3)
    s3 = hop(rest, (1, 0), (0, 3))
    shape = (N_ROW, N_COL * PER_PEER, HALF)
    blocks = [b.reshape(1, 2, *shape) for b in (own, r1, r2, r3)]
    blocks += [b.reshape(2, 2, *shape) for b in (s1, s3, s2)]

    total = pltpu.VMEM((ROW_TILES, TILE, HALF), F32)
    source = held(CHIPS, 2, N_ROW, N_COL * PER_PEER, HALF)
    keep1, send1, source, tiles0 = call(
        tiles_y_kernel,
        [smem, smem, vmem, pinned, pinned] + [pinned] * BLOCKS,
        [held(4, SLOTS, HALF), held(4, SLOTS, HALF), source, staged],
        [total, pltpu.SemaphoreType.DMA((CHIPS,)), pltpu.SemaphoreType.DMA],
    )(meta, plans[1], tiles1, tiles, other_tiles, *blocks)
    row0 = call(
        tiles_x_kernel,
        [smem, smem, vmem, vmem],
        [held(2, SLOTS, HALF)] * 4,
        [total],
    )(meta, plans[0], tiles0, source)
    got0 = [lax.ppermute(row0[k], "col", x_moves(k)) for k in (1, 3, 2)]
    got1 = lax.ppermute(send1, "col", y_moves())
    wide, narrow = held(SLOTS, HALF, dtype=F32), held(SLOTS, HALF)
    keep1, *send1 = call(y_summed_kernel, [smem] + [vmem] * 2, [wide] + [narrow] * 3)(
        meta, keep1, got1
    )
    got1 = [lax.ppermute(send1[k - 1], "col", x_moves(k)) for k in (1, 3, 2)]
    keep0, send0 = call(x_summed_kernel, [smem] + [vmem] * 4, [wide, narrow])(
        meta, after(row0[0], got1[0]), *got0
    )
    got0 = lax.ppermute(send0, "col", y_moves())
    mine, others = call(sums_kernel, [smem] + [vmem] * 6, [wide] * 2)(
        meta, keep0, got0, keep1, *got1
    )
    theirs = lax.ppermute(others, "row", swap)
    cotangent = lax.dynamic_slice_in_dim(out_cotangent, col * SLOTS, SLOTS, 0)
    activations, slope = call(
        layer_kernel, [smem] + [vmem] * 4, [array(SLOTS, F), held(SLOTS, F)]
    )(
        meta, mine, theirs, weight, cotangent
    )
    other_slope = lax.ppermute(slope, "row", swap)
    half = call(gradient_kernel, [vmem] * 4, held(HALF, F))(
        mine, others, slope, other_slope
    )

    same_core = [[chip * 2 + c for chip in range(CHIPS)] for c in range(2)]
    shape = (CHIPS, HALF // CHIPS, F)
    piece = added(exchange(half.reshape(shape), "row", same_core))
    piece = added(exchange(jnp.broadcast_to(piece, shape), "col"))
    half = exchange(jnp.broadcast_to(piece.astype(BF16), shape), "row", same_core)
    half = half.reshape(HALF, F)
    other = lax.ppermute(half, "row", swap)
    first = jnp.where(core == 0, half, other).astype(F32)
    second = jnp.where(core == 0, other, half).astype(F32)
    return activations, jnp.concatenate([first, second])


def solution(mesh):
    placed = (
        P(("row", "col"), None),
        P(("row", "col")),
        P(),
        P("row", "col", None, None, None),
        P("row", "col", None),
        P("row", "col", None),
        P("row", "col"),
        P("row", None),
    )
    return jax.shard_map(
        shards,
        mesh=mesh,
        in_specs=placed,
        out_specs=(P(("row", "col"), None), P()),
        check_vma=False,
    )
```

```python
import jax
import jax.numpy as jnp
from jax import lax
from jax.experimental import pallas as pl
from jax.experimental.pallas import tpu as pltpu
from jax.sharding import PartitionSpec as P

N_ROW = 16
N_COL = 8
TILE = 128
SLOTS = 512
F = 512
PER_PEER = 4
HALF = 256
CHIPS = 8
BLOCKS = 7
SLOT_CAP = 192
ROW_TILES = 32
GROUP_BITS = 2
GROUP = 1 << GROUP_BITS
PLAN = SLOT_CAP + ROW_TILES * (GROUP - 1)
UNROLL_BITS = 3
UNROLL = 1 << UNROLL_BITS
BF16 = jnp.bfloat16
F32 = jnp.float32


def params(limit=16):
    return pltpu.CompilerParams(vmem_limit_bytes=limit * 1024 * 1024)


def selection(position, rows, columns):
    wanted = lax.broadcasted_iota(jnp.int32, (rows, columns), 0)
    return jnp.where(position == wanted, 1.0, 0.0).astype(BF16)


def group_kernel(part_ref, features_hbm, out_ref, features_ref, sem):
    copy = pltpu.make_async_copy(features_hbm, features_ref, sem)
    copy.start()
    part = part_ref[...]
    devices = N_ROW * N_COL
    before = jnp.where(
        lax.broadcasted_iota(jnp.int32, (SLOTS, SLOTS), 0)
        < lax.broadcasted_iota(jnp.int32, (SLOTS, SLOTS), 1),
        1.0,
        0.0,
    ).astype(BF16)
    member = jnp.where(
        part == lax.broadcasted_iota(jnp.int32, (devices, SLOTS), 0), 1.0, 0.0
    )
    earlier = jnp.dot(member.astype(BF16), before, preferred_element_type=F32)
    rank = jnp.sum(member * earlier, axis=0, keepdims=True).astype(jnp.int32)
    place = ((part & (N_COL - 1)) * N_ROW + (part >> 3)) * PER_PEER + rank
    pick = selection(place, SLOTS, SLOTS)
    copy.wait()
    for c in range(2):
        wanted = features_ref[:, c * HALF : (c + 1) * HALF]
        picked = jnp.dot(pick, wanted, preferred_element_type=F32).astype(BF16)
        out_ref[c * N_COL : (c + 1) * N_COL] = picked.reshape(N_COL, SLOTS // N_COL, HALF)


def interleave_kernel(arrived_ref, out_ref):
    source = lax.broadcasted_iota(jnp.int32, (1, SLOTS), 1)
    giver, inner = source >> 6, source & 63
    place = (inner >> 2) * (N_COL * PER_PEER) + giver * PER_PEER + (inner & 3)
    pick = selection(place, SLOTS, SLOTS)
    for c in range(2):
        rows = arrived_ref[c * N_COL : (c + 1) * N_COL].reshape(SLOTS, HALF)
        out_ref[c] = jnp.dot(pick, rows, preferred_element_type=F32).astype(BF16)


def pair_kernel(a_ref, b_ref, out_ref):
    out_ref[0] = a_ref[...]
    out_ref[1] = b_ref[...]


def rest_kernel(meta_ref, pair_ref, a_ref, b_ref, passed_hbm, out_ref):
    core = meta_ref[0]

    @pl.when(core == 0)
    def _():
        out_ref[0] = a_ref[...]
        out_ref[1] = b_ref[...]

    @pl.when(core != 0)
    def _():
        out_ref[...] = pair_ref[...]


def plan_kernel(count_ref, rows_ref, cols_ref, plan_ref):
    slot = lax.broadcasted_iota(jnp.int32, (1, SLOT_CAP), 1)
    rows = rows_ref[...]
    live = slot < count_ref[0]
    kinds = lax.broadcasted_iota(jnp.int32, (ROW_TILES, SLOT_CAP), 0)
    member = jnp.where(live & (rows == kinds), 1.0, 0.0)
    before = jnp.where(
        lax.broadcasted_iota(jnp.int32, (SLOT_CAP, SLOT_CAP), 0)
        < lax.broadcasted_iota(jnp.int32, (SLOT_CAP, SLOT_CAP), 1),
        1.0,
        0.0,
    ).astype(BF16)
    earlier = jnp.dot(member.astype(BF16), before, preferred_element_type=F32)
    number = jnp.sum(member, axis=1, keepdims=True).astype(jnp.int32)
    groups = jnp.broadcast_to((number + (GROUP - 1)) >> GROUP_BITS, (ROW_TILES, TILE))
    below = jnp.where(
        lax.broadcasted_iota(jnp.int32, (ROW_TILES, ROW_TILES), 1)
        < lax.broadcasted_iota(jnp.int32, (ROW_TILES, ROW_TILES), 0),
        1.0,
        0.0,
    ).astype(BF16)
    groups = groups.astype(F32)
    start = jnp.dot(below, groups.astype(BF16), preferred_element_type=F32)[:, :1]
    total = jnp.sum(groups, axis=0, keepdims=True)[:, :1]
    place = jnp.sum(member * (GROUP * start + earlier + 1.0), axis=0, keepdims=True) - 1.0
    taken = selection(place.astype(jnp.int32), PLAN, SLOT_CAP)
    line = lax.broadcasted_iota(jnp.int32, (8, SLOT_CAP), 0)
    values = jnp.where(line == 0, slot - SLOT_CAP, jnp.where(line == 1, cols_ref[...], rows))
    found = lax.dot_general(
        values.astype(F32).astype(BF16),
        taken,
        (((1,), (1,)), ((), ())),
        preferred_element_type=F32,
    )
    line = lax.broadcasted_iota(jnp.int32, (8, PLAN), 0)
    found = jnp.where(line == 0, found + SLOT_CAP, jnp.where(line == 3, total, found))
    plan_ref[...] = found.astype(jnp.int32)


def start_tiles(part, core, own_hbm, other_hbm, out, sem):
    out[SLOT_CAP] = jnp.zeros((TILE, TILE), BF16)
    for mine, hbm in ((True, own_hbm), (False, other_hbm)):

        @pl.when((core == part) == mine)
        def _():
            pltpu.make_async_copy(hbm, out.at[pl.ds(0, SLOT_CAP)], sem).start()

    return pltpu.make_async_copy(own_hbm, out.at[pl.ds(0, SLOT_CAP)], sem)


def stage_kernel(meta_ref, own_hbm, other_hbm, out_ref, sem):
    start_tiles(1, meta_ref[0], own_hbm, other_hbm, out_ref, sem).wait()


def add_tiles(plan_ref, tiles, source, total):
    total[...] = jnp.zeros_like(total)

    def product(g):
        left, right = [], []
        for e in range(GROUP):
            u = plan_ref[1, g * GROUP + e]
            left.append(tiles[plan_ref[0, g * GROUP + e]])
            right.append(source[pl.ds((u & 3) * 2, 2), :, u >> 2].reshape(TILE, HALF))
        return jnp.dot(
            jnp.concatenate(left, axis=1),
            jnp.concatenate(right, axis=0),
            preferred_element_type=F32,
        )

    def some_groups(h, carry):
        found = [
            (plan_ref[2, (h * UNROLL + k) * GROUP], product(h * UNROLL + k))
            for k in range(UNROLL)
        ]
        for place, value in found:
            total[place] += value
        return carry

    lax.fori_loop(0, (plan_ref[3, 0] + UNROLL - 1) >> UNROLL_BITS, some_groups, 0)


def narrow_block(total, yh, x):
    rows = total[pl.ds((yh * 4 + x) * 4, 4)].astype(BF16)
    return rows.reshape(SLOTS, HALF)


def tiles_y_kernel(meta_ref, plan_ref, tiles, own_hbm, other_hbm, *refs):
    blocks, (keep_ref, send_ref, source, next_tiles) = refs[:BLOCKS], refs[BLOCKS:-3]
    total, sems, tiles_sem = refs[-3:]
    core, yh = meta_ref[0], meta_ref[2]

    own, r1, r2, r3, s1, s3, s2 = blocks
    shared = [(own, 0), (r1, 0), (s1, 0), (s1, 1), (s3, 0), (s3, 1)]

    def fetch(block, k):
        return pltpu.make_async_copy(
            block[0].at[block[1]], source.at[meta_ref[4 + k]], sems.at[k]
        )

    for k, block in enumerate(shared):
        fetch(block, k).start()
    for c, rest in enumerate((((r2, 0), (r3, 0)), ((s2, 0), (s2, 1)))):

        @pl.when(core == c)
        def _():
            for k, block in enumerate(rest):
                fetch(block, len(shared) + k).start()

    for k in range(CHIPS):
        fetch(shared[0], k).wait()
    coming = start_tiles(0, core, own_hbm, other_hbm, next_tiles, tiles_sem)
    add_tiles(plan_ref, tiles, source, total)
    for out, to in ((send_ref, 1 - yh), (keep_ref, yh)):
        for x in range(4):
            out[x] = narrow_block(total, to, x)
    coming.wait()


def tiles_x_kernel(meta_ref, plan_ref, tiles, source, *refs):
    outs, total = refs[:4], refs[4]
    x = meta_ref[1]
    add_tiles(plan_ref, tiles, source, total)
    for k, out in enumerate(outs):
        for yh in range(2):
            out[yh] = narrow_block(total, yh, (x + k) & 3)


def x_summed_kernel(meta_ref, own_ref, a_ref, b_ref, c_ref, keep_ref, send_ref):
    yh = meta_ref[2]

    def summed(k):
        pair = own_ref[k].astype(F32) + a_ref[k].astype(F32)
        return pair + (b_ref[k].astype(F32) + c_ref[k].astype(F32))

    keep_ref[...] = summed(yh)
    send_ref[...] = summed(1 - yh).astype(BF16)


def y_summed_kernel(meta_ref, own_ref, got_ref, keep_ref, a_ref, b_ref, c_ref):
    x = meta_ref[1]

    def summed(k):
        return own_ref[k].astype(F32) + got_ref[k].astype(F32)

    keep_ref[...] = summed(x)
    for k, out in ((1, a_ref), (2, b_ref), (3, c_ref)):
        out[...] = summed((x + k) & 3).astype(BF16)


def sums_kernel(meta_ref, keep0, got0, keep1, a_ref, b_ref, c_ref, mine_ref, send_ref):
    core = meta_ref[0]
    first = keep0[...] + got0[...].astype(F32)
    second = keep1[...] + a_ref[...].astype(F32)
    second = second + (b_ref[...].astype(F32) + c_ref[...].astype(F32))
    mine_ref[...] = jnp.where(core == 0, first, second)
    send_ref[...] = jnp.where(core == 0, second, first)


def two_parts(value):
    high = value.astype(BF16)
    return high, (value - high.astype(F32)).astype(BF16)


def layer_kernel(meta_ref, mine_ref, got_ref, weight_ref, cotangent_ref, act_ref, slope_ref):
    core = meta_ref[0]
    pre = jnp.zeros((SLOTS, F), F32)
    for half, mixed in ((core, mine_ref[...]), (1 - core, got_ref[...])):
        weight = weight_ref[pl.ds(pl.multiple_of(half * HALF, HALF), HALF), :]
        for piece in two_parts(mixed):
            pre = pre + jnp.dot(piece, weight, preferred_element_type=F32)
    sigmoid = jax.nn.sigmoid(pre)
    act_ref[...] = (pre * sigmoid).astype(BF16)
    slope_ref[...] = (
        cotangent_ref[...].astype(F32) * (sigmoid * (1.0 + pre * (1.0 - sigmoid)))
    ).astype(BF16)


def gradient_kernel(mine_ref, other_ref, slope_ref, other_slope_ref, grad_ref):
    contract = (((0,), (0,)), ((), ()))
    grad = jnp.zeros((HALF, F), F32)
    for mixed, slope in ((mine_ref, slope_ref), (other_ref, other_slope_ref)):
        for piece in two_parts(mixed[...]):
            grad = grad + lax.dot_general(
                piece, slope[...], contract, preferred_element_type=F32
            )
    grad_ref[...] = (grad * (1.0 / 256.0)).astype(BF16)


def row_moves(move):
    pairs = []
    for yl in range(2):
        for z in range(4):
            for c in range(2):
                to = move(yl, z, c)
                if to is not None:
                    a, b, d = to
                    pairs.append(((yl * 4 + z) * 2 + c, (a * 4 + b) * 2 + d))
    return pairs


def x_moves(k):
    return [(yh * 4 + x, yh * 4 + (x + k) % 4) for yh in range(2) for x in range(4)]


def y_moves():
    return [(yh * 4 + x, (1 - yh) * 4 + x) for yh in range(2) for x in range(4)]


def exchange(parts, axis, groups=None):
    return lax.all_to_all(
        parts, axis, split_axis=0, concat_axis=0, axis_index_groups=groups, tiled=True
    )


def added(parts):
    parts = parts.astype(F32)
    a = (parts[0] + parts[1]) + (parts[2] + parts[3])
    return a + ((parts[4] + parts[5]) + (parts[6] + parts[7]))


def call(kernel, in_specs, outs, scratch=(), limit=16):
    made = pl.pallas_call(
        kernel,
        in_specs=in_specs,
        out_specs=jax.tree.map(lambda _: pl.BlockSpec(memory_space=pltpu.VMEM), outs),
        out_shape=outs,
        scratch_shapes=list(scratch),
        compiler_params=params(limit),
    )

    def run(*operands):
        held = [
            pltpu.with_memory_space_constraint(o, spec.memory_space)
            if spec.memory_space in (pltpu.VMEM, pltpu.MemorySpace.HBM)
            else o
            for spec, o in zip(in_specs, operands)
        ]
        return made(*held)

    return run


def array(*shape, dtype=BF16):
    return jax.ShapeDtypeStruct(shape, dtype)


def held(*shape, dtype=BF16):
    return pltpu.VMEM(shape, dtype)


def after(value, *others):
    return lax.optimization_barrier((value, *others))[0]


def shards(
    features, partition_of, weight, tile_values, tile_rows, tile_cols, tile_count, out_cotangent
):
    row = lax.axis_index("row")
    col = lax.axis_index("col")
    core, z, yl = row % 2, (row // 2) % 4, row // 8
    x, yh = col % 4, col // 4
    vmem = pl.BlockSpec(memory_space=pltpu.VMEM)
    smem = pl.BlockSpec(memory_space=pltpu.SMEM)
    hbm = pl.BlockSpec(memory_space=pl.ANY)
    pinned = pl.BlockSpec(memory_space=pltpu.MemorySpace.HBM)

    here, there = yl * 4, (1 - yl) * 4
    near = [here + (z - k) % 4 for k in range(4)]
    far = [there + (z - k) % 4 for k in range(4)]
    first = core == 0
    places = [
        near[0],
        jnp.where(first, near[1], far[0]),
        jnp.where(first, far[0], near[1]),
        far[1],
        jnp.where(first, far[3], near[3]),
        jnp.where(first, far[2], far[3]),
        jnp.where(first, near[3], near[2]),
        jnp.where(first, near[2], far[2]),
    ]
    meta = jnp.stack([core, x, yh, z] + places).astype(jnp.int32)

    swap = row_moves(lambda yl, z, c: (yl, z, 1 - c))
    tiles = tile_values.reshape(-1, TILE, TILE)
    part = partition_of.reshape(1, SLOTS)
    plan = call(plan_kernel, [smem, vmem, vmem], array(8, PLAN, dtype=jnp.int32))(
        tile_count.reshape(1), tile_rows.reshape(1, -1), tile_cols.reshape(1, -1)
    )
    other_plan = lax.ppermute(plan, "row", swap)
    plans = [jnp.where(core == c, plan, other_plan) for c in range(2)]
    grouped = call(
        group_kernel,
        [vmem, pinned],
        held(2 * N_COL, SLOTS // N_COL, HALF),
        [pltpu.VMEM((SLOTS, F), BF16), pltpu.SemaphoreType.DMA],
    )(part, features)
    other_tiles = lax.ppermute(after(tiles, grouped), "row", swap)
    near_chips = [[k * 2 * N_COL + m for m in range(2 * N_COL)] for k in range(CHIPS)]
    arrived = exchange(grouped, ("row", "col"), near_chips)
    own = call(interleave_kernel, [vmem], array(2, SLOTS, HALF))(arrived)
    own = after(own, other_tiles, other_plan)

    staged = held(SLOT_CAP + 1, TILE, TILE)
    tiles1 = call(stage_kernel, [smem, pinned, pinned], staged, [pltpu.SemaphoreType.DMA])(
        meta, tiles, after(other_tiles, own)
    )

    def hop(block, *moves):
        def move(yl, z, c):
            if moves[c] is None:
                return None
            return (yl + moves[c][0]) % 2, (z + moves[c][1]) % 4, c

        return lax.ppermute(block, "row", row_moves(move))

    r1 = hop(own, (0, 1), (1, 0))
    r2 = hop(own, (0, 3), None)
    r3 = hop(r2, (0, 3), None)
    both = held(2, 2, SLOTS, HALF)
    pair = call(pair_kernel, [vmem] * 2, both)(own, r1)
    s1 = hop(pair, (1, 0), (0, 1))
    s2 = hop(s1, None, (0, 1))
    rest = call(rest_kernel, [smem] + [vmem] * 3 + [pinned], both)(meta, pair, r2, r3, s1)
    s3 = hop(rest, (1, 0), (0, 3))
    shape = (N_ROW, N_COL * PER_PEER, HALF)
    blocks = [b.reshape(1, 2, *shape) for b in (own, r1, r2, r3)]
    blocks += [b.reshape(2, 2, *shape) for b in (s1, s3, s2)]

    total = pltpu.VMEM((ROW_TILES, TILE, HALF), F32)
    source = held(CHIPS, 2, N_ROW, N_COL * PER_PEER, HALF)
    keep1, send1, source, tiles0 = call(
        tiles_y_kernel,
        [smem, smem, vmem, pinned, pinned] + [pinned] * BLOCKS,
        [held(4, SLOTS, HALF), held(4, SLOTS, HALF), source, staged],
        [total, pltpu.SemaphoreType.DMA((CHIPS,)), pltpu.SemaphoreType.DMA],
    )(meta, plans[1], tiles1, tiles, other_tiles, *blocks)
    row0 = call(
        tiles_x_kernel,
        [smem, smem, vmem, vmem],
        [held(2, SLOTS, HALF)] * 4,
        [total],
    )(meta, plans[0], tiles0, source)
    got0 = [lax.ppermute(row0[k], "col", x_moves(k)) for k in (1, 3, 2)]
    got1 = lax.ppermute(send1, "col", y_moves())
    wide, narrow = held(SLOTS, HALF, dtype=F32), held(SLOTS, HALF)
    keep1, *send1 = call(y_summed_kernel, [smem] + [vmem] * 2, [wide] + [narrow] * 3)(
        meta, keep1, got1
    )
    got1 = [lax.ppermute(send1[k - 1], "col", x_moves(k)) for k in (1, 3, 2)]
    keep0, send0 = call(x_summed_kernel, [smem] + [vmem] * 4, [wide, narrow])(
        meta, after(row0[0], got1[0]), *got0
    )
    got0 = lax.ppermute(send0, "col", y_moves())
    mine, others = call(sums_kernel, [smem] + [vmem] * 6, [wide] * 2)(
        meta, keep0, got0, keep1, *got1
    )
    theirs = lax.ppermute(others, "row", swap)
    cotangent = lax.dynamic_slice_in_dim(out_cotangent, col * SLOTS, SLOTS, 0)
    activations, slope = call(
        layer_kernel, [smem] + [vmem] * 4, [array(SLOTS, F), held(SLOTS, F)]
    )(
        meta, mine, theirs, weight, cotangent
    )
    other_slope = lax.ppermute(slope, "row", swap)
    half = call(gradient_kernel, [vmem] * 4, held(HALF, F))(
        mine, others, slope, other_slope
    )

    same_core = [[chip * 2 + c for chip in range(CHIPS)] for c in range(2)]
    shape = (CHIPS, HALF // CHIPS, F)
    piece = added(exchange(half.reshape(shape), "row", same_core))
    piece = added(exchange(jnp.broadcast_to(piece, shape), "col"))
    half = exchange(jnp.broadcast_to(piece.astype(BF16), shape), "row", same_core)
    half = half.reshape(HALF, F)
    other = lax.ppermute(half, "row", swap)
    first = jnp.where(core == 0, half, other).astype(F32)
    second = jnp.where(core == 0, other, half).astype(F32)
    return activations, jnp.concatenate([first, second])


def solution(mesh):
    placed = (
        P(("row", "col"), None),
        P(("row", "col")),
        P(),
        P("row", "col", None, None, None),
        P("row", "col", None),
        P("row", "col", None),
        P("row", "col"),
        P("row", None),
    )
    return jax.shard_map(
        shards,
        mesh=mesh,
        in_specs=placed,
        out_specs=(P(("row", "col"), None), P()),
        check_vma=False,
    )
```

```python
import jax
import jax.numpy as jnp
from jax import lax
from jax.experimental import pallas as pl
from jax.experimental.pallas import tpu as pltpu
from jax.sharding import PartitionSpec as P

N_ROW = 16
N_COL = 8
TILE = 128
SLOTS = 512
F = 512
PER_PEER = 4
HALF = 256
CHIPS = 8
SHARED = 4
BLOCKS = 2 * CHIPS - SHARED
SLOT_CAP = 192
ROW_TILES = 32
GROUP_BITS = 2
GROUP = 1 << GROUP_BITS
PLAN = SLOT_CAP + ROW_TILES * (GROUP - 1)
UNROLL_BITS = 3
UNROLL = 1 << UNROLL_BITS
BF16 = jnp.bfloat16
F32 = jnp.float32


def params(limit=16):
    return pltpu.CompilerParams(vmem_limit_bytes=limit * 1024 * 1024)


def selection(position, rows, columns):
    wanted = lax.broadcasted_iota(jnp.int32, (rows, columns), 0)
    return jnp.where(position == wanted, 1.0, 0.0).astype(BF16)


def group_kernel(part_ref, features_hbm, out_ref, features_ref, sem):
    copy = pltpu.make_async_copy(features_hbm, features_ref, sem)
    copy.start()
    part = part_ref[...]
    devices = N_ROW * N_COL
    before = jnp.where(
        lax.broadcasted_iota(jnp.int32, (SLOTS, SLOTS), 0)
        < lax.broadcasted_iota(jnp.int32, (SLOTS, SLOTS), 1),
        1.0,
        0.0,
    ).astype(BF16)
    member = jnp.where(
        part == lax.broadcasted_iota(jnp.int32, (devices, SLOTS), 0), 1.0, 0.0
    )
    earlier = jnp.dot(member.astype(BF16), before, preferred_element_type=F32)
    rank = jnp.sum(member * earlier, axis=0, keepdims=True).astype(jnp.int32)
    place = ((part & (N_COL - 1)) * N_ROW + (part >> 3)) * PER_PEER + rank
    pick = selection(place, SLOTS, SLOTS)
    copy.wait()
    for c in range(2):
        wanted = features_ref[:, c * HALF : (c + 1) * HALF]
        picked = jnp.dot(pick, wanted, preferred_element_type=F32).astype(BF16)
        out_ref[c * N_COL : (c + 1) * N_COL] = picked.reshape(N_COL, SLOTS // N_COL, HALF)


def interleave_kernel(arrived_ref, out_ref):
    source = lax.broadcasted_iota(jnp.int32, (1, SLOTS), 1)
    giver, inner = source >> 6, source & 63
    place = (inner >> 2) * (N_COL * PER_PEER) + giver * PER_PEER + (inner & 3)
    pick = selection(place, SLOTS, SLOTS)
    for c in range(2):
        rows = arrived_ref[c * N_COL : (c + 1) * N_COL].reshape(SLOTS, HALF)
        out_ref[c] = jnp.dot(pick, rows, preferred_element_type=F32).astype(BF16)


def plan_kernel(count_ref, rows_ref, cols_ref, plan_ref):
    slot = lax.broadcasted_iota(jnp.int32, (1, SLOT_CAP), 1)
    rows = rows_ref[...]
    live = slot < count_ref[0]
    kinds = lax.broadcasted_iota(jnp.int32, (ROW_TILES, SLOT_CAP), 0)
    member = jnp.where(live & (rows == kinds), 1.0, 0.0)
    before = jnp.where(
        lax.broadcasted_iota(jnp.int32, (SLOT_CAP, SLOT_CAP), 0)
        < lax.broadcasted_iota(jnp.int32, (SLOT_CAP, SLOT_CAP), 1),
        1.0,
        0.0,
    ).astype(BF16)
    earlier = jnp.dot(member.astype(BF16), before, preferred_element_type=F32)
    number = jnp.sum(member, axis=1, keepdims=True).astype(jnp.int32)
    groups = jnp.broadcast_to((number + (GROUP - 1)) >> GROUP_BITS, (ROW_TILES, TILE))
    below = jnp.where(
        lax.broadcasted_iota(jnp.int32, (ROW_TILES, ROW_TILES), 1)
        < lax.broadcasted_iota(jnp.int32, (ROW_TILES, ROW_TILES), 0),
        1.0,
        0.0,
    ).astype(BF16)
    groups = groups.astype(F32)
    start = jnp.dot(below, groups.astype(BF16), preferred_element_type=F32)[:, :1]
    total = jnp.sum(groups, axis=0, keepdims=True)[:, :1]
    place = jnp.sum(member * (GROUP * start + earlier + 1.0), axis=0, keepdims=True) - 1.0
    taken = selection(place.astype(jnp.int32), PLAN, SLOT_CAP)
    line = lax.broadcasted_iota(jnp.int32, (8, SLOT_CAP), 0)
    values = jnp.where(line == 0, slot - SLOT_CAP, jnp.where(line == 1, cols_ref[...], rows))
    found = lax.dot_general(
        values.astype(F32).astype(BF16),
        taken,
        (((1,), (1,)), ((), ())),
        preferred_element_type=F32,
    )
    line = lax.broadcasted_iota(jnp.int32, (8, PLAN), 0)
    found = jnp.where(line == 0, found + SLOT_CAP, jnp.where(line == 3, total, found))
    plan_ref[...] = found.astype(jnp.int32)


def start_tiles(part, core, own_hbm, other_hbm, out, sem):
    out[SLOT_CAP] = jnp.zeros((TILE, TILE), BF16)
    for mine, hbm in ((True, own_hbm), (False, other_hbm)):

        @pl.when((core == part) == mine)
        def _():
            pltpu.make_async_copy(hbm, out.at[pl.ds(0, SLOT_CAP)], sem).start()

    return pltpu.make_async_copy(own_hbm, out.at[pl.ds(0, SLOT_CAP)], sem)


def stage_kernel(meta_ref, own_hbm, other_hbm, out_ref, sem):
    start_tiles(1, meta_ref[0], own_hbm, other_hbm, out_ref, sem).wait()


def add_tiles(plan_ref, tiles, source, total):
    total[...] = jnp.zeros_like(total)

    def product(g):
        left, right = [], []
        for e in range(GROUP):
            u = plan_ref[1, g * GROUP + e]
            left.append(tiles[plan_ref[0, g * GROUP + e]])
            right.append(source[pl.ds((u & 3) * 2, 2), :, u >> 2].reshape(TILE, HALF))
        return jnp.dot(
            jnp.concatenate(left, axis=1),
            jnp.concatenate(right, axis=0),
            preferred_element_type=F32,
        )

    def some_groups(h, carry):
        found = [
            (plan_ref[2, (h * UNROLL + k) * GROUP], product(h * UNROLL + k))
            for k in range(UNROLL)
        ]
        for place, value in found:
            total[place] += value
        return carry

    lax.fori_loop(0, (plan_ref[3, 0] + UNROLL - 1) >> UNROLL_BITS, some_groups, 0)


def narrow_block(total, yh, x):
    rows = total[pl.ds((yh * 4 + x) * 4, 4)].astype(BF16)
    return rows.reshape(SLOTS, HALF)


def tiles_y_kernel(meta_ref, plan_ref, tiles, own_hbm, other_hbm, *refs):
    blocks, (keep_ref, send_ref, source, next_tiles) = refs[:BLOCKS], refs[BLOCKS:-3]
    total, sems, tiles_sem = refs[-3:]
    core, yh = meta_ref[0], meta_ref[2]

    def fetch(block, k):
        return pltpu.make_async_copy(block, source.at[meta_ref[4 + k]], sems.at[k])

    for k in range(SHARED):
        fetch(blocks[k], k).start()
    for c in range(2):

        @pl.when(core == c)
        def _():
            for k in range(SHARED, CHIPS):
                fetch(blocks[k + c * (CHIPS - SHARED)], k).start()

    for k in range(CHIPS):
        fetch(blocks[k], k).wait()
    coming = start_tiles(0, core, own_hbm, other_hbm, next_tiles, tiles_sem)
    add_tiles(plan_ref, tiles, source, total)
    for out, to in ((send_ref, 1 - yh), (keep_ref, yh)):
        for x in range(4):
            out[x] = narrow_block(total, to, x)
    coming.wait()


def tiles_x_kernel(meta_ref, plan_ref, tiles, source, *refs):
    outs, total = refs[:4], refs[4]
    x = meta_ref[1]
    add_tiles(plan_ref, tiles, source, total)
    for k, out in enumerate(outs):
        for yh in range(2):
            out[yh] = narrow_block(total, yh, (x + k) & 3)


def x_summed_kernel(meta_ref, own_ref, a_ref, b_ref, c_ref, keep_ref, send_ref):
    yh = meta_ref[2]

    def summed(k):
        pair = own_ref[k].astype(F32) + a_ref[k].astype(F32)
        return pair + (b_ref[k].astype(F32) + c_ref[k].astype(F32))

    keep_ref[...] = summed(yh)
    send_ref[...] = summed(1 - yh).astype(BF16)


def y_summed_kernel(meta_ref, own_ref, got_ref, keep_ref, a_ref, b_ref, c_ref):
    x = meta_ref[1]

    def summed(k):
        return own_ref[k].astype(F32) + got_ref[k].astype(F32)

    keep_ref[...] = summed(x)
    for k, out in ((1, a_ref), (2, b_ref), (3, c_ref)):
        out[...] = summed((x + k) & 3).astype(BF16)


def sums_kernel(meta_ref, keep0, got0, keep1, a_ref, b_ref, c_ref, mine_ref, send_ref):
    core = meta_ref[0]
    first = keep0[...] + got0[...].astype(F32)
    second = keep1[...] + a_ref[...].astype(F32)
    second = second + (b_ref[...].astype(F32) + c_ref[...].astype(F32))
    mine_ref[...] = jnp.where(core == 0, first, second)
    send_ref[...] = jnp.where(core == 0, second, first)


def two_parts(value):
    high = value.astype(BF16)
    return high, (value - high.astype(F32)).astype(BF16)


def layer_kernel(meta_ref, mine_ref, got_ref, weight_ref, cotangent_ref, act_ref, slope_ref):
    core = meta_ref[0]
    pre = jnp.zeros((SLOTS, F), F32)
    for half, mixed in ((core, mine_ref[...]), (1 - core, got_ref[...])):
        weight = weight_ref[pl.ds(pl.multiple_of(half * HALF, HALF), HALF), :]
        for piece in two_parts(mixed):
            pre = pre + jnp.dot(piece, weight, preferred_element_type=F32)
    sigmoid = jax.nn.sigmoid(pre)
    act_ref[...] = (pre * sigmoid).astype(BF16)
    slope_ref[...] = (
        cotangent_ref[...].astype(F32) * (sigmoid * (1.0 + pre * (1.0 - sigmoid)))
    ).astype(BF16)


def gradient_kernel(mine_ref, other_ref, slope_ref, other_slope_ref, grad_ref):
    contract = (((0,), (0,)), ((), ()))
    grad = jnp.zeros((HALF, F), F32)
    for mixed, slope in ((mine_ref, slope_ref), (other_ref, other_slope_ref)):
        for piece in two_parts(mixed[...]):
            grad = grad + lax.dot_general(
                piece, slope[...], contract, preferred_element_type=F32
            )
    grad_ref[...] = (grad * (1.0 / 256.0)).astype(BF16)


def row_moves(move):
    pairs = []
    for yl in range(2):
        for z in range(4):
            for c in range(2):
                to = move(yl, z, c)
                if to is not None:
                    a, b, d = to
                    pairs.append(((yl * 4 + z) * 2 + c, (a * 4 + b) * 2 + d))
    return pairs


def x_moves(k):
    return [(yh * 4 + x, yh * 4 + (x + k) % 4) for yh in range(2) for x in range(4)]


def y_moves():
    return [(yh * 4 + x, (1 - yh) * 4 + x) for yh in range(2) for x in range(4)]


def exchange(parts, axis, groups=None):
    return lax.all_to_all(
        parts, axis, split_axis=0, concat_axis=0, axis_index_groups=groups, tiled=True
    )


def added(parts):
    parts = parts.astype(F32)
    a = (parts[0] + parts[1]) + (parts[2] + parts[3])
    return a + ((parts[4] + parts[5]) + (parts[6] + parts[7]))


def call(kernel, in_specs, outs, scratch=(), limit=16):
    made = pl.pallas_call(
        kernel,
        in_specs=in_specs,
        out_specs=jax.tree.map(lambda _: pl.BlockSpec(memory_space=pltpu.VMEM), outs),
        out_shape=outs,
        scratch_shapes=list(scratch),
        compiler_params=params(limit),
    )

    def run(*operands):
        held = [
            pltpu.with_memory_space_constraint(o, spec.memory_space)
            if spec.memory_space in (pltpu.VMEM, pltpu.MemorySpace.HBM)
            else o
            for spec, o in zip(in_specs, operands)
        ]
        return made(*held)

    return run


def array(*shape, dtype=BF16):
    return jax.ShapeDtypeStruct(shape, dtype)


def held(*shape, dtype=BF16):
    return pltpu.VMEM(shape, dtype)


def after(value, *others):
    return lax.optimization_barrier((value, *others))[0]


def shards(
    features, partition_of, weight, tile_values, tile_rows, tile_cols, tile_count, out_cotangent
):
    row = lax.axis_index("row")
    col = lax.axis_index("col")
    core, z, yl = row % 2, (row // 2) % 4, row // 8
    x, yh = col % 4, col // 4
    vmem = pl.BlockSpec(memory_space=pltpu.VMEM)
    smem = pl.BlockSpec(memory_space=pltpu.SMEM)
    hbm = pl.BlockSpec(memory_space=pl.ANY)
    pinned = pl.BlockSpec(memory_space=pltpu.MemorySpace.HBM)

    here, there = yl * 4, (1 - yl) * 4
    near = [here + (z - k) % 4 for k in range(4)]
    far = [there + (z - k) % 4 for k in range(4)]
    first = core == 0
    places = [
        near[0],
        jnp.where(first, near[1], far[0]),
        jnp.where(first, far[0], near[1]),
        far[1],
        jnp.where(first, near[3], far[3]),
        jnp.where(first, near[2], near[3]),
        jnp.where(first, far[3], near[2]),
        far[2],
    ]
    meta = jnp.stack([core, x, yh, z] + places).astype(jnp.int32)

    swap = row_moves(lambda yl, z, c: (yl, z, 1 - c))
    tiles = tile_values.reshape(-1, TILE, TILE)
    part = partition_of.reshape(1, SLOTS)
    plan = call(plan_kernel, [smem, vmem, vmem], array(8, PLAN, dtype=jnp.int32))(
        tile_count.reshape(1), tile_rows.reshape(1, -1), tile_cols.reshape(1, -1)
    )
    other_plan = lax.ppermute(plan, "row", swap)
    plans = [jnp.where(core == c, plan, other_plan) for c in range(2)]
    grouped = call(
        group_kernel,
        [vmem, pinned],
        held(2 * N_COL, SLOTS // N_COL, HALF),
        [pltpu.VMEM((SLOTS, F), BF16), pltpu.SemaphoreType.DMA],
    )(part, features)
    other_tiles = lax.ppermute(after(tiles, grouped), "row", swap)
    near_chips = [[k * 2 * N_COL + m for m in range(2 * N_COL)] for k in range(CHIPS)]
    arrived = exchange(grouped, ("row", "col"), near_chips)
    own = call(interleave_kernel, [vmem], array(2, SLOTS, HALF))(arrived)
    own = after(own, other_tiles, other_plan)

    staged = held(SLOT_CAP + 1, TILE, TILE)
    tiles1 = call(stage_kernel, [smem, pinned, pinned], staged, [pltpu.SemaphoreType.DMA])(
        meta, tiles, after(other_tiles, own)
    )

    def hop(block, *moves):
        def move(yl, z, c):
            if moves[c] is None:
                return None
            return (yl + moves[c][0]) % 2, (z + moves[c][1]) % 4, c

        return lax.ppermute(block, "row", row_moves(move))

    r1 = hop(own, (0, 1), (1, 0))
    r2 = hop(own, (0, 3), None)
    r3 = hop(own, (0, 2), None)
    r4 = hop(own, (1, 0), (0, 1))
    s1 = hop(r1, (1, 0), (0, 1))
    s2 = hop(r2, (1, 0), None)
    s3 = hop(r3, (1, 0), None)
    later = after(own, r1)
    t1 = hop(r1, None, (0, 3))
    t2 = hop(later, None, (0, 3))
    t3 = hop(later, None, (0, 2))
    t4 = hop(s1, None, (0, 1))
    blocks = [
        b.reshape(2, N_ROW, N_COL * PER_PEER, HALF)
        for b in (own, r1, r4, s1, r2, r3, s2, s3, t1, t2, t3, t4)
    ]

    total = pltpu.VMEM((ROW_TILES, TILE, HALF), F32)
    source = held(CHIPS, 2, N_ROW, N_COL * PER_PEER, HALF)
    keep1, send1, source, tiles0 = call(
        tiles_y_kernel,
        [smem, smem, vmem, pinned, pinned] + [hbm] * BLOCKS,
        [held(4, SLOTS, HALF), held(4, SLOTS, HALF), source, staged],
        [total, pltpu.SemaphoreType.DMA((CHIPS,)), pltpu.SemaphoreType.DMA],
    )(meta, plans[1], tiles1, tiles, other_tiles, *blocks)
    row0 = call(
        tiles_x_kernel,
        [smem, smem, vmem, vmem],
        [held(2, SLOTS, HALF)] * 4,
        [total],
    )(meta, plans[0], tiles0, source)
    got0 = [lax.ppermute(row0[k], "col", x_moves(k)) for k in (1, 3, 2)]
    got1 = lax.ppermute(send1, "col", y_moves())
    wide, narrow = held(SLOTS, HALF, dtype=F32), held(SLOTS, HALF)
    keep1, *send1 = call(y_summed_kernel, [smem] + [vmem] * 2, [wide] + [narrow] * 3)(
        meta, keep1, got1
    )
    got1 = [lax.ppermute(send1[k - 1], "col", x_moves(k)) for k in (1, 3, 2)]
    keep0, send0 = call(x_summed_kernel, [smem] + [vmem] * 4, [wide, narrow])(
        meta, after(row0[0], got1[0]), *got0
    )
    got0 = lax.ppermute(send0, "col", y_moves())
    mine, others = call(sums_kernel, [smem] + [vmem] * 6, [wide] * 2)(
        meta, keep0, got0, keep1, *got1
    )
    theirs = lax.ppermute(others, "row", swap)
    cotangent = lax.dynamic_slice_in_dim(out_cotangent, col * SLOTS, SLOTS, 0)
    activations, slope = call(
        layer_kernel, [smem] + [vmem] * 4, [array(SLOTS, F), held(SLOTS, F)]
    )(
        meta, mine, theirs, weight, cotangent
    )
    other_slope = lax.ppermute(slope, "row", swap)
    half = call(gradient_kernel, [vmem] * 4, held(HALF, F))(
        mine, others, slope, other_slope
    )

    same_core = [[chip * 2 + c for chip in range(CHIPS)] for c in range(2)]
    shape = (CHIPS, HALF // CHIPS, F)
    piece = added(exchange(half.reshape(shape), "row", same_core))
    piece = added(exchange(jnp.broadcast_to(piece, shape), "col"))
    half = exchange(jnp.broadcast_to(piece.astype(BF16), shape), "row", same_core)
    half = half.reshape(HALF, F)
    other = lax.ppermute(half, "row", swap)
    first = jnp.where(core == 0, half, other).astype(F32)
    second = jnp.where(core == 0, other, half).astype(F32)
    return activations, jnp.concatenate([first, second])


def solution(mesh):
    placed = (
        P(("row", "col"), None),
        P(("row", "col")),
        P(),
        P("row", "col", None, None, None),
        P("row", "col", None),
        P("row", "col", None),
        P("row", "col"),
        P("row", None),
    )
    return jax.shard_map(
        shards,
        mesh=mesh,
        in_specs=placed,
        out_specs=(P(("row", "col"), None), P()),
        check_vma=False,
    )
```

```python
import jax
import jax.numpy as jnp
from jax import lax
from jax.experimental import pallas as pl
from jax.experimental.pallas import tpu as pltpu
from jax.sharding import PartitionSpec as P

N_ROW = 16
N_COL = 8
TILE = 128
SLOTS = 512
F = 512
PER_PEER = 4
HALF = 256
CHIPS = 8
SHARED = 4
BLOCKS = 2 * CHIPS - SHARED
SLOT_CAP = 192
ROW_TILES = 32
GROUP_BITS = 2
GROUP = 1 << GROUP_BITS
PLAN = SLOT_CAP + ROW_TILES * (GROUP - 1)
UNROLL_BITS = 3
UNROLL = 1 << UNROLL_BITS
BF16 = jnp.bfloat16
F32 = jnp.float32


def params(limit=16):
    return pltpu.CompilerParams(vmem_limit_bytes=limit * 1024 * 1024)


def selection(position, rows, columns):
    wanted = lax.broadcasted_iota(jnp.int32, (rows, columns), 0)
    return jnp.where(position == wanted, 1.0, 0.0).astype(BF16)


def group_kernel(part_ref, features_hbm, out_ref, features_ref, sem):
    copy = pltpu.make_async_copy(features_hbm, features_ref, sem)
    copy.start()
    part = part_ref[...]
    devices = N_ROW * N_COL
    before = jnp.where(
        lax.broadcasted_iota(jnp.int32, (SLOTS, SLOTS), 0)
        < lax.broadcasted_iota(jnp.int32, (SLOTS, SLOTS), 1),
        1.0,
        0.0,
    ).astype(BF16)
    member = jnp.where(
        part == lax.broadcasted_iota(jnp.int32, (devices, SLOTS), 0), 1.0, 0.0
    )
    earlier = jnp.dot(member.astype(BF16), before, preferred_element_type=F32)
    rank = jnp.sum(member * earlier, axis=0, keepdims=True).astype(jnp.int32)
    place = ((part & (N_COL - 1)) * N_ROW + (part >> 3)) * PER_PEER + rank
    pick = selection(place, SLOTS, SLOTS)
    copy.wait()
    for c in range(2):
        wanted = features_ref[:, c * HALF : (c + 1) * HALF]
        picked = jnp.dot(pick, wanted, preferred_element_type=F32).astype(BF16)
        out_ref[c * N_COL : (c + 1) * N_COL] = picked.reshape(N_COL, SLOTS // N_COL, HALF)


def interleave_kernel(arrived_ref, out_ref):
    source = lax.broadcasted_iota(jnp.int32, (1, SLOTS), 1)
    giver, inner = source >> 6, source & 63
    place = (inner >> 2) * (N_COL * PER_PEER) + giver * PER_PEER + (inner & 3)
    pick = selection(place, SLOTS, SLOTS)
    for c in range(2):
        rows = arrived_ref[c * N_COL : (c + 1) * N_COL].reshape(SLOTS, HALF)
        out_ref[c] = jnp.dot(pick, rows, preferred_element_type=F32).astype(BF16)


def plan_kernel(count_ref, rows_ref, cols_ref, plan_ref):
    slot = lax.broadcasted_iota(jnp.int32, (1, SLOT_CAP), 1)
    rows = rows_ref[...]
    live = slot < count_ref[0]
    kinds = lax.broadcasted_iota(jnp.int32, (ROW_TILES, SLOT_CAP), 0)
    member = jnp.where(live & (rows == kinds), 1.0, 0.0)
    before = jnp.where(
        lax.broadcasted_iota(jnp.int32, (SLOT_CAP, SLOT_CAP), 0)
        < lax.broadcasted_iota(jnp.int32, (SLOT_CAP, SLOT_CAP), 1),
        1.0,
        0.0,
    ).astype(BF16)
    earlier = jnp.dot(member.astype(BF16), before, preferred_element_type=F32)
    number = jnp.sum(member, axis=1, keepdims=True).astype(jnp.int32)
    groups = jnp.broadcast_to((number + (GROUP - 1)) >> GROUP_BITS, (ROW_TILES, TILE))
    below = jnp.where(
        lax.broadcasted_iota(jnp.int32, (ROW_TILES, ROW_TILES), 1)
        < lax.broadcasted_iota(jnp.int32, (ROW_TILES, ROW_TILES), 0),
        1.0,
        0.0,
    ).astype(BF16)
    groups = groups.astype(F32)
    start = jnp.dot(below, groups.astype(BF16), preferred_element_type=F32)[:, :1]
    total = jnp.sum(groups, axis=0, keepdims=True)[:, :1]
    place = jnp.sum(member * (GROUP * start + earlier + 1.0), axis=0, keepdims=True) - 1.0
    taken = selection(place.astype(jnp.int32), PLAN, SLOT_CAP)
    line = lax.broadcasted_iota(jnp.int32, (8, SLOT_CAP), 0)
    values = jnp.where(line == 0, slot - SLOT_CAP, jnp.where(line == 1, cols_ref[...], rows))
    found = lax.dot_general(
        values.astype(F32).astype(BF16),
        taken,
        (((1,), (1,)), ((), ())),
        preferred_element_type=F32,
    )
    line = lax.broadcasted_iota(jnp.int32, (8, PLAN), 0)
    found = jnp.where(line == 0, found + SLOT_CAP, jnp.where(line == 3, total, found))
    plan_ref[...] = found.astype(jnp.int32)


def start_tiles(part, core, own_hbm, other_hbm, out, sem):
    out[SLOT_CAP] = jnp.zeros((TILE, TILE), BF16)
    for mine, hbm in ((True, own_hbm), (False, other_hbm)):

        @pl.when((core == part) == mine)
        def _():
            pltpu.make_async_copy(hbm, out.at[pl.ds(0, SLOT_CAP)], sem).start()

    return pltpu.make_async_copy(own_hbm, out.at[pl.ds(0, SLOT_CAP)], sem)


def stage_kernel(meta_ref, own_hbm, other_hbm, out_ref, sem):
    start_tiles(1, meta_ref[0], own_hbm, other_hbm, out_ref, sem).wait()


def add_tiles(plan_ref, tiles, source, total):
    total[...] = jnp.zeros_like(total)

    def product(g):
        left, right = [], []
        for e in range(GROUP):
            u = plan_ref[1, g * GROUP + e]
            left.append(tiles[plan_ref[0, g * GROUP + e]])
            right.append(source[pl.ds((u & 3) * 2, 2), :, u >> 2].reshape(TILE, HALF))
        return jnp.dot(
            jnp.concatenate(left, axis=1),
            jnp.concatenate(right, axis=0),
            preferred_element_type=F32,
        )

    def some_groups(h, carry):
        found = [
            (plan_ref[2, (h * UNROLL + k) * GROUP], product(h * UNROLL + k))
            for k in range(UNROLL)
        ]
        for place, value in found:
            total[place] += value
        return carry

    lax.fori_loop(0, (plan_ref[3, 0] + UNROLL - 1) >> UNROLL_BITS, some_groups, 0)


def narrow_block(total, yh, x):
    rows = total[pl.ds((yh * 4 + x) * 4, 4)].astype(BF16)
    return rows.reshape(SLOTS, HALF)


def tiles_y_kernel(meta_ref, plan_ref, tiles, own_hbm, other_hbm, *refs):
    blocks, (keep_ref, send_ref, source, next_tiles) = refs[:BLOCKS], refs[BLOCKS:-3]
    total, sems, tiles_sem = refs[-3:]
    core, yh = meta_ref[0], meta_ref[2]

    def fetch(block, k):
        return pltpu.make_async_copy(block, source.at[meta_ref[4 + k]], sems.at[k])

    for k in range(SHARED):
        fetch(blocks[k], k).start()
    for c in range(2):

        @pl.when(core == c)
        def _():
            for k in range(SHARED, CHIPS):
                fetch(blocks[k + c * (CHIPS - SHARED)], k).start()

    for k in range(CHIPS):
        fetch(blocks[k], k).wait()
    coming = start_tiles(0, core, own_hbm, other_hbm, next_tiles, tiles_sem)
    add_tiles(plan_ref, tiles, source, total)
    for out, to in ((send_ref, 1 - yh), (keep_ref, yh)):
        for x in range(4):
            out[x] = narrow_block(total, to, x)
    coming.wait()


def tiles_x_kernel(meta_ref, plan_ref, tiles, source, *refs):
    outs, total = refs[:4], refs[4]
    x = meta_ref[1]
    add_tiles(plan_ref, tiles, source, total)
    for k, out in enumerate(outs):
        for yh in range(2):
            out[yh] = narrow_block(total, yh, (x + k) & 3)


def x_summed_kernel(meta_ref, own_ref, a_ref, b_ref, c_ref, keep_ref, send_ref):
    yh = meta_ref[2]

    def summed(k):
        pair = own_ref[k].astype(F32) + a_ref[k].astype(F32)
        return pair + (b_ref[k].astype(F32) + c_ref[k].astype(F32))

    keep_ref[...] = summed(yh)
    send_ref[...] = summed(1 - yh).astype(BF16)


def y_summed_kernel(meta_ref, own_ref, got_ref, keep_ref, a_ref, b_ref, c_ref):
    x = meta_ref[1]

    def summed(k):
        return own_ref[k].astype(F32) + got_ref[k].astype(F32)

    keep_ref[...] = summed(x)
    for k, out in ((1, a_ref), (2, b_ref), (3, c_ref)):
        out[...] = summed((x + k) & 3).astype(BF16)


def sums_kernel(meta_ref, keep0, got0, keep1, a_ref, b_ref, c_ref, mine_ref, send_ref):
    core = meta_ref[0]
    first = keep0[...] + got0[...].astype(F32)
    second = keep1[...] + a_ref[...].astype(F32)
    second = second + (b_ref[...].astype(F32) + c_ref[...].astype(F32))
    mine_ref[...] = jnp.where(core == 0, first, second)
    send_ref[...] = jnp.where(core == 0, second, first)


def two_parts(value):
    high = value.astype(BF16)
    return high, (value - high.astype(F32)).astype(BF16)


def layer_kernel(meta_ref, mine_ref, got_ref, weight_ref, cotangent_ref, act_ref, slope_ref):
    core = meta_ref[0]
    pre = jnp.zeros((SLOTS, F), F32)
    for half, mixed in ((core, mine_ref[...]), (1 - core, got_ref[...])):
        weight = weight_ref[pl.ds(pl.multiple_of(half * HALF, HALF), HALF), :]
        for piece in two_parts(mixed):
            pre = pre + jnp.dot(piece, weight, preferred_element_type=F32)
    sigmoid = jax.nn.sigmoid(pre)
    act_ref[...] = (pre * sigmoid).astype(BF16)
    slope_ref[...] = (
        cotangent_ref[...].astype(F32) * (sigmoid * (1.0 + pre * (1.0 - sigmoid)))
    ).astype(BF16)


def gradient_kernel(mine_ref, other_ref, slope_ref, other_slope_ref, grad_ref):
    contract = (((0,), (0,)), ((), ()))
    grad = jnp.zeros((HALF, F), F32)
    for mixed, slope in ((mine_ref, slope_ref), (other_ref, other_slope_ref)):
        for piece in two_parts(mixed[...]):
            grad = grad + lax.dot_general(
                piece, slope[...], contract, preferred_element_type=F32
            )
    grad_ref[...] = (grad * (1.0 / 256.0)).astype(BF16)


def row_moves(move):
    pairs = []
    for yl in range(2):
        for z in range(4):
            for c in range(2):
                to = move(yl, z, c)
                if to is not None:
                    a, b, d = to
                    pairs.append(((yl * 4 + z) * 2 + c, (a * 4 + b) * 2 + d))
    return pairs


def x_moves(k):
    return [(yh * 4 + x, yh * 4 + (x + k) % 4) for yh in range(2) for x in range(4)]


def y_moves():
    return [(yh * 4 + x, (1 - yh) * 4 + x) for yh in range(2) for x in range(4)]


def exchange(parts, axis, groups=None):
    return lax.all_to_all(
        parts, axis, split_axis=0, concat_axis=0, axis_index_groups=groups, tiled=True
    )


def added(parts):
    parts = parts.astype(F32)
    a = (parts[0] + parts[1]) + (parts[2] + parts[3])
    return a + ((parts[4] + parts[5]) + (parts[6] + parts[7]))


def call(kernel, in_specs, outs, scratch=(), limit=16):
    made = pl.pallas_call(
        kernel,
        in_specs=in_specs,
        out_specs=jax.tree.map(lambda _: pl.BlockSpec(memory_space=pltpu.VMEM), outs),
        out_shape=outs,
        scratch_shapes=list(scratch),
        compiler_params=params(limit),
    )

    def run(*operands):
        held = [
            pltpu.with_memory_space_constraint(o, spec.memory_space)
            if spec.memory_space in (pltpu.VMEM, pltpu.MemorySpace.HBM)
            else o
            for spec, o in zip(in_specs, operands)
        ]
        return made(*held)

    return run


def array(*shape, dtype=BF16):
    return jax.ShapeDtypeStruct(shape, dtype)


def held(*shape, dtype=BF16):
    return pltpu.VMEM(shape, dtype)


def after(value, *others):
    return lax.optimization_barrier((value, *others))[0]


def shards(
    features, partition_of, weight, tile_values, tile_rows, tile_cols, tile_count, out_cotangent
):
    row = lax.axis_index("row")
    col = lax.axis_index("col")
    core, z, yl = row % 2, (row // 2) % 4, row // 8
    x, yh = col % 4, col // 4
    vmem = pl.BlockSpec(memory_space=pltpu.VMEM)
    smem = pl.BlockSpec(memory_space=pltpu.SMEM)
    hbm = pl.BlockSpec(memory_space=pl.ANY)
    pinned = pl.BlockSpec(memory_space=pltpu.MemorySpace.HBM)

    here, there = yl * 4, (1 - yl) * 4
    near = [here + (z - k) % 4 for k in range(4)]
    far = [there + (z - k) % 4 for k in range(4)]
    first = core == 0
    places = [
        near[0],
        jnp.where(first, near[1], far[0]),
        jnp.where(first, far[0], near[1]),
        far[1],
        jnp.where(first, near[3], far[3]),
        jnp.where(first, near[2], near[3]),
        jnp.where(first, far[3], near[2]),
        far[2],
    ]
    meta = jnp.stack([core, x, yh, z] + places).astype(jnp.int32)

    swap = row_moves(lambda yl, z, c: (yl, z, 1 - c))
    tiles = tile_values.reshape(-1, TILE, TILE)
    part = partition_of.reshape(1, SLOTS)
    plan = call(plan_kernel, [smem, vmem, vmem], array(8, PLAN, dtype=jnp.int32))(
        tile_count.reshape(1), tile_rows.reshape(1, -1), tile_cols.reshape(1, -1)
    )
    other_plan = lax.ppermute(plan, "row", swap)
    plans = [jnp.where(core == c, plan, other_plan) for c in range(2)]
    grouped = call(
        group_kernel,
        [vmem, pinned],
        held(2 * N_COL, SLOTS // N_COL, HALF),
        [pltpu.VMEM((SLOTS, F), BF16), pltpu.SemaphoreType.DMA],
    )(part, features)
    other_tiles = lax.ppermute(after(tiles, grouped), "row", swap)
    near_chips = [[k * 2 * N_COL + m for m in range(2 * N_COL)] for k in range(CHIPS)]
    arrived = exchange(grouped, ("row", "col"), near_chips)
    own = call(interleave_kernel, [vmem], array(2, SLOTS, HALF))(arrived)
    own = after(own, other_tiles, other_plan)

    staged = held(SLOT_CAP + 1, TILE, TILE)
    tiles1 = call(stage_kernel, [smem, pinned, pinned], staged, [pltpu.SemaphoreType.DMA])(
        meta, tiles, after(other_tiles, own)
    )

    def hop(block, *moves):
        def move(yl, z, c):
            if moves[c] is None:
                return None
            return (yl + moves[c][0]) % 2, (z + moves[c][1]) % 4, c

        return lax.ppermute(block, "row", row_moves(move))

    r1 = hop(own, (0, 1), (1, 0))
    r2 = hop(own, (0, 3), None)
    r3 = hop(own, (0, 2), None)
    r4 = hop(own, (1, 0), (0, 1))
    s1 = hop(r1, (1, 0), (0, 1))
    s2 = hop(r2, (1, 0), None)
    s3 = hop(r3, (1, 0), None)
    later = after(own, r1)
    t1 = hop(r1, None, (0, 3))
    t2 = hop(later, None, (0, 3))
    t3 = hop(later, None, (0, 2))
    t4 = hop(r1, None, (0, 2))
    blocks = [
        b.reshape(2, N_ROW, N_COL * PER_PEER, HALF)
        for b in (own, r1, r4, s1, r2, r3, s2, s3, t1, t2, t3, t4)
    ]

    total = pltpu.VMEM((ROW_TILES, TILE, HALF), F32)
    source = held(CHIPS, 2, N_ROW, N_COL * PER_PEER, HALF)
    keep1, send1, source, tiles0 = call(
        tiles_y_kernel,
        [smem, smem, vmem, pinned, pinned] + [hbm] * BLOCKS,
        [held(4, SLOTS, HALF), held(4, SLOTS, HALF), source, staged],
        [total, pltpu.SemaphoreType.DMA((CHIPS,)), pltpu.SemaphoreType.DMA],
    )(meta, plans[1], tiles1, tiles, other_tiles, *blocks)
    row0 = call(
        tiles_x_kernel,
        [smem, smem, vmem, vmem],
        [held(2, SLOTS, HALF)] * 4,
        [total],
    )(meta, plans[0], tiles0, source)
    got0 = [lax.ppermute(row0[k], "col", x_moves(k)) for k in (1, 3, 2)]
    got1 = lax.ppermute(send1, "col", y_moves())
    wide, narrow = held(SLOTS, HALF, dtype=F32), held(SLOTS, HALF)
    keep1, *send1 = call(y_summed_kernel, [smem] + [vmem] * 2, [wide] + [narrow] * 3)(
        meta, keep1, got1
    )
    got1 = [lax.ppermute(send1[k - 1], "col", x_moves(k)) for k in (1, 3, 2)]
    keep0, send0 = call(x_summed_kernel, [smem] + [vmem] * 4, [wide, narrow])(
        meta, after(row0[0], got1[0]), *got0
    )
    got0 = lax.ppermute(send0, "col", y_moves())
    mine, others = call(sums_kernel, [smem] + [vmem] * 6, [wide] * 2)(
        meta, keep0, got0, keep1, *got1
    )
    theirs = lax.ppermute(others, "row", swap)
    cotangent = lax.dynamic_slice_in_dim(out_cotangent, col * SLOTS, SLOTS, 0)
    activations, slope = call(
        layer_kernel, [smem] + [vmem] * 4, [array(SLOTS, F), held(SLOTS, F)]
    )(
        meta, mine, theirs, weight, cotangent
    )
    other_slope = lax.ppermute(slope, "row", swap)
    half = call(gradient_kernel, [vmem] * 4, held(HALF, F))(
        mine, others, slope, other_slope
    )

    same_core = [[chip * 2 + c for chip in range(CHIPS)] for c in range(2)]
    shape = (CHIPS, HALF // CHIPS, F)
    piece = added(exchange(half.reshape(shape), "row", same_core))
    piece = added(exchange(jnp.broadcast_to(piece.astype(BF16), shape), "col"))
    half = exchange(jnp.broadcast_to(piece.astype(BF16), shape), "row", same_core)
    half = half.reshape(HALF, F)
    other = lax.ppermute(half, "row", swap)
    first = jnp.where(core == 0, half, other).astype(F32)
    second = jnp.where(core == 0, other, half).astype(F32)
    return activations, jnp.concatenate([first, second])


def solution(mesh):
    placed = (
        P(("row", "col"), None),
        P(("row", "col")),
        P(),
        P("row", "col", None, None, None),
        P("row", "col", None),
        P("row", "col", None),
        P("row", "col"),
        P("row", None),
    )
    return jax.shard_map(
        shards,
        mesh=mesh,
        in_specs=placed,
        out_specs=(P(("row", "col"), None), P()),
        check_vma=False,
    )
```

```python
import jax
import jax.numpy as jnp
from jax import lax
from jax.experimental import pallas as pl
from jax.experimental.pallas import tpu as pltpu
from jax.sharding import PartitionSpec as P

N_ROW = 16
N_COL = 8
TILE = 128
SLOTS = 512
F = 512
PER_PEER = 4
HALF = 256
CHIPS = 8
SHARED = 4
BLOCKS = 2 * CHIPS - SHARED
SLOT_CAP = 192
ROW_TILES = 32
GROUP_BITS = 2
GROUP = 1 << GROUP_BITS
PLAN = SLOT_CAP + ROW_TILES * (GROUP - 1)
UNROLL_BITS = 3
UNROLL = 1 << UNROLL_BITS
BF16 = jnp.bfloat16
F32 = jnp.float32


def params(limit=16):
    return pltpu.CompilerParams(vmem_limit_bytes=limit * 1024 * 1024)


def selection(position, rows, columns):
    wanted = lax.broadcasted_iota(jnp.int32, (rows, columns), 0)
    return jnp.where(position == wanted, 1.0, 0.0).astype(BF16)


def group_kernel(part_ref, features_hbm, out_ref, features_ref, sem):
    copy = pltpu.make_async_copy(features_hbm, features_ref, sem)
    copy.start()
    part = part_ref[...]
    devices = N_ROW * N_COL
    before = jnp.where(
        lax.broadcasted_iota(jnp.int32, (SLOTS, SLOTS), 0)
        < lax.broadcasted_iota(jnp.int32, (SLOTS, SLOTS), 1),
        1.0,
        0.0,
    ).astype(BF16)
    member = jnp.where(
        part == lax.broadcasted_iota(jnp.int32, (devices, SLOTS), 0), 1.0, 0.0
    )
    earlier = jnp.dot(member.astype(BF16), before, preferred_element_type=F32)
    rank = jnp.sum(member * earlier, axis=0, keepdims=True).astype(jnp.int32)
    place = ((part & (N_COL - 1)) * N_ROW + (part >> 3)) * PER_PEER + rank
    pick = selection(place, SLOTS, SLOTS)
    copy.wait()
    for c in range(2):
        wanted = features_ref[:, c * HALF : (c + 1) * HALF]
        picked = jnp.dot(pick, wanted, preferred_element_type=F32).astype(BF16)
        out_ref[c * N_COL : (c + 1) * N_COL] = picked.reshape(N_COL, SLOTS // N_COL, HALF)


def interleave_kernel(arrived_ref, out_ref):
    source = lax.broadcasted_iota(jnp.int32, (1, SLOTS), 1)
    giver, inner = source >> 6, source & 63
    place = (inner >> 2) * (N_COL * PER_PEER) + giver * PER_PEER + (inner & 3)
    pick = selection(place, SLOTS, SLOTS)
    for c in range(2):
        rows = arrived_ref[c * N_COL : (c + 1) * N_COL].reshape(SLOTS, HALF)
        out_ref[c] = jnp.dot(pick, rows, preferred_element_type=F32).astype(BF16)


def plan_kernel(count_ref, rows_ref, cols_ref, plan_ref):
    slot = lax.broadcasted_iota(jnp.int32, (1, SLOT_CAP), 1)
    rows = rows_ref[...]
    live = slot < count_ref[0]
    kinds = lax.broadcasted_iota(jnp.int32, (ROW_TILES, SLOT_CAP), 0)
    member = jnp.where(live & (rows == kinds), 1.0, 0.0)
    before = jnp.where(
        lax.broadcasted_iota(jnp.int32, (SLOT_CAP, SLOT_CAP), 0)
        < lax.broadcasted_iota(jnp.int32, (SLOT_CAP, SLOT_CAP), 1),
        1.0,
        0.0,
    ).astype(BF16)
    earlier = jnp.dot(member.astype(BF16), before, preferred_element_type=F32)
    number = jnp.sum(member, axis=1, keepdims=True).astype(jnp.int32)
    groups = jnp.broadcast_to((number + (GROUP - 1)) >> GROUP_BITS, (ROW_TILES, TILE))
    below = jnp.where(
        lax.broadcasted_iota(jnp.int32, (ROW_TILES, ROW_TILES), 1)
        < lax.broadcasted_iota(jnp.int32, (ROW_TILES, ROW_TILES), 0),
        1.0,
        0.0,
    ).astype(BF16)
    groups = groups.astype(F32)
    start = jnp.dot(below, groups.astype(BF16), preferred_element_type=F32)[:, :1]
    total = jnp.sum(groups, axis=0, keepdims=True)[:, :1]
    place = jnp.sum(member * (GROUP * start + earlier + 1.0), axis=0, keepdims=True) - 1.0
    taken = selection(place.astype(jnp.int32), PLAN, SLOT_CAP)
    line = lax.broadcasted_iota(jnp.int32, (8, SLOT_CAP), 0)
    values = jnp.where(line == 0, slot - SLOT_CAP, jnp.where(line == 1, cols_ref[...], rows))
    found = lax.dot_general(
        values.astype(F32).astype(BF16),
        taken,
        (((1,), (1,)), ((), ())),
        preferred_element_type=F32,
    )
    line = lax.broadcasted_iota(jnp.int32, (8, PLAN), 0)
    found = jnp.where(line == 0, found + SLOT_CAP, jnp.where(line == 3, total, found))
    plan_ref[...] = found.astype(jnp.int32)


def start_tiles(part, core, own_hbm, other_hbm, out, sem):
    out[SLOT_CAP] = jnp.zeros((TILE, TILE), BF16)
    for mine, hbm in ((True, own_hbm), (False, other_hbm)):

        @pl.when((core == part) == mine)
        def _():
            pltpu.make_async_copy(hbm, out.at[pl.ds(0, SLOT_CAP)], sem).start()

    return pltpu.make_async_copy(own_hbm, out.at[pl.ds(0, SLOT_CAP)], sem)


def stage_kernel(meta_ref, own_hbm, other_hbm, out_ref, sem):
    start_tiles(1, meta_ref[0], own_hbm, other_hbm, out_ref, sem).wait()


def add_tiles(plan_ref, tiles, source, total):
    total[...] = jnp.zeros_like(total)

    def product(g):
        left, right = [], []
        for e in range(GROUP):
            u = plan_ref[1, g * GROUP + e]
            left.append(tiles[plan_ref[0, g * GROUP + e]])
            right.append(source[pl.ds((u & 3) * 2, 2), :, u >> 2].reshape(TILE, HALF))
        return jnp.dot(
            jnp.concatenate(left, axis=1),
            jnp.concatenate(right, axis=0),
            preferred_element_type=F32,
        )

    def some_groups(h, carry):
        found = [
            (plan_ref[2, (h * UNROLL + k) * GROUP], product(h * UNROLL + k))
            for k in range(UNROLL)
        ]
        for place, value in found:
            total[place] += value
        return carry

    lax.fori_loop(0, (plan_ref[3, 0] + UNROLL - 1) >> UNROLL_BITS, some_groups, 0)


def narrow_block(total, yh, x):
    rows = total[pl.ds((yh * 4 + x) * 4, 4)].astype(BF16)
    return rows.reshape(SLOTS, HALF)


def tiles_y_kernel(meta_ref, plan_ref, tiles, own_hbm, other_hbm, *refs):
    blocks, (keep_ref, send_ref, source, next_tiles) = refs[:BLOCKS], refs[BLOCKS:-3]
    total, sems, tiles_sem = refs[-3:]
    core, yh = meta_ref[0], meta_ref[2]

    def fetch(block, k):
        return pltpu.make_async_copy(block, source.at[meta_ref[4 + k]], sems.at[k])

    for k in range(SHARED):
        fetch(blocks[k], k).start()
    for c in range(2):

        @pl.when(core == c)
        def _():
            for k in range(SHARED, CHIPS):
                fetch(blocks[k + c * (CHIPS - SHARED)], k).start()

    for k in range(CHIPS):
        fetch(blocks[k], k).wait()
    coming = start_tiles(0, core, own_hbm, other_hbm, next_tiles, tiles_sem)
    add_tiles(plan_ref, tiles, source, total)
    for out, to in ((send_ref, 1 - yh), (keep_ref, yh)):
        for x in range(4):
            out[x] = narrow_block(total, to, x)
    coming.wait()


def tiles_x_kernel(meta_ref, plan_ref, tiles, source, *refs):
    outs, total = refs[:4], refs[4]
    x = meta_ref[1]
    add_tiles(plan_ref, tiles, source, total)
    for k, out in enumerate(outs):
        for yh in range(2):
            out[yh] = narrow_block(total, yh, (x + k) & 3)


def x_summed_kernel(meta_ref, own_ref, a_ref, b_ref, c_ref, keep_ref, send_ref):
    yh = meta_ref[2]

    def summed(k):
        pair = own_ref[k].astype(F32) + a_ref[k].astype(F32)
        return pair + (b_ref[k].astype(F32) + c_ref[k].astype(F32))

    keep_ref[...] = summed(yh)
    send_ref[...] = summed(1 - yh).astype(BF16)


def y_summed_kernel(meta_ref, own_ref, got_ref, keep_ref, a_ref, b_ref, c_ref):
    x = meta_ref[1]

    def summed(k):
        return own_ref[k].astype(F32) + got_ref[k].astype(F32)

    keep_ref[...] = summed(x)
    for k, out in ((1, a_ref), (2, b_ref), (3, c_ref)):
        out[...] = summed((x + k) & 3).astype(BF16)


def sums_kernel(meta_ref, keep0, got0, keep1, a_ref, b_ref, c_ref, mine_ref, send_ref):
    core = meta_ref[0]
    first = keep0[...] + got0[...].astype(F32)
    second = keep1[...] + a_ref[...].astype(F32)
    second = second + (b_ref[...].astype(F32) + c_ref[...].astype(F32))
    mine_ref[...] = jnp.where(core == 0, first, second)
    send_ref[...] = jnp.where(core == 0, second, first)


def two_parts(value):
    high = value.astype(BF16)
    return high, (value - high.astype(F32)).astype(BF16)


def half_product(pre, mixed, weight_ref, half):
    weight = weight_ref[pl.ds(pl.multiple_of(half * HALF, HALF), HALF), :]
    for piece in two_parts(mixed):
        pre = pre + jnp.dot(piece, weight, preferred_element_type=F32)
    return pre


def half_layer_kernel(meta_ref, mine_ref, weight_ref, pre_ref):
    start = jnp.zeros((SLOTS, F), F32)
    pre_ref[...] = half_product(start, mine_ref[...], weight_ref, meta_ref[0])


def layer_kernel(meta_ref, pre_ref, got_ref, weight_ref, cotangent_ref, act_ref, slope_ref):
    pre = half_product(pre_ref[...], got_ref[...], weight_ref, 1 - meta_ref[0])
    sigmoid = jax.nn.sigmoid(pre)
    act_ref[...] = (pre * sigmoid).astype(BF16)
    slope_ref[...] = (
        cotangent_ref[...].astype(F32) * (sigmoid * (1.0 + pre * (1.0 - sigmoid)))
    ).astype(BF16)


def gradient_kernel(mine_ref, other_ref, slope_ref, other_slope_ref, grad_ref):
    contract = (((0,), (0,)), ((), ()))
    grad = jnp.zeros((HALF, F), F32)
    for mixed, slope in ((mine_ref, slope_ref), (other_ref, other_slope_ref)):
        for piece in two_parts(mixed[...]):
            grad = grad + lax.dot_general(
                piece, slope[...], contract, preferred_element_type=F32
            )
    grad_ref[...] = (grad * (1.0 / 256.0)).astype(BF16)


def row_moves(move):
    pairs = []
    for yl in range(2):
        for z in range(4):
            for c in range(2):
                to = move(yl, z, c)
                if to is not None:
                    a, b, d = to
                    pairs.append(((yl * 4 + z) * 2 + c, (a * 4 + b) * 2 + d))
    return pairs


def x_moves(k):
    return [(yh * 4 + x, yh * 4 + (x + k) % 4) for yh in range(2) for x in range(4)]


def y_moves():
    return [(yh * 4 + x, (1 - yh) * 4 + x) for yh in range(2) for x in range(4)]


def exchange(parts, axis, groups=None):
    return lax.all_to_all(
        parts, axis, split_axis=0, concat_axis=0, axis_index_groups=groups, tiled=True
    )


def added(parts):
    parts = parts.astype(F32)
    a = (parts[0] + parts[1]) + (parts[2] + parts[3])
    return a + ((parts[4] + parts[5]) + (parts[6] + parts[7]))


def call(kernel, in_specs, outs, scratch=(), limit=16):
    made = pl.pallas_call(
        kernel,
        in_specs=in_specs,
        out_specs=jax.tree.map(lambda _: pl.BlockSpec(memory_space=pltpu.VMEM), outs),
        out_shape=outs,
        scratch_shapes=list(scratch),
        compiler_params=params(limit),
    )

    def run(*operands):
        held = [
            pltpu.with_memory_space_constraint(o, spec.memory_space)
            if spec.memory_space in (pltpu.VMEM, pltpu.MemorySpace.HBM)
            else o
            for spec, o in zip(in_specs, operands)
        ]
        return made(*held)

    return run


def array(*shape, dtype=BF16):
    return jax.ShapeDtypeStruct(shape, dtype)


def held(*shape, dtype=BF16):
    return pltpu.VMEM(shape, dtype)


def after(value, *others):
    return lax.optimization_barrier((value, *others))[0]


def shards(
    features, partition_of, weight, tile_values, tile_rows, tile_cols, tile_count, out_cotangent
):
    row = lax.axis_index("row")
    col = lax.axis_index("col")
    core, z, yl = row % 2, (row // 2) % 4, row // 8
    x, yh = col % 4, col // 4
    vmem = pl.BlockSpec(memory_space=pltpu.VMEM)
    smem = pl.BlockSpec(memory_space=pltpu.SMEM)
    hbm = pl.BlockSpec(memory_space=pl.ANY)
    pinned = pl.BlockSpec(memory_space=pltpu.MemorySpace.HBM)

    here, there = yl * 4, (1 - yl) * 4
    near = [here + (z - k) % 4 for k in range(4)]
    far = [there + (z - k) % 4 for k in range(4)]
    first = core == 0
    places = [
        near[0],
        jnp.where(first, near[1], far[0]),
        jnp.where(first, far[0], near[1]),
        far[1],
        jnp.where(first, near[3], far[3]),
        jnp.where(first, near[2], near[3]),
        jnp.where(first, far[3], near[2]),
        far[2],
    ]
    meta = jnp.stack([core, x, yh, z] + places).astype(jnp.int32)

    swap = row_moves(lambda yl, z, c: (yl, z, 1 - c))
    tiles = tile_values.reshape(-1, TILE, TILE)
    part = partition_of.reshape(1, SLOTS)
    plan = call(plan_kernel, [smem, vmem, vmem], array(8, PLAN, dtype=jnp.int32))(
        tile_count.reshape(1), tile_rows.reshape(1, -1), tile_cols.reshape(1, -1)
    )
    other_plan = lax.ppermute(plan, "row", swap)
    plans = [jnp.where(core == c, plan, other_plan) for c in range(2)]
    grouped = call(
        group_kernel,
        [vmem, pinned],
        held(2 * N_COL, SLOTS // N_COL, HALF),
        [pltpu.VMEM((SLOTS, F), BF16), pltpu.SemaphoreType.DMA],
    )(part, features)
    other_tiles = lax.ppermute(after(tiles, grouped), "row", swap)
    near_chips = [[k * 2 * N_COL + m for m in range(2 * N_COL)] for k in range(CHIPS)]
    arrived = exchange(grouped, ("row", "col"), near_chips)
    own = call(interleave_kernel, [vmem], array(2, SLOTS, HALF))(arrived)
    own = after(own, other_tiles, other_plan)

    staged = held(SLOT_CAP + 1, TILE, TILE)
    tiles1 = call(stage_kernel, [smem, pinned, pinned], staged, [pltpu.SemaphoreType.DMA])(
        meta, tiles, after(other_tiles, own)
    )

    def hop(block, *moves):
        def move(yl, z, c):
            if moves[c] is None:
                return None
            return (yl + moves[c][0]) % 2, (z + moves[c][1]) % 4, c

        return lax.ppermute(block, "row", row_moves(move))

    r1 = hop(own, (0, 1), (1, 0))
    r2 = hop(own, (0, 3), None)
    r3 = hop(own, (0, 2), None)
    r4 = hop(own, (1, 0), (0, 1))
    s1 = hop(r1, (1, 0), (0, 1))
    s2 = hop(r2, (1, 0), None)
    s3 = hop(r3, (1, 0), None)
    later = after(own, r1)
    t1 = hop(r1, None, (0, 3))
    t2 = hop(later, None, (0, 3))
    t3 = hop(later, None, (0, 2))
    t4 = hop(r1, None, (0, 2))
    blocks = [
        b.reshape(2, N_ROW, N_COL * PER_PEER, HALF)
        for b in (own, r1, r4, s1, r2, r3, s2, s3, t1, t2, t3, t4)
    ]

    total = pltpu.VMEM((ROW_TILES, TILE, HALF), F32)
    source = held(CHIPS, 2, N_ROW, N_COL * PER_PEER, HALF)
    keep1, send1, source, tiles0 = call(
        tiles_y_kernel,
        [smem, smem, vmem, pinned, pinned] + [pinned] * BLOCKS,
        [held(4, SLOTS, HALF), held(4, SLOTS, HALF), source, staged],
        [total, pltpu.SemaphoreType.DMA((CHIPS,)), pltpu.SemaphoreType.DMA],
    )(meta, plans[1], tiles1, tiles, other_tiles, *blocks)
    row0 = call(
        tiles_x_kernel,
        [smem, smem, vmem, vmem],
        [held(2, SLOTS, HALF)] * 4,
        [total],
    )(meta, plans[0], tiles0, source)
    got0 = [lax.ppermute(row0[k], "col", x_moves(k)) for k in (1, 3, 2)]
    got1 = lax.ppermute(send1, "col", y_moves())
    wide, narrow = held(SLOTS, HALF, dtype=F32), held(SLOTS, HALF)
    keep1, *send1 = call(y_summed_kernel, [smem] + [vmem] * 2, [wide] + [narrow] * 3)(
        meta, keep1, got1
    )
    got1 = [lax.ppermute(send1[k - 1], "col", x_moves(k)) for k in (1, 3, 2)]
    keep0, send0 = call(x_summed_kernel, [smem] + [vmem] * 4, [wide, narrow])(
        meta, after(row0[0], got1[0]), *got0
    )
    got0 = lax.ppermute(send0, "col", y_moves())
    mine, others = call(sums_kernel, [smem] + [vmem] * 6, [wide] * 2)(
        meta, keep0, got0, keep1, *got1
    )
    theirs = lax.ppermute(others, "row", swap)
    half = call(half_layer_kernel, [smem] + [vmem] * 2, held(SLOTS, F, dtype=F32))(
        meta, mine, weight
    )
    cotangent = lax.dynamic_slice_in_dim(out_cotangent, col * SLOTS, SLOTS, 0)
    activations, slope = call(
        layer_kernel, [smem] + [vmem] * 4, [array(SLOTS, F), held(SLOTS, F)]
    )(
        meta, half, theirs, weight, cotangent
    )
    other_slope = lax.ppermute(slope, "row", swap)
    half = call(gradient_kernel, [vmem] * 4, held(HALF, F))(
        mine, others, slope, other_slope
    )

    same_core = [[chip * 2 + c for chip in range(CHIPS)] for c in range(2)]
    shape = (CHIPS, HALF // CHIPS, F)
    piece = added(exchange(half.reshape(shape), "row", same_core))
    piece = added(exchange(jnp.broadcast_to(piece.astype(BF16), shape), "col"))
    half = exchange(jnp.broadcast_to(piece.astype(BF16), shape), "row", same_core)
    half = half.reshape(HALF, F)
    other = lax.ppermute(half, "row", swap)
    first = jnp.where(core == 0, half, other).astype(F32)
    second = jnp.where(core == 0, other, half).astype(F32)
    return activations, jnp.concatenate([first, second])


def solution(mesh):
    placed = (
        P(("row", "col"), None),
        P(("row", "col")),
        P(),
        P("row", "col", None, None, None),
        P("row", "col", None),
        P("row", "col", None),
        P("row", "col"),
        P("row", None),
    )
    return jax.shard_map(
        shards,
        mesh=mesh,
        in_specs=placed,
        out_specs=(P(("row", "col"), None), P()),
        check_vma=False,
    )
```

```python
import jax
import jax.numpy as jnp
from jax import lax
from jax.experimental import pallas as pl
from jax.experimental.pallas import tpu as pltpu
from jax.sharding import PartitionSpec as P

N_ROW = 16
N_COL = 8
TILE = 128
SLOTS = 512
F = 512
PER_PEER = 4
HALF = 256
CHIPS = 8
SHARED = 4
BLOCKS = 2 * CHIPS - SHARED
SLOT_CAP = 192
ROW_TILES = 32
GROUP_BITS = 2
GROUP = 1 << GROUP_BITS
PLAN = SLOT_CAP + ROW_TILES * (GROUP - 1)
UNROLL_BITS = 3
UNROLL = 1 << UNROLL_BITS
BF16 = jnp.bfloat16
F32 = jnp.float32


def params(limit=16):
    return pltpu.CompilerParams(vmem_limit_bytes=limit * 1024 * 1024)


def selection(position, rows, columns):
    wanted = lax.broadcasted_iota(jnp.int32, (rows, columns), 0)
    return jnp.where(position == wanted, 1.0, 0.0).astype(BF16)


def group_kernel(part_ref, features_hbm, out_ref, features_ref, sem):
    copy = pltpu.make_async_copy(features_hbm, features_ref, sem)
    copy.start()
    part = part_ref[...]
    devices = N_ROW * N_COL
    before = jnp.where(
        lax.broadcasted_iota(jnp.int32, (SLOTS, SLOTS), 0)
        < lax.broadcasted_iota(jnp.int32, (SLOTS, SLOTS), 1),
        1.0,
        0.0,
    ).astype(BF16)
    member = jnp.where(
        part == lax.broadcasted_iota(jnp.int32, (devices, SLOTS), 0), 1.0, 0.0
    )
    earlier = jnp.dot(member.astype(BF16), before, preferred_element_type=F32)
    rank = jnp.sum(member * earlier, axis=0, keepdims=True).astype(jnp.int32)
    place = ((part & (N_COL - 1)) * N_ROW + (part >> 3)) * PER_PEER + rank
    pick = selection(place, SLOTS, SLOTS)
    copy.wait()
    for c in range(2):
        wanted = features_ref[:, c * HALF : (c + 1) * HALF]
        picked = jnp.dot(pick, wanted, preferred_element_type=F32).astype(BF16)
        out_ref[c * N_COL : (c + 1) * N_COL] = picked.reshape(N_COL, SLOTS // N_COL, HALF)


def interleave_kernel(arrived_ref, out_ref):
    source = lax.broadcasted_iota(jnp.int32, (1, SLOTS), 1)
    giver, inner = source >> 6, source & 63
    place = (inner >> 2) * (N_COL * PER_PEER) + giver * PER_PEER + (inner & 3)
    pick = selection(place, SLOTS, SLOTS)
    for c in range(2):
        rows = arrived_ref[c * N_COL : (c + 1) * N_COL].reshape(SLOTS, HALF)
        out_ref[c] = jnp.dot(pick, rows, preferred_element_type=F32).astype(BF16)


def plan_kernel(count_ref, rows_ref, cols_ref, plan_ref):
    slot = lax.broadcasted_iota(jnp.int32, (1, SLOT_CAP), 1)
    rows = rows_ref[...]
    live = slot < count_ref[0]
    kinds = lax.broadcasted_iota(jnp.int32, (ROW_TILES, SLOT_CAP), 0)
    member = jnp.where(live & (rows == kinds), 1.0, 0.0)
    before = jnp.where(
        lax.broadcasted_iota(jnp.int32, (SLOT_CAP, SLOT_CAP), 0)
        < lax.broadcasted_iota(jnp.int32, (SLOT_CAP, SLOT_CAP), 1),
        1.0,
        0.0,
    ).astype(BF16)
    earlier = jnp.dot(member.astype(BF16), before, preferred_element_type=F32)
    number = jnp.sum(member, axis=1, keepdims=True).astype(jnp.int32)
    groups = jnp.broadcast_to((number + (GROUP - 1)) >> GROUP_BITS, (ROW_TILES, TILE))
    below = jnp.where(
        lax.broadcasted_iota(jnp.int32, (ROW_TILES, ROW_TILES), 1)
        < lax.broadcasted_iota(jnp.int32, (ROW_TILES, ROW_TILES), 0),
        1.0,
        0.0,
    ).astype(BF16)
    groups = groups.astype(F32)
    start = jnp.dot(below, groups.astype(BF16), preferred_element_type=F32)[:, :1]
    total = jnp.sum(groups, axis=0, keepdims=True)[:, :1]
    place = jnp.sum(member * (GROUP * start + earlier + 1.0), axis=0, keepdims=True) - 1.0
    taken = selection(place.astype(jnp.int32), PLAN, SLOT_CAP)
    line = lax.broadcasted_iota(jnp.int32, (8, SLOT_CAP), 0)
    values = jnp.where(line == 0, slot - SLOT_CAP, jnp.where(line == 1, cols_ref[...], rows))
    found = lax.dot_general(
        values.astype(F32).astype(BF16),
        taken,
        (((1,), (1,)), ((), ())),
        preferred_element_type=F32,
    )
    line = lax.broadcasted_iota(jnp.int32, (8, PLAN), 0)
    found = jnp.where(line == 0, found + SLOT_CAP, jnp.where(line == 3, total, found))
    plan_ref[...] = found.astype(jnp.int32)


def start_tiles(part, core, own_hbm, other_hbm, out, sem):
    out[SLOT_CAP] = jnp.zeros((TILE, TILE), BF16)
    for mine, hbm in ((True, own_hbm), (False, other_hbm)):

        @pl.when((core == part) == mine)
        def _():
            pltpu.make_async_copy(hbm, out.at[pl.ds(0, SLOT_CAP)], sem).start()

    return pltpu.make_async_copy(own_hbm, out.at[pl.ds(0, SLOT_CAP)], sem)


def stage_kernel(meta_ref, own_hbm, other_hbm, out_ref, sem):
    start_tiles(1, meta_ref[0], own_hbm, other_hbm, out_ref, sem).wait()


def add_tiles(plan_ref, tiles, source, total):
    total[...] = jnp.zeros_like(total)

    def product(g):
        left, right = [], []
        for e in range(GROUP):
            u = plan_ref[1, g * GROUP + e]
            left.append(tiles[plan_ref[0, g * GROUP + e]])
            right.append(source[pl.ds((u & 3) * 2, 2), :, u >> 2].reshape(TILE, HALF))
        return jnp.dot(
            jnp.concatenate(left, axis=1),
            jnp.concatenate(right, axis=0),
            preferred_element_type=F32,
        )

    def some_groups(h, carry):
        found = [
            (plan_ref[2, (h * UNROLL + k) * GROUP], product(h * UNROLL + k))
            for k in range(UNROLL)
        ]
        for place, value in found:
            total[place] += value
        return carry

    lax.fori_loop(0, (plan_ref[3, 0] + UNROLL - 1) >> UNROLL_BITS, some_groups, 0)


def narrow_block(total, yh, x):
    rows = total[pl.ds((yh * 4 + x) * 4, 4)].astype(BF16)
    return rows.reshape(SLOTS, HALF)


def tiles_y_kernel(meta_ref, plan_ref, tiles, own_hbm, other_hbm, *refs):
    blocks, (keep_ref, send_ref, source, next_tiles) = refs[:BLOCKS], refs[BLOCKS:-3]
    total, sems, tiles_sem = refs[-3:]
    core, yh = meta_ref[0], meta_ref[2]

    def fetch(block, k):
        return pltpu.make_async_copy(block, source.at[meta_ref[4 + k]], sems.at[k])

    for k in range(SHARED):
        fetch(blocks[k], k).start()
    for c in range(2):

        @pl.when(core == c)
        def _():
            for k in range(SHARED, CHIPS):
                fetch(blocks[k + c * (CHIPS - SHARED)], k).start()

    for k in range(CHIPS):
        fetch(blocks[k], k).wait()
    coming = start_tiles(0, core, own_hbm, other_hbm, next_tiles, tiles_sem)
    add_tiles(plan_ref, tiles, source, total)
    for out, to in ((send_ref, 1 - yh), (keep_ref, yh)):
        for x in range(4):
            out[x] = narrow_block(total, to, x)
    coming.wait()


def tiles_x_kernel(meta_ref, plan_ref, tiles, source, *refs):
    outs, total = refs[:4], refs[4]
    x = meta_ref[1]
    add_tiles(plan_ref, tiles, source, total)
    for k, out in enumerate(outs):
        for yh in range(2):
            out[yh] = narrow_block(total, yh, (x + k) & 3)


def x_summed_kernel(meta_ref, own_ref, a_ref, b_ref, c_ref, keep_ref, send_ref):
    yh = meta_ref[2]

    def summed(k):
        pair = own_ref[k].astype(F32) + a_ref[k].astype(F32)
        return pair + (b_ref[k].astype(F32) + c_ref[k].astype(F32))

    keep_ref[...] = summed(yh)
    send_ref[...] = summed(1 - yh).astype(BF16)


def y_summed_kernel(meta_ref, own_ref, got_ref, keep_ref, a_ref, b_ref, c_ref):
    x = meta_ref[1]

    def summed(k):
        return own_ref[k].astype(F32) + got_ref[k].astype(F32)

    keep_ref[...] = summed(x)
    for k, out in ((1, a_ref), (2, b_ref), (3, c_ref)):
        out[...] = summed((x + k) & 3).astype(BF16)


def sums_kernel(meta_ref, keep0, got0, keep1, a_ref, b_ref, c_ref, mine_ref, send_ref):
    core = meta_ref[0]
    first = keep0[...] + got0[...].astype(F32)
    second = keep1[...] + a_ref[...].astype(F32)
    second = second + (b_ref[...].astype(F32) + c_ref[...].astype(F32))
    mine_ref[...] = jnp.where(core == 0, first, second)
    send_ref[...] = jnp.where(core == 0, second, first)


def two_parts(value):
    high = value.astype(BF16)
    return high, (value - high.astype(F32)).astype(BF16)


def half_product(pre, mixed, weight_ref, half):
    weight = weight_ref[pl.ds(pl.multiple_of(half * HALF, HALF), HALF), :]
    for piece in two_parts(mixed):
        pre = pre + jnp.dot(piece, weight, preferred_element_type=F32)
    return pre


def half_layer_kernel(meta_ref, mine_ref, weight_ref, pre_ref):
    start = jnp.zeros((SLOTS, F), F32)
    pre_ref[...] = half_product(start, mine_ref[...], weight_ref, meta_ref[0])


def layer_kernel(meta_ref, pre_ref, got_ref, weight_ref, cotangent_ref, act_ref, slope_ref):
    pre = half_product(pre_ref[...], got_ref[...], weight_ref, 1 - meta_ref[0])
    sigmoid = jax.nn.sigmoid(pre)
    act_ref[...] = (pre * sigmoid).astype(BF16)
    slope_ref[...] = (
        cotangent_ref[...].astype(F32) * (sigmoid * (1.0 + pre * (1.0 - sigmoid)))
    ).astype(BF16)


def gradient_kernel(mine_ref, other_ref, slope_ref, other_slope_ref, grad_ref):
    contract = (((0,), (0,)), ((), ()))
    grad = jnp.zeros((HALF, F), F32)
    for mixed, slope in ((mine_ref, slope_ref), (other_ref, other_slope_ref)):
        for piece in two_parts(mixed[...]):
            grad = grad + lax.dot_general(
                piece, slope[...], contract, preferred_element_type=F32
            )
    grad_ref[...] = (grad * (1.0 / 256.0)).astype(BF16)


def row_moves(move):
    pairs = []
    for yl in range(2):
        for z in range(4):
            for c in range(2):
                to = move(yl, z, c)
                if to is not None:
                    a, b, d = to
                    pairs.append(((yl * 4 + z) * 2 + c, (a * 4 + b) * 2 + d))
    return pairs


def x_moves(k):
    return [(yh * 4 + x, yh * 4 + (x + k) % 4) for yh in range(2) for x in range(4)]


def y_moves():
    return [(yh * 4 + x, (1 - yh) * 4 + x) for yh in range(2) for x in range(4)]


def exchange(parts, axis, groups=None):
    return lax.all_to_all(
        parts, axis, split_axis=0, concat_axis=0, axis_index_groups=groups, tiled=True
    )


def added(parts):
    parts = parts.astype(F32)
    a = (parts[0] + parts[1]) + (parts[2] + parts[3])
    return a + ((parts[4] + parts[5]) + (parts[6] + parts[7]))


def call(kernel, in_specs, outs, scratch=(), limit=16):
    made = pl.pallas_call(
        kernel,
        in_specs=in_specs,
        out_specs=jax.tree.map(lambda _: pl.BlockSpec(memory_space=pltpu.VMEM), outs),
        out_shape=outs,
        scratch_shapes=list(scratch),
        compiler_params=params(limit),
    )

    def run(*operands):
        held = [
            pltpu.with_memory_space_constraint(o, spec.memory_space)
            if spec.memory_space in (pltpu.VMEM, pltpu.MemorySpace.HBM)
            else o
            for spec, o in zip(in_specs, operands)
        ]
        return made(*held)

    return run


def array(*shape, dtype=BF16):
    return jax.ShapeDtypeStruct(shape, dtype)


def held(*shape, dtype=BF16):
    return pltpu.VMEM(shape, dtype)


def after(value, *others):
    return lax.optimization_barrier((value, *others))[0]


def shards(
    features, partition_of, weight, tile_values, tile_rows, tile_cols, tile_count, out_cotangent
):
    row = lax.axis_index("row")
    col = lax.axis_index("col")
    core, z, yl = row % 2, (row // 2) % 4, row // 8
    x, yh = col % 4, col // 4
    vmem = pl.BlockSpec(memory_space=pltpu.VMEM)
    smem = pl.BlockSpec(memory_space=pltpu.SMEM)
    hbm = pl.BlockSpec(memory_space=pl.ANY)
    pinned = pl.BlockSpec(memory_space=pltpu.MemorySpace.HBM)

    here, there = yl * 4, (1 - yl) * 4
    near = [here + (z - k) % 4 for k in range(4)]
    far = [there + (z - k) % 4 for k in range(4)]
    first = core == 0
    places = [
        near[0],
        jnp.where(first, near[1], far[0]),
        jnp.where(first, far[0], near[1]),
        far[1],
        jnp.where(first, near[3], far[3]),
        jnp.where(first, near[2], near[3]),
        jnp.where(first, far[3], near[2]),
        far[2],
    ]
    meta = jnp.stack([core, x, yh, z] + places).astype(jnp.int32)

    swap = row_moves(lambda yl, z, c: (yl, z, 1 - c))
    tiles = tile_values.reshape(-1, TILE, TILE)
    part = partition_of.reshape(1, SLOTS)
    plan = call(plan_kernel, [smem, vmem, vmem], array(8, PLAN, dtype=jnp.int32))(
        tile_count.reshape(1), tile_rows.reshape(1, -1), tile_cols.reshape(1, -1)
    )
    other_plan = lax.ppermute(plan, "row", swap)
    plans = [jnp.where(core == c, plan, other_plan) for c in range(2)]
    grouped = call(
        group_kernel,
        [vmem, pinned],
        held(2 * N_COL, SLOTS // N_COL, HALF),
        [pltpu.VMEM((SLOTS, F), BF16), pltpu.SemaphoreType.DMA],
    )(part, features)
    other_tiles = lax.ppermute(after(tiles, grouped), "row", swap)
    near_chips = [[k * 2 * N_COL + m for m in range(2 * N_COL)] for k in range(CHIPS)]
    arrived = exchange(grouped, ("row", "col"), near_chips)
    own = call(interleave_kernel, [vmem], array(2, SLOTS, HALF))(arrived)
    own = after(own, other_tiles, other_plan)

    staged = held(SLOT_CAP + 1, TILE, TILE)
    tiles1 = call(stage_kernel, [smem, pinned, pinned], staged, [pltpu.SemaphoreType.DMA])(
        meta, tiles, after(other_tiles, own)
    )

    def hop(block, *moves):
        def move(yl, z, c):
            if moves[c] is None:
                return None
            return (yl + moves[c][0]) % 2, (z + moves[c][1]) % 4, c

        return lax.ppermute(block, "row", row_moves(move))

    r1 = hop(own, (0, 1), (1, 0))
    r2 = hop(own, (0, 3), None)
    r3 = hop(own, (0, 2), None)
    r4 = hop(own, (1, 0), (0, 1))
    s1 = hop(r1, (1, 0), (0, 1))
    s2 = hop(r2, (1, 0), None)
    s3 = hop(r3, (1, 0), None)
    later = after(own, r1)
    t1 = hop(r1, None, (0, 3))
    t2 = hop(later, None, (0, 3))
    t3 = hop(later, None, (0, 2))
    t4 = hop(r1, None, (0, 2))
    blocks = [
        b.reshape(2, N_ROW, N_COL * PER_PEER, HALF)
        for b in (own, r1, r4, s1, r2, r3, s2, s3, t1, t2, t3, t4)
    ]

    total = pltpu.VMEM((ROW_TILES, TILE, HALF), F32)
    source = held(CHIPS, 2, N_ROW, N_COL * PER_PEER, HALF)
    keep1, send1, source, tiles0 = call(
        tiles_y_kernel,
        [smem, smem, vmem, pinned, pinned] + [hbm] * BLOCKS,
        [held(4, SLOTS, HALF), held(4, SLOTS, HALF), source, staged],
        [total, pltpu.SemaphoreType.DMA((CHIPS,)), pltpu.SemaphoreType.DMA],
    )(meta, plans[1], tiles1, tiles, other_tiles, *blocks)
    row0 = call(
        tiles_x_kernel,
        [smem, smem, vmem, vmem],
        [held(2, SLOTS, HALF)] * 4,
        [total],
    )(meta, plans[0], tiles0, source)
    got0 = [lax.ppermute(row0[k], "col", x_moves(k)) for k in (1, 3, 2)]
    got1 = lax.ppermute(send1, "col", y_moves())
    wide, narrow = held(SLOTS, HALF, dtype=F32), held(SLOTS, HALF)
    keep1, *send1 = call(y_summed_kernel, [smem] + [vmem] * 2, [wide] + [narrow] * 3)(
        meta, keep1, got1
    )
    got1 = [lax.ppermute(send1[k - 1], "col", x_moves(k)) for k in (1, 3, 2)]
    keep0, send0 = call(x_summed_kernel, [smem] + [vmem] * 4, [wide, narrow])(
        meta, after(row0[0], got1[0]), *got0
    )
    got0 = lax.ppermute(send0, "col", y_moves())
    mine, others = call(sums_kernel, [smem] + [vmem] * 6, [wide] * 2)(
        meta, keep0, got0, keep1, *got1
    )
    theirs = lax.ppermute(others, "row", swap)
    half = call(half_layer_kernel, [smem] + [vmem] * 2, held(SLOTS, F, dtype=F32))(
        meta, mine, weight
    )
    cotangent = lax.dynamic_slice_in_dim(out_cotangent, col * SLOTS, SLOTS, 0)
    activations, slope = call(
        layer_kernel, [smem] + [vmem] * 4, [array(SLOTS, F), held(SLOTS, F)]
    )(
        meta, half, theirs, weight, cotangent
    )
    other_slope = lax.ppermute(slope, "row", swap)
    half = call(gradient_kernel, [vmem] * 4, held(HALF, F))(
        mine, others, slope, other_slope
    )

    same_core = [[chip * 2 + c for chip in range(CHIPS)] for c in range(2)]
    shape = (CHIPS, HALF // CHIPS, F)
    piece = added(exchange(half.reshape(shape), "row", same_core))
    piece = added(exchange(jnp.broadcast_to(piece.astype(BF16), shape), "col"))
    half = exchange(jnp.broadcast_to(piece.astype(BF16), shape), "row", same_core)
    half = half.reshape(HALF, F)
    other = lax.ppermute(half, "row", swap)
    first = jnp.where(core == 0, half, other).astype(F32)
    second = jnp.where(core == 0, other, half).astype(F32)
    return activations, jnp.concatenate([first, second])


def solution(mesh):
    placed = (
        P(("row", "col"), None),
        P(("row", "col")),
        P(),
        P("row", "col", None, None, None),
        P("row", "col", None),
        P("row", "col", None),
        P("row", "col"),
        P("row", None),
    )
    return jax.shard_map(
        shards,
        mesh=mesh,
        in_specs=placed,
        out_specs=(P(("row", "col"), None), P()),
        check_vma=False,
    )
```
